32 devices in a mesh: seq: 16 (over z, y, x), head: 2 (over core).
Axes of the slice: x: 2, y: 2, z: 4, core: 2. Of those that a mesh axis runs over, the one named last changes fastest.
Arguments:
- inputs: bfloat16 [4, 2048, 768], P(None, ('seq', 'head')), may hold values from -6 to 6
- cotangent: bfloat16 [4, 2048, 768], P(None, ('seq', 'head')), may hold values from -6 to 6
- lengths: int32 [4], replicated, may hold values from 512 to 2048, as said below
- query_weight: bfloat16 [2, 768, 768], P(None, None, 'head'), may hold values from -0.375 to 0.375
- key_weight: bfloat16 [2, 768, 768], P(None, None, 'head'), may hold values from -0.375 to 0.375
- value_weight: bfloat16 [2, 768, 768], P(None, None, 'head'), may hold values from -0.21875 to 0.21875
- conv_weight: float32 [2, 12, 33], P(None, 'head'), may hold values from -0.6 to 0.6
- out_weight: bfloat16 [2, 768, 768], P(None, 'head'), may hold values from -0.3125 to 0.3125
- gain_one: float32 [2, 768], replicated, may hold values from 0.1 to 1.9
- shift_one: float32 [2, 768], replicated, may hold values from -1.5 to 1.5
- up_weight: bfloat16 [2, 768, 3072], P(None, None, 'head'), may hold values from -0.21875 to 0.21875
- up_bias: float32 [2, 3072], P(None, 'head'), may hold values from -2.5 to 2.5
- down_weight: bfloat16 [2, 3072, 768], P(None, 'head'), may hold values from -0.15625 to 0.15625
- gain_two: float32 [2, 768], replicated, may hold values from 0.1 to 1.9
- shift_two: float32 [2, 768], replicated, may hold values from -1.5 to 1.5
Outputs:
- output: float32 [4, 2048, 768], P(None, ('seq', 'head'))
- grad_inputs: float32 [4, 2048, 768], P(None, ('seq', 'head'))
- query_grad: float32 [2, 768, 768], P(None, 'seq', 'head')
- key_grad: float32 [2, 768, 768], P(None, 'seq', 'head')
- value_grad: float32 [2, 768, 768], P(None, 'seq', 'head')
- conv_grad: float32 [2, 12, 33], replicated
- out_grad: float32 [2, 768, 768], P(None, 'head', 'seq')
- gain_one_grad: float32 [2, 768], replicated
- shift_one_grad: float32 [2, 768], replicated
- up_grad: float32 [2, 768, 3072], P(None, 'seq', 'head')
- up_bias_grad: float32 [2, 3072], replicated
- down_grad: float32 [2, 3072, 768], P(None, 'head', 'seq')
- gain_two_grad: float32 [2, 768], replicated
- shift_two_grad: float32 [2, 768], replicated
The draws below stay inside these ranges and needn't reach their ends.
Inputs may be any that keep to these rules, and one draw needn't show every extreme that they name: `lengths`: one document, drawn from the seed, has length 2048.
All inputs are finite; a program needn't handle non-finite values.
Results may differ from the reference program's by a relative error of at most 0.02.
Values may be sent and summed in bfloat16 or wider, within the bound.
No kernel may reach another device: no remote copies, remote signals or barrier semaphores. Data moves between devices by JAX's collectives and lax.ppermute only.
A program may use at most 256 MiB of HBM per device.

```python
import math
import jax
import jax.numpy as jnp
from jax import lax

D = 768
HEADS = 12
HEAD_DIM = 64
FF = 3072
LANDMARKS = 64
TAPS = 33
PINV_STEPS = 6
LAYERS = 2
DOCS = 4
PAD = 2048


def draw_inputs(key, part):
    key = jax.random.fold_in(key, 5)
    rough_key, amp_key, phase_key = jax.random.split(key, 3)
    places = jnp.arange(PAD, dtype=jnp.float32)[None, :, None] / PAD
    rough = 0.7 * jax.random.normal(rough_key, (DOCS, PAD, D), jnp.float32)
    amplitude = 0.6 * jax.random.normal(amp_key, (3, DOCS, 1, D), jnp.float32)
    phases = jax.random.uniform(phase_key, (3, DOCS, 1, D), jnp.float32, -math.pi, math.pi)
    summed = rough
    for wave_index, cycles in enumerate((3.0, 7.0, 13.0)):
        summed = summed + amplitude[wave_index] * jnp.sin(2.0 * math.pi * cycles * places + phases[wave_index])
    return jnp.clip(summed, -6.0, 6.0).astype(jnp.bfloat16)


def draw_lengths(key, part):
    key = jax.random.fold_in(key, 11)
    first_key, second_key = jax.random.split(key)
    drawn = jax.random.randint(first_key, (DOCS,), PAD // 4, PAD + 1, dtype=jnp.int32)
    chosen = jax.random.randint(second_key, (), 0, DOCS, dtype=jnp.int32)
    return jnp.where(jnp.arange(DOCS, dtype=jnp.int32) == chosen, jnp.int32(PAD), drawn)


def level_of(rng, dims, cuts, low, high):
    loudness, own = 1.0, jax.random.fold_in(rng, 6)
    for axis_at, shards_of in cuts:
        draws = jnp.exp(jax.random.uniform(jax.random.fold_in(own, axis_at), (shards_of,), jnp.float32, low / len(cuts), high / len(cuts)))
        loudness = loudness * jnp.repeat(draws, dims[axis_at] // shards_of).reshape([-1 if axis == axis_at else 1 for axis in range(len(dims))])
    return loudness


def gaussian(stream_key, dims, deviation, limit, cuts=(), kind=jnp.bfloat16):
    result = jax.random.normal(stream_key, dims, jnp.float32) * deviation
    if len(cuts) > 0:
        result = level_of(stream_key, dims, cuts, -0.22, 0.18) * result
    return jnp.clip(result, min=-limit, max=limit).astype(kind)


def setup_inputs(seed: int = 0) -> dict:
    key_of = jax.random.split(jax.random.key(seed), 16)
    return {
        "inputs": draw_inputs(jax.random.fold_in(key_of[15], 71), 0),
        "cotangent": gaussian(key_of[1], (DOCS, PAD, D), 1.0, 6.0, ((1, 32),)),
        "lengths": draw_lengths(jax.random.fold_in(key_of[15], 71), 0),
        "query_weight": gaussian(key_of[3], (LAYERS, D, D), (D // 3) ** -0.5, 0.375, ((2, 2),)),
        "key_weight": gaussian(key_of[4], (LAYERS, D, D), (D // 3) ** -0.5, 0.375, ((2, 2),)),
        "value_weight": gaussian(key_of[5], (LAYERS, D, D), D ** -0.5, 0.21875, ((2, 2),)),
        "conv_weight": gaussian(key_of[6], (LAYERS, HEADS, TAPS), 0.1, 0.6, ((1, 2),), jnp.float32),
        "out_weight": gaussian(key_of[7], (LAYERS, D, D), (D // 2) ** -0.5, 0.3125, ((1, 2),)),
        "gain_one": jnp.clip(1.0 + 0.18 * jax.random.normal(key_of[8], (LAYERS, D), jnp.float32), 0.1, 1.9),
        "shift_one": gaussian(key_of[9], (LAYERS, D), 0.3, 1.5, (), jnp.float32),
        "up_weight": gaussian(key_of[10], (LAYERS, D, FF), D ** -0.5, 0.21875, ((2, 2),)),
        "up_bias": gaussian(key_of[11], (LAYERS, FF), 0.5, 2.5, ((1, 2),), jnp.float32),
        "down_weight": gaussian(key_of[12], (LAYERS, FF, D), (FF // 2) ** -0.5, 0.15625, ((1, 2),)),
        "gain_two": jnp.clip(1.0 + 0.18 * jax.random.normal(key_of[13], (LAYERS, D), jnp.float32), 0.1, 1.9),
        "shift_two": gaussian(key_of[14], (LAYERS, D), 0.3, 1.5, (), jnp.float32),
    }


highest = lax.Precision.HIGHEST
norm_eps = 1e-05
masked_score = -1e+30

@jax.custom_vjp
def low(v):
    return lax.optimization_barrier(v.astype(jnp.bfloat16)).astype(jnp.float32)

@jax.custom_vjp
def low_back(v):
    return v

def low_keep(v):
    return (low(v), None)

def low_pass(kept, grad):
    return (grad,)

def back_keep(v):
    return (v, None)

def back_low(kept, grad):
    return (low(grad),)
low.defvjp(low_keep, low_pass)
low_back.defvjp(back_keep, back_low)

def product(left, right):
    return jnp.matmul(left, right, precision=highest)

def layer_norm(entries, factor, offset):
    row_mean = lax.optimization_barrier(jnp.mean(entries, axis=-1, keepdims=True))
    centred = entries - row_mean
    spread = lax.optimization_barrier(jnp.mean(centred * centred, axis=-1, keepdims=True))
    return centred * lax.rsqrt(spread + norm_eps) * factor + offset

def segment_table(lengths):
    places = jnp.arange(PAD, dtype=jnp.int32)
    marks = jnp.arange(LANDMARKS + 1, dtype=jnp.int32)
    bounds = marks[None, :] * lengths[:, None] // LANDMARKS
    inside = (places[None, None, :] >= bounds[:, :-1, None]) & (places[None, None, :] < bounds[:, 1:, None])
    counts = (bounds[:, 1:] - bounds[:, :-1]).astype(jnp.float32)
    return (inside.astype(jnp.float32), counts)

def pseudo_inverse(kernel):
    identity = jnp.eye(LANDMARKS, dtype=jnp.float32)
    approx = jnp.swapaxes(kernel, -1, -2) / lax.optimization_barrier(jnp.sum(kernel * kernel, axis=(-2, -1), keepdims=True))
    for step_index in range(PINV_STEPS):
        kernel_times = product(kernel, approx)
        inner_term = 7.0 * identity - kernel_times
        inner_term = 15.0 * identity - product(kernel_times, inner_term)
        inner_term = 13.0 * identity - product(kernel_times, inner_term)
        approx = 0.25 * product(approx, inner_term)
    return approx

def doc_attention(queries, key_rows, values, inside, counts, valid, conv_weight):
    score_scale = HEAD_DIM ** (-0.5)
    masked = values * valid[:, None, None]
    query_marks = jnp.einsum('mt,the->mhe', inside, queries, precision=highest) / counts[:, None, None]
    key_marks = jnp.einsum('mt,the->mhe', inside, key_rows, precision=highest) / counts[:, None, None]
    near = jax.nn.softmax(score_scale * jnp.einsum('the,mhe->htm', queries, key_marks, precision=highest), axis=-1)
    middle = jax.nn.softmax(score_scale * jnp.einsum('mhe,nhe->hmn', query_marks, key_marks, precision=highest), axis=-1)
    far_scores = score_scale * jnp.einsum('mhe,the->hmt', query_marks, key_rows, precision=highest)
    far_scores = jnp.where(valid[None, None, :] > 0, far_scores, masked_score)
    far = jax.nn.softmax(far_scores, axis=-1)
    summary = jnp.einsum('hmt,the->hme', far, masked, precision=highest)
    mixed_marks = product(pseudo_inverse(middle), summary)
    attended = jnp.einsum('htm,hme->the', near, mixed_marks, precision=highest)
    rim_width = TAPS // 2
    padded = jnp.pad(masked, ((rim_width, rim_width), (0, 0), (0, 0)))
    for tap_index in range(TAPS):
        attended = attended + padded[tap_index:tap_index + PAD] * conv_weight[:, tap_index][None, :, None]
    return attended

def one_layer(state_rows, weights, tables):
    query_weight, key_weight, value_weight, conv_weight, out_weight, gain_one, shift_one, up_weight, up_bias, down_weight, gain_two, shift_two = weights
    inside, counts, valid = tables
    rounded = low(state_rows)
    queries = low_back(product(rounded, query_weight))
    key_rows = low_back(product(rounded, key_weight))
    values = low_back(product(rounded, value_weight))
    head_shape = (DOCS, PAD, HEADS, HEAD_DIM)

    def attend(member):
        return doc_attention(member[0], member[1], member[2], member[3], member[4], member[5], conv_weight)
    attended = lax.map(jax.checkpoint(attend), (queries.reshape(head_shape), key_rows.reshape(head_shape), values.reshape(head_shape), inside, counts, valid))
    attended = attended.reshape(DOCS, PAD, D)
    branch = low_back(product(low(attended), out_weight))
    first_rows = layer_norm(state_rows + branch, gain_one, shift_one)
    upper_rows = low_back(product(low(first_rows), up_weight) + up_bias)
    hidden_low = low(jax.nn.gelu(upper_rows, approximate=False))
    down_rows = low_back(product(hidden_low, down_weight))
    return layer_norm(first_rows + down_rows, gain_two, shift_two) * valid[:, :, None]

def reference(inputs, cotangent, lengths, query_weight, key_weight, value_weight, conv_weight, out_weight, gain_one, shift_one, up_weight, up_bias, down_weight, gain_two, shift_two):
    inside, counts = segment_table(lengths)
    valid = (jnp.arange(PAD, dtype=jnp.int32)[None, :] < lengths[:, None]).astype(jnp.float32)
    params = tuple((member.astype(jnp.float32) for member in (query_weight, key_weight, value_weight, conv_weight, out_weight, gain_one, shift_one, up_weight, up_bias, down_weight, gain_two, shift_two)))

    def forward(state_rows, layer_params):
        for layer_index in range(LAYERS):
            state_rows = one_layer(state_rows, tuple((member[layer_index] for member in layer_params)), (inside, counts, valid))
        return state_rows
    output, pullback = jax.vjp(forward, inputs.astype(jnp.float32), params)
    grad_inputs, weight_grads = pullback(cotangent.astype(jnp.float32))
    return (output, grad_inputs, weight_grads[0], weight_grads[1], weight_grads[2], weight_grads[3], weight_grads[4], weight_grads[5], weight_grads[6], weight_grads[7], weight_grads[8], weight_grads[9], weight_grads[10], weight_grads[11])
```

```python
import jax
import jax.numpy as jnp
from jax import lax
from jax.experimental import pallas as pl
from jax.experimental.pallas import tpu as pltpu
from jax.sharding import Mesh, PartitionSpec as P

HEADS = 12
HEAD_DIM = 64
LANDMARKS = 64
TAPS = 33
RIM = TAPS // 2
PINV_STEPS = 6
LAYERS = 2
OWN_HEADS = 2
OWN_COLS = OWN_HEADS * HEAD_DIM
SCALE = HEAD_DIM ** (-0.5)
EPS = 1e-05
MASKED = -1e30
FF_TILE = 512
VMEM_LIMIT = 56 * 1024 * 1024

f32 = jnp.float32
bf16 = jnp.bfloat16

NN = ((1,), (0,))
NT = ((1,), (1,))
TN = ((0,), (0,))


def dg(a, b, dims):
    return lax.dot_general(a, b, (dims, ((), ())), preferred_element_type=f32)


def split2(x):
    hi = x.astype(bf16)
    return hi, (x - hi.astype(f32)).astype(bf16)


def split3(x):
    hi = x.astype(bf16)
    rest = x - hi.astype(f32)
    mid = rest.astype(bf16)
    return hi, mid, (rest - mid.astype(f32)).astype(bf16)


def dot3(a, b, dims):
    a1, a2 = split2(a)
    b1, b2 = split2(b)
    return dg(a1, b1, dims) + (dg(a1, b2, dims) + dg(a2, b1, dims))


def mm(a, b):
    a1, a2, a3 = split3(a)
    b1, b2, b3 = split3(b)
    n = b.shape[1]
    top = jnp.concatenate([b1, b2, b3], axis=1)
    low = jnp.concatenate([b1, b2, jnp.zeros_like(b3)], axis=1)
    wide = dg(jnp.concatenate([a1, a2], axis=1), jnp.concatenate([top, low], axis=0), NN)
    last = dg(a3, b1, NN)
    return wide[:, :n] + (wide[:, n : 2 * n] + (wide[:, 2 * n :] + last))


def head_mask(rows, cols):
    r = lax.broadcasted_iota(jnp.int32, (rows, cols), 0) // HEAD_DIM
    c = lax.broadcasted_iota(jnp.int32, (rows, cols), 1) // HEAD_DIM
    return r == c


def spread(x):
    n = x.shape[1]
    tall = jnp.concatenate([x] * (n // HEAD_DIM), axis=0)
    return jnp.where(head_mask(n, n), tall, 0.0)


def collect(x):
    n = x.shape[1]
    x = jnp.where(head_mask(n, n), x, 0.0)
    total = x[0:HEAD_DIM]
    for h in range(1, n // HEAD_DIM):
        total = total + x[h * HEAD_DIM : (h + 1) * HEAD_DIM]
    return total


def head_max(s):
    lane = lax.broadcasted_iota(jnp.int32, s.shape, 1) // HEAD_DIM
    out = s
    for h in range(s.shape[1] // HEAD_DIM):
        top = jnp.max(jnp.where(lane == h, s, MASKED), axis=1, keepdims=True)
        out = jnp.where(lane == h, top, out)
    return out


def head_sum(e):
    n = e.shape[1]
    ones = jnp.where(head_mask(n, n), 1.0, 0.0).astype(bf16)
    e1, e2 = split2(e)
    return dg(e1, ones, NN) + dg(e2, ones, NN)


def down_form(lanes):
    n = lanes.shape[1]
    return collect(jnp.broadcast_to(lanes, (n, n)).T)


def block(ref, b):
    return ref[:, 256 * b : 256 * (b + 1)]


def norm_rows(r):
    mean = jnp.mean(r, axis=-1, keepdims=True)
    c = r - mean
    q = lax.rsqrt(jnp.mean(c * c, axis=-1, keepdims=True) + EPS)
    return c * q, q


def norm_pull(r, gy, gain):
    n, q = norm_rows(r)
    dgain = jnp.sum(gy * n, axis=0, keepdims=True)
    dshift = jnp.sum(gy, axis=0, keepdims=True)
    a = gy * gain
    am = jnp.mean(a, axis=-1, keepdims=True)
    anm = jnp.mean(a * n, axis=-1, keepdims=True)
    return q * (a - am - n * anm), dgain, dshift


def conv_block(padded, taps, rows):
    acc = None
    for res in range(8):
        sh = padded if res == 0 else padded[res : res + rows + 24]
        for a in range(5):
            r = 8 * a + res
            if r < TAPS:
                term = sh[8 * a : 8 * a + rows] * taps[r : r + 1]
                acc = term if acc is None else acc + term
    return acc


def padded_chunk(mid_ref, prev_ref, next_ref, c, rows, lanes):
    return jnp.concatenate(
        [
            prev_ref[RIM * c : RIM * (c + 1), lanes],
            mid_ref[rows * c : rows * (c + 1), lanes],
            next_ref[RIM * c : RIM * (c + 1), lanes],
        ],
        axis=0,
    )


def call(body, outs, args, specs=None, out_specs=None, grid=None, scratch=(), cost=None):
    kw = {}
    if grid is not None:
        kw["grid"] = grid
    if specs is not None:
        kw["in_specs"] = specs
    if out_specs is not None:
        kw["out_specs"] = out_specs
    if cost is not None:
        kw["cost_estimate"] = pl.CostEstimate(flops=cost[0], bytes_accessed=cost[1], transcendentals=0)
    return pl.pallas_call(
        body,
        out_shape=[jax.ShapeDtypeStruct(s, t) for s, t in outs],
        scratch_shapes=list(scratch),
        compiler_params=pltpu.CompilerParams(vmem_limit_bytes=VMEM_LIMIT),
        **kw,
    )(*args)


def whole(a):
    nd = len(a.shape)
    return pl.BlockSpec(a.shape, lambda *_: (0,) * nd)


def of_layer(a, layer):
    nd = len(a.shape)
    return pl.BlockSpec((1,) + a.shape[1:], lambda *_: (layer,) + (0,) * (nd - 1))


def project(xr, wq, wk, wv, valid, layer):
    rows, width = xr.shape
    half = wq[0].shape[2]

    def body(x_ref, q0, q1, k0, k1, v0, v1, valid_ref, q_ref, k_ref, v_ref):
        x = x_ref[...]
        for (w0, w1), o in (((q0, q1), q_ref), ((k0, k1), k_ref)):
            o[:, :half] = dg(x, w0[0], NN)
            o[:, half:] = dg(x, w1[0], NN)
        va = valid_ref[...]
        v_ref[:, :half] = dg(x, v0[0], NN) * va
        v_ref[:, half:] = dg(x, v1[0], NN) * va

    args = (xr, *wq, *wk, *wv, valid)
    specs = [whole(xr)] + [of_layer(w, layer) for w in (*wq, *wk, *wv)] + [whole(valid)]
    outs = [((rows, 2 * half), f32)] * 3
    return call(
        body, outs, args, specs, [whole(jax.ShapeDtypeStruct(*o)) for o in outs], (1,),
        cost=(2 * rows * width * 6 * half, 4 * width * 6 * half),
    )


def scores(q, k, v, xbar, icounts, wq, wk, valid, layer):
    rows, width = q.shape
    half = width // 2

    def body(q_ref, k_ref, v_ref, xb_ref, ic_ref, q0, q1, k0, k1, valid_ref,
             near_ref, e_ref, qm_ref, km_ref, part_ref):
        x1, x2, x3 = split3(xb_ref[...] * ic_ref[...])
        xs = jnp.concatenate([x1, x2, x3], axis=0)
        for w, o, at in ((q0, qm_ref, 0), (q1, qm_ref, half), (k0, km_ref, 0), (k1, km_ref, half)):
            p = dg(xs, w[0], NN)
            o[:, at : at + half] = (
                p[:LANDMARKS] + (p[LANDMARKS : 2 * LANDMARKS] + p[2 * LANDMARKS :])
            )
        live = valid_ref[...] > 0
        for b in range(width // 256):
            at = slice(256 * b, 256 * (b + 1))
            s = dot3(q_ref[:, at] * SCALE, spread(km_ref[:, at]), NT)
            e = jnp.exp(s - head_max(s))
            near_ref[:, at] = e / head_sum(e)
            s = dot3(k_ref[:, at], spread(qm_ref[:, at] * SCALE), NT)
            s = jnp.where(live, s, MASKED)
            top = jnp.max(s, axis=0, keepdims=True)
            e = jnp.where(live, jnp.exp(s - top), 0.0)
            e_ref[:, at] = e
            part_ref[0:LANDMARKS, at] = collect(dot3(e, v_ref[:, at], TN))
            part_ref[LANDMARKS : LANDMARKS + 8, at] = jnp.concatenate(
                [top, jnp.sum(e, axis=0, keepdims=True), jnp.zeros((6, 256), f32)], axis=0
            )

    args = (q, k, v, xbar, icounts, *wq, *wk, valid)
    specs = [whole(a) for a in (q, k, v, xbar, icounts)]
    specs += [of_layer(w, layer) for w in (*wq, *wk)] + [whole(valid)]
    outs = [((rows, width), f32)] * 2 + [((LANDMARKS, width), f32)] * 2
    outs += [((LANDMARKS + 8, width), f32)]
    return call(
        body, outs, args, specs, [whole(jax.ShapeDtypeStruct(*o)) for o in outs], (1,),
        cost=(2 * rows * width * 256 * 9, 10 * 4 * rows * width),
    )


def eye(n):
    return jnp.where(
        lax.broadcasted_iota(jnp.int32, (n, n), 0) == lax.broadcasted_iota(jnp.int32, (n, n), 1),
        1.0, 0.0,
    )


def head_total(column):
    n = column.shape[0]
    row = lax.broadcasted_iota(jnp.int32, (n, 1), 0) // HEAD_DIM
    out = column
    for h in range(n // HEAD_DIM):
        s = jnp.sum(column[h * HEAD_DIM : (h + 1) * HEAD_DIM], axis=0, keepdims=True)
        out = jnp.where(row == h, s, out)
    return out


def inverse(qm, km):
    n = qm.shape[1]

    def body(q_ref, k_ref, a_ref, z_ref, p_ref, t2_ref, t3_ref):
        ident = eye(n)
        s = mm(spread(q_ref[...] * SCALE), spread(k_ref[...]).T)
        s = jnp.where(head_mask(n, n), s, MASKED)
        e = jnp.exp(s - jnp.max(s, axis=1, keepdims=True))
        a = e / jnp.sum(e, axis=1, keepdims=True)
        a_ref[...] = a
        z = a.T / head_total(jnp.sum(a * a, axis=1, keepdims=True))
        for step in range(PINV_STEPS):
            p = mm(a, z)
            t2 = 15.0 * ident - mm(p, 7.0 * ident - p)
            t3 = 13.0 * ident - mm(p, t2)
            z_ref[step] = z
            p_ref[step] = p
            t2_ref[step] = t2
            t3_ref[step] = t3
            z = 0.25 * mm(z, t3)
        z_ref[PINV_STEPS] = z

    outs = [((n, n), f32), ((PINV_STEPS + 1, n, n), f32)] + [((PINV_STEPS, n, n), f32)] * 3
    return call(body, outs, (qm, km), cost=(2 * n**3 * 6 * 25 * 4, 4 * 26 * n * n))


def merge(parts, z):
    count, rows, n = parts.shape

    def body(p_ref, z_ref, out_ref, sum_ref):
        top = p_ref[0, LANDMARKS : LANDMARKS + 1]
        for d in range(1, count):
            top = jnp.maximum(top, p_ref[d, LANDMARKS : LANDMARKS + 1])
        total = jnp.zeros_like(top)
        carried = jnp.zeros((LANDMARKS, n), f32)
        for d in range(count):
            w = jnp.exp(p_ref[d, LANDMARKS : LANDMARKS + 1] - top)
            total = total + w * p_ref[d, LANDMARKS + 1 : LANDMARKS + 2]
            carried = carried + down_form(w) * p_ref[d, 0:LANDMARKS]
        summary = carried / down_form(total)
        sum_ref[...] = summary
        out_ref[0:LANDMARKS] = collect(mm(z_ref[PINV_STEPS], spread(summary)))
        out_ref[LANDMARKS : LANDMARKS + 8] = jnp.concatenate(
            [top, total, jnp.zeros((6, n), f32)], axis=0
        )

    return call(body, [((rows, n), f32), ((LANDMARKS, n), f32)], (parts, z))


def forward_rows(near, mixed, v, prev, nxt, taps, x, weights, gains, valid, inside, layer):
    wo, wu, wd, bias = weights
    rows, width = x.shape
    chunk = rows * RIM // prev.shape[0]
    half = width // 2
    tiles = wu[0].shape[2] // FF_TILE

    def body(near_ref, mix_ref, v_ref, prev_ref, next_ref, taps_ref, x_ref, o0, o1, u0, u1, d0, d1,
             bias_ref, g1, s1, g2, s2, valid_ref, in_ref,
             al_ref, r1_ref, fl_ref, dgelu_ref, hid_ref, r2_ref, xn_ref, xr_ref, xb_ref,
             att, first, acc):
        i = pl.program_id(0)

        @pl.when(i == 0)
        def _():
            for b in range(width // 256):
                at = slice(256 * b, 256 * (b + 1))
                att[:, at] = dot3(near_ref[:, at], spread(mix_ref[0:LANDMARKS, at]), NN)
            for b in range(width // 128):
                at = slice(128 * b, 128 * (b + 1))
                taps_here = taps_ref[:, at]
                for c in range(rows // chunk):
                    here = slice(chunk * c, chunk * (c + 1))
                    att[here, at] += conv_block(
                        padded_chunk(v_ref, prev_ref, next_ref, c, chunk, at), taps_here, chunk
                    )
            low = att[...].astype(bf16)
            al_ref[...] = low
            r1 = x_ref[...].astype(f32) + (dg(low[:, :half], o0[0], NN) + dg(low[:, half:], o1[0], NN))
            r1_ref[...] = r1
            n, _q = norm_rows(r1)
            rows1 = n * g1[layer : layer + 1] + s1[layer : layer + 1]
            first[...] = rows1
            fl_ref[...] = rows1.astype(bf16)
            acc[...] = jnp.zeros_like(acc)

        def tile(u, d):
            up = dg(fl_ref[...], u[0], NN) + bias_ref[...]
            phi = 0.5 * (1.0 + lax.erf(up * (0.5**0.5)))
            dgelu_ref[...] = phi + up * (jnp.exp(-0.5 * up * up) * 0.3989422804014327)
            hid = (up * phi).astype(bf16)
            hid_ref[...] = hid
            acc[...] += dg(hid, d[0], NN)

        @pl.when(i < tiles)
        def _():
            tile(u0, d0)

        @pl.when(i >= tiles)
        def _():
            tile(u1, d1)

        @pl.when(i == 2 * tiles - 1)
        def _():
            r2 = first[...] + acc[...]
            r2_ref[...] = r2
            n, _q = norm_rows(r2)
            xn = (n * g2[layer : layer + 1] + s2[layer : layer + 1]) * valid_ref[...]
            xn_ref[...] = xn
            xr = xn.astype(bf16)
            xr_ref[...] = xr
            xb_ref[...] = dg(in_ref[...], xr, TN)

    own = lambda i: jnp.minimum(i, tiles - 1)
    oth = lambda i: jnp.maximum(i - tiles, 0)
    up_spec = lambda f: pl.BlockSpec((1, width, FF_TILE), lambda i: (layer, 0, f(i)))
    down_spec = lambda f: pl.BlockSpec((1, FF_TILE, width), lambda i: (layer, f(i), 0))
    args = (near, mixed, v, prev, nxt, taps, x, *wo, *wu, *wd, bias, *gains, valid, inside)
    specs = [whole(a) for a in (near, mixed, v, prev, nxt, taps, x)]
    specs += [of_layer(w, layer) for w in wo]
    specs += [up_spec(own), up_spec(oth), down_spec(own), down_spec(oth)]
    specs += [pl.BlockSpec((1, FF_TILE), lambda i: (0, i))]
    specs += [whole(a) for a in (*gains, valid, inside)]
    ff = 2 * tiles * FF_TILE
    row = ((rows, width), f32)
    low = ((rows, width), bf16)
    outs = [low, row, low, ((rows, ff), f32), ((rows, ff), bf16), row, row, low,
            ((LANDMARKS, width), f32)]
    wide = pl.BlockSpec((rows, FF_TILE), lambda i: (0, i))
    out_specs = [wide if s[1] == ff else whole(jax.ShapeDtypeStruct(s, t)) for s, t in outs]
    return call(
        body, outs, args, specs, out_specs, (2 * tiles,), [pltpu.VMEM((rows, width), f32)] * 3,
        cost=(2 * rows * width * (2 * ff + width) * 2, 30 * rows * width * 4),
    )


def backward_rows(g, r1, r2, dgelu, near, mixed, q, km, weights, gains, valid, layer):
    wo, wu, wd = weights
    rows, width = r1.shape
    half = width // 2
    tiles = wu[0].shape[2] // FF_TILE

    def body(g_ref, r1_ref, r2_ref, near_ref, mix_ref, q_ref, km_ref, dgelu_ref,
             o0, o1, u0, u1, d0, d1, g1, g2, valid_ref,
             gd_ref, gu_ref, bias_ref, gr1_ref, gb_ref, gatt_ref, gqn_ref, mk_ref, small_ref, acc):
        i = pl.program_id(0)

        @pl.when(i == 0)
        def _():
            gy = g_ref[...].astype(f32) * valid_ref[...]
            gr2, dgain, dshift = norm_pull(r2_ref[...], gy, g2[layer : layer + 1])
            acc[...] = gr2
            gd_ref[...] = gr2.astype(bf16)
            small_ref[2:3] = dgain
            small_ref[3:4] = dshift

        def tile(u, d):
            gh = dg(gd_ref[...], d[0], NT)
            gu = (gh * dgelu_ref[...]).astype(bf16)
            gu_ref[...] = gu
            bias_ref[...] = jnp.sum(gu.astype(f32), axis=0, keepdims=True)
            acc[...] += dg(gu, u[0], NT)

        @pl.when(i < tiles)
        def _():
            tile(u0, d0)

        @pl.when(i >= tiles)
        def _():
            tile(u1, d1)

        @pl.when(i == 2 * tiles - 1)
        def _():
            gr1, dgain, dshift = norm_pull(r1_ref[...], acc[...], g1[layer : layer + 1])
            small_ref[0:1] = dgain
            small_ref[1:2] = dshift
            small_ref[4:8] = jnp.zeros((4, width), f32)
            gr1_ref[...] = gr1
            gb = gr1.astype(bf16)
            gb_ref[...] = gb
            gatt_ref[:, :half] = dg(gb, o0[0], NT)
            gatt_ref[:, half:] = dg(gb, o1[0], NT)
            for b in range(width // 256):
                at = slice(256 * b, 256 * (b + 1))
                gatt = gatt_ref[:, at]
                nr = near_ref[:, at]
                gn = dot3(gatt, spread(mix_ref[0:LANDMARKS, at]), NT)
                gs = nr * (gn - head_sum(nr * gn)) * SCALE
                gqn_ref[:, at] = dot3(gs, spread(km_ref[:, at]), NN)
                mk_ref[0:LANDMARKS, at] = collect(dot3(nr, gatt, TN))
                mk_ref[LANDMARKS:, at] = collect(dot3(gs, q_ref[:, at], TN))

    own = lambda i: jnp.minimum(i, tiles - 1)
    oth = lambda i: jnp.maximum(i - tiles, 0)
    up_spec = lambda f: pl.BlockSpec((1, width, FF_TILE), lambda i: (layer, 0, f(i)))
    down_spec = lambda f: pl.BlockSpec((1, FF_TILE, width), lambda i: (layer, f(i), 0))
    wide = pl.BlockSpec((rows, FF_TILE), lambda i: (0, i))
    first = (g, r1, r2, near, mixed, q, km)
    args = (*first, dgelu, *wo, *wu, *wd, *gains, valid)
    specs = [whole(a) for a in first] + [wide] + [of_layer(w, layer) for w in wo]
    specs += [up_spec(own), up_spec(oth), down_spec(own), down_spec(oth)]
    specs += [whole(a) for a in (*gains, valid)]
    ff = 2 * tiles * FF_TILE
    row = ((rows, width), f32)
    low = ((rows, width), bf16)
    outs = [low, ((rows, ff), bf16), ((1, ff), f32), row, low, row, row,
            ((2 * LANDMARKS, width), f32), ((8, width), f32)]
    out_specs = [whole(jax.ShapeDtypeStruct(s, t)) for s, t in outs]
    out_specs[1] = wide
    out_specs[2] = pl.BlockSpec((1, FF_TILE), lambda i: (0, i))
    return call(
        body, outs, args, specs, out_specs, (2 * tiles,), [pltpu.VMEM((rows, width), f32)],
        cost=(2 * rows * width * (2 * ff + width) * 2, 30 * rows * width * 4),
    )


def inverse_pull(parts, qm, km, summary, a, zs, ps, t2s, t3s):
    count, rows, n = parts.shape

    def body(g_ref, q_ref, k_ref, s_ref, a_ref, z_ref, p_ref, t2_ref, t3_ref, out_ref):
        ident = eye(n)
        mask = head_mask(n, n)
        g = g_ref[0]
        for d in range(1, count):
            g = g + g_ref[d]
        gm = spread(g[0:LANDMARKS])
        sm = s_ref[...]
        sb = spread(sm)
        a = a_ref[...]
        at = a.T
        gz = mm(gm, sb.T)
        gs = collect(mm(z_ref[PINV_STEPS].T, gm))
        ga = jnp.zeros((n, n), f32)
        for step in reversed(range(PINV_STEPS)):
            z, p, t2, t3 = z_ref[step], p_ref[step], t2_ref[step], t3_ref[step]
            zt, pt = z.T, p.T
            gt3 = 0.25 * mm(zt, gz)
            gt2 = -mm(pt, gt3)
            gt1 = -mm(pt, gt2)
            gp = -(mm(gt3, t2.T) + mm(gt2, (7.0 * ident - p).T) + gt1)
            gz = 0.25 * mm(gz, t3.T) + mm(at, gp)
            ga = ga + mm(gp, zt)
        norm = head_total(jnp.sum(a * a, axis=1, keepdims=True))
        gn = -head_total(jnp.sum(gz * at, axis=1, keepdims=True)) / (norm * norm)
        ga = ga + gz.T / norm + 2.0 * a * gn
        gsc = jnp.where(mask, a * (ga - jnp.sum(a * ga, axis=1, keepdims=True)), 0.0) * SCALE
        out_ref[0:LANDMARKS] = gs
        out_ref[LANDMARKS : 2 * LANDMARKS] = collect(mm(gsc, spread(k_ref[...])))
        out_ref[2 * LANDMARKS : 3 * LANDMARKS] = g[LANDMARKS:] + collect(
            mm(gsc.T, spread(q_ref[...]))
        )
        centre = jnp.sum(spread(gs * sm), axis=1, keepdims=True)
        out_ref[3 * LANDMARKS : 3 * LANDMARKS + 8] = jnp.broadcast_to(centre, (n, n)).T[0:8]

    return call(
        body, [((3 * LANDMARKS + 8, n), f32)], (parts, qm, km, summary, a, zs, ps, t2s, t3s),
        cost=(2 * n**3 * 6 * 52 * 4, 4 * 26 * n * n),
    )[0]


def far_pull(e, top, mixed, marks, qm, k, v, gatt, prev, nxt, vprev, vnext, taps, flipped, inside,
             icounts, valid):
    rows, width = k.shape
    chunk = rows * RIM // prev.shape[0]

    def body(e_ref, top_ref, mix_ref, mk_ref, qm_ref, k_ref, v_ref, ga_ref, prev_ref, next_ref,
             vprev_ref, vnext_ref, flip_ref, in_ref, ic_ref, valid_ref,
             gk_ref, gv_ref, gq_ref, cg_ref, gv):
        tops = mix_ref[LANDMARKS : LANDMARKS + 1]
        scale = jnp.exp(top_ref[...] - tops) / mix_ref[LANDMARKS + 1 : LANDMARKS + 2]
        ins = in_ref[...]
        ins3 = jnp.concatenate([ins, ins, ins], axis=1)
        for b in range(width // 256):
            at = slice(256 * b, 256 * (b + 1))
            far = e_ref[:, at] * scale[:, at]
            gs = spread(mk_ref[0:LANDMARKS, at])
            gf = dot3(v_ref[:, at], gs, NT)
            sc = far * (gf - mk_ref[3 * LANDMARKS : 3 * LANDMARKS + 1, at]) * SCALE
            gv[:, at] = dot3(far, gs, NN)
            gq_ref[:, at] = collect(dot3(sc, k_ref[:, at], TN))
            gkm = mk_ref[2 * LANDMARKS : 3 * LANDMARKS, at] * ic_ref[...]
            gk = dot3(sc, spread(qm_ref[:, at]), NN) + dg(
                ins3, jnp.concatenate(split3(gkm), axis=0), NN
            )
            gk_ref[:, at] = gk.astype(bf16)
        for b in range(width // 128):
            at = slice(128 * b, 128 * (b + 1))
            flip_here = flip_ref[:, at]
            sums = [None] * TAPS
            for c in range(rows // chunk):
                here = slice(chunk * c, chunk * (c + 1))
                gv[here, at] += conv_block(
                    padded_chunk(ga_ref, prev_ref, next_ref, c, chunk, at), flip_here, chunk
                )
                vp = padded_chunk(v_ref, vprev_ref, vnext_ref, c, chunk, at)
                ga = ga_ref[here, at]
                for res in range(8):
                    sh = vp if res == 0 else vp[res : res + chunk + 24]
                    for a in range(5):
                        r = 8 * a + res
                        if r < TAPS:
                            prod = ga * sh[8 * a : 8 * a + chunk]
                            s = prod[0:8]
                            for j in range(1, chunk // 8):
                                s = s + prod[8 * j : 8 * (j + 1)]
                            sums[r] = s if sums[r] is None else sums[r] + s
            for r in range(TAPS):
                cg_ref[r : r + 1, at] = jnp.sum(sums[r], axis=0, keepdims=True)
        gv_ref[...] = (gv[...] * valid_ref[...]).astype(bf16)

    args = (e, top, mixed, marks, qm, k, v, gatt, prev, nxt, vprev, vnext, flipped, inside,
            icounts, valid)
    outs = [((rows, width), bf16)] * 2 + [((LANDMARKS, width), f32), ((TAPS, width), f32)]
    return call(
        body, outs, args, scratch=[pltpu.VMEM((rows, width), f32)],
        cost=(2 * rows * width * 256 * 15, 12 * 4 * rows * width),
    )


def input_pull(gqn, gqm, marks, inside, icounts, gk, gv, gr1, wq, wk, wv, layer):
    rows, width = gqn.shape
    half = width // 2

    def body(gqn_ref, gqm_ref, mk_ref, in_ref, ic_ref, gk_ref, gv_ref, gr1_ref,
             q0, q1, k0, k1, v0, v1, gq_ref, gx_ref):
        ins = in_ref[...]
        ins3 = jnp.concatenate([ins, ins, ins], axis=1)
        gm = (gqm_ref[...] + mk_ref[LANDMARKS : 2 * LANDMARKS]) * ic_ref[...]
        gq = (gqn_ref[...] + dg(ins3, jnp.concatenate(split3(gm), axis=0), NN)).astype(bf16)
        gq_ref[...] = gq
        gx = gr1_ref[...]
        for g, w0, w1 in ((gq, q0, q1), (gk_ref[...], k0, k1), (gv_ref[...], v0, v1)):
            gx = gx + (dg(g[:, :half], w0[0], NT) + dg(g[:, half:], w1[0], NT))
        gx_ref[...] = gx

    first = (gqn, gqm, marks, inside, icounts, gk, gv, gr1)
    args = (*first, *wq, *wk, *wv)
    specs = [whole(a) for a in first] + [of_layer(w, layer) for w in (*wq, *wk, *wv)]
    outs = [((rows, width), bf16), ((rows, width), f32)]
    return call(
        body, outs, args, specs, [whole(jax.ShapeDtypeStruct(*o)) for o in outs], (1,),
        cost=(2 * rows * width * 3 * width, 8 * 4 * rows * width),
    )


def partner(x, axis, mask):
    n = lax.axis_size(axis)
    return lax.ppermute(x, axis, [(i, i ^ mask) for i in range(n)])


def swap(x):
    return partner(x, "core", 1)


def sum_over(x, axis):
    n = lax.axis_size(axis)
    if n <= 4:
        parts = [partner(x, axis, m) for m in range(1, n)]
        for p in parts:
            x = x + p
        return x
    bit = 1
    while bit < n:
        x = x + partner(x, axis, bit)
        bit *= 2
    return x


def by_core(own, oth, axis):
    first = lax.axis_index("core") == 0
    return jnp.where(
        first, jnp.concatenate([own, oth], axis=axis), jnp.concatenate([oth, own], axis=axis)
    )


def sum_doc(x):
    first = lax.axis_index("core") == 0
    half = x.shape[1] // 2
    keep = jnp.where(first, x[:, :half], x[:, half:])
    send = jnp.where(first, x[:, half:], x[:, :half])
    total = sum_over(keep + swap(send), "part")
    return by_core(total, swap(total), 1)


def sum_heads(x):
    half = x.shape[1] // 2
    total = sum_over(x[:, :half] + swap(x[:, half:]), "part")
    return jnp.concatenate([total, swap(total)], axis=1)


def owner_pieces(x):
    half = x.shape[1] // 2
    owners = half // OWN_COLS
    parts = lax.axis_size("part")
    zero = jnp.zeros((x.shape[0], OWN_COLS), x.dtype)

    def pieces(at):
        return jnp.stack(
            [x[:, at + p * OWN_COLS : at + (p + 1) * OWN_COLS] if p < owners else zero
             for p in range(parts)]
        )

    own, oth = pieces(0), pieces(half)
    first = lax.axis_index("core") == 0
    out = jnp.where(first, jnp.stack([own, oth], axis=1), jnp.stack([oth, own], axis=1))
    return out.reshape(2 * parts, x.shape[0], OWN_COLS)


def to_owners(x):
    return lax.all_to_all(owner_pieces(x), ("part", "core"), 0, 0, tiled=True)


def from_owners(x, owners):
    got = lax.all_gather(x, ("part", "core"), axis=0)
    got = got.reshape(-1, 2, *x.shape)[:owners]
    cols = [jnp.concatenate([got[p, c] for p in range(owners)], axis=1) for c in range(2)]
    return by_core(cols[0], cols[1], 1)


def own_slice(x):
    owners = x.shape[1] // 2 // OWN_COLS
    p = jnp.minimum(lax.axis_index("part"), owners - 1)
    return lax.dynamic_slice_in_dim(x, p * OWN_COLS, OWN_COLS, axis=1)


def xor_order(x, index):
    n = x.shape[0]
    bit = 1
    while bit < n:
        other = jnp.stack([x[k ^ bit] for k in range(n)])
        x = jnp.where((index & bit) > 0, other, x)
        bit *= 2
    return x


def to_docs(x):
    x = xor_order(x, lax.axis_index("doc"))
    got = [x[0]] + [partner(x[k], "doc", k) for k in range(1, x.shape[0])]
    return jnp.concatenate(got, axis=0)


def from_docs(x, docs):
    x = x.reshape(docs, -1, x.shape[-1])
    got = [x[0]] + [partner(x[k], "doc", k) for k in range(1, docs)]
    return xor_order(jnp.stack(got), lax.axis_index("doc"))


def rims(x, docs):
    rows = x.shape[0] // docs
    width = x.shape[1]
    chunks = x.reshape(docs, rows, width)
    parts = lax.axis_size("part")
    n = 2 * parts
    me = 2 * lax.axis_index("part") + lax.axis_index("core")
    doc = lax.axis_index("doc")
    axes = ("part", "core")
    prev = lax.ppermute(chunks[:, rows - RIM :], axes, [(i, (i + 1) % n) for i in range(n)])
    nxt = lax.ppermute(chunks[:, :RIM], axes, [((i + 1) % n, i) for i in range(n)])
    half = width // 2
    prev, nxt = (
        jnp.concatenate([a[..., half:], a[..., :half]], axis=-1) for a in (prev, nxt)
    )
    zero = jnp.zeros((1, RIM, width), x.dtype)
    before = xor_order(jnp.concatenate([zero, xor_order(prev, doc)[:-1]]), doc)
    after = xor_order(jnp.concatenate([xor_order(nxt, doc)[1:], zero]), doc)
    prev = jnp.where(me == 0, before, prev)
    nxt = jnp.where(me == n - 1, after, nxt)
    return prev.reshape(docs * RIM, width), nxt.reshape(docs * RIM, width)


def halve_parts(x, low_first):
    me = lax.axis_index("part")
    n = x.shape[1]
    bit = 1 if low_first else n // 2
    while n > 1:
        if low_first:
            v = x.reshape(x.shape[0], n // 2, 2, *x.shape[2:])
            axis = 2
        else:
            v = x.reshape(x.shape[0], 2, n // 2, *x.shape[2:])
            axis = 1
        mine = (me & bit) // bit
        keep = lax.dynamic_index_in_dim(v, mine, axis, keepdims=False)
        send = lax.dynamic_index_in_dim(v, 1 - mine, axis, keepdims=False)
        got = partner(send, "part", bit)
        x = (keep.astype(f32) + got.astype(f32)).astype(bf16)
        n //= 2
        bit = bit * 2 if low_first else bit // 2
    return x[:, 0]


def reduce_rows(grad):
    docs, parts = lax.axis_size("doc"), lax.axis_size("part")
    rows, cols = grad.shape
    x = grad.reshape(docs, parts, rows // (docs * parts), cols)
    cut = (cols // 256) * 128
    x = jnp.concatenate(
        [halve_parts(x[..., :cut], True), halve_parts(x[..., cut:], False)], axis=-1
    )
    x = xor_order(x, lax.axis_index("doc"))
    total = x[0].astype(f32)
    for k in range(1, docs):
        total = total + partner(x[k], "doc", k).astype(f32)
    return total


def weight_grad(left, right):
    return dg(left, right, TN).astype(bf16)


def both(x):
    return jnp.concatenate([x, swap(x)], axis=0)


def both_own(x):
    half = x.shape[1] // 2
    return jnp.concatenate([x[:, :half], swap(x[:, half:])], axis=0)


def local(inputs, cotangent, lengths, query_weight, key_weight, value_weight, conv_weight,
          out_weight, gain_one, shift_one, up_weight, up_bias, down_weight, gain_two, shift_two):
    docs, chunk, width = inputs.shape
    parts = lax.axis_size("part")
    doc, part, core = (lax.axis_index(a) for a in ("doc", "part", "core"))
    half = query_weight.shape[2]
    owners = half // OWN_COLS
    rows = docs * chunk

    length = lengths[doc]
    group = jnp.arange(docs, dtype=jnp.int32) ^ doc
    place = ((group * parts + part) * 2 + core) * chunk
    place = (place[:, None] + jnp.arange(chunk, dtype=jnp.int32)[None, :]).reshape(rows)
    valid = (place < length).astype(f32)[:, None]
    bounds = jnp.arange(LANDMARKS + 1, dtype=jnp.int32) * length // LANDMARKS
    inside = (
        (place[:, None] >= bounds[None, :-1]) & (place[:, None] < bounds[None, 1:])
    ).astype(bf16)
    icounts = 1.0 / (bounds[1:] - bounds[:-1]).astype(f32)[:, None]

    state = to_docs(inputs)
    grad = to_docs(cotangent)
    wq = (query_weight, swap(query_weight))
    wk = (key_weight, swap(key_weight))
    wv = (value_weight, swap(value_weight))
    wo = (out_weight, swap(out_weight))
    wu = (up_weight, swap(up_weight))
    wd = (down_weight, swap(down_weight))
    bias = jnp.concatenate([up_bias, swap(up_bias)], axis=1)
    conv = jnp.concatenate([conv_weight, swap(conv_weight)], axis=1)
    taps_all = jnp.repeat(jnp.swapaxes(conv, 1, 2), HEAD_DIM, axis=2)

    low = state
    xbar = dg(inside, low, TN)
    kept = []
    for layer in range(LAYERS):
        taps = taps_all[layer]
        xbar = sum_doc(xbar)
        q, k, v = project(low, wq, wk, wv, valid, layer)
        vprev, vnext = rims(v, docs)
        near, e, qm, km, part_sums = scores(q, k, v, xbar, icounts, wq, wk, valid, layer)
        top = part_sums[LANDMARKS : LANDMARKS + 1]
        qm_own, km_own = own_slice(qm), own_slice(km)
        inv = inverse(qm_own, km_own)
        merged, summary = merge(to_owners(part_sums), inv[1])
        mixed = from_owners(merged, owners)
        al, r1, fl, dgelu, hid, r2, nxt_state, nxt_low, nxt_xbar = forward_rows(
            near, mixed, v, vprev, vnext, taps, state, (wo, wu, wd, bias[layer : layer + 1]),
            (gain_one, shift_one, gain_two, shift_two), valid, inside, layer,
        )
        kept.append(dict(
            low=low, q=q, k=k, v=v, vprev=vprev, vnext=vnext, near=near, e=e, qm=qm, km=km, top=top,
            qm_own=qm_own, km_own=km_own, inv=inv, summary=summary, mixed=mixed, al=al, r1=r1,
            fl=fl, dgelu=dgelu, hid=hid, r2=r2, taps=taps,
        ))
        state, low, xbar = nxt_state, nxt_low, nxt_xbar
    output = from_docs(state, docs)

    mats = [None] * LAYERS
    smalls = [None] * LAYERS
    for layer in reversed(range(LAYERS)):
        s = kept[layer]
        gd, gu, gbias, gr1, gb, gatt, gqn, mk, small = backward_rows(
            grad, s["r1"], s["r2"], s["dgelu"], s["near"], s["mixed"], s["q"], s["km"],
            (wo, wu, wd), (gain_one, gain_two), valid, layer,
        )
        gprev, gnext = rims(gatt, docs)
        down_t = reduce_rows(weight_grad(both(gd), both_own(s["hid"])))
        up = reduce_rows(weight_grad(both(s["fl"]), both_own(gu)))
        out_t = reduce_rows(weight_grad(both(gb), both_own(s["al"])))
        a, zs, ps, t2s, t3s = s["inv"]
        pulled = inverse_pull(
            to_owners(mk), s["qm_own"], s["km_own"], s["summary"], a, zs, ps, t2s, t3s
        )
        marks = from_owners(pulled, owners)
        gk, gv, gqm, cg = far_pull(
            s["e"], s["top"], s["mixed"], marks, s["qm"], s["k"], s["v"], gatt, gprev, gnext,
            s["vprev"], s["vnext"], s["taps"], s["taps"][::-1], inside, icounts, valid,
        )
        gqm = sum_heads(gqm)
        gq, grad = input_pull(gqn, gqm, marks, inside, icounts, gk, gv, gr1, wq, wk, wv, layer)
        low2 = both(s["low"])
        qkv = reduce_rows(
            weight_grad(low2, jnp.concatenate([both_own(gq), both_own(gk), both_own(gv)], axis=1))
        )
        mats[layer] = (
            qkv[:, :half], qkv[:, half : 2 * half], qkv[:, 2 * half :], out_t.T, up, down_t.T
        )
        fh = gbias.shape[1] // 2
        gbias = by_core(gbias[:, :fh], gbias[:, fh:], 1)
        cg = jnp.sum(cg.reshape(TAPS, HEADS, HEAD_DIM), axis=-1).T
        cg = by_core(cg[: HEADS // 2], cg[HEADS // 2 :], 0)
        flat = [small[:4].reshape(-1), gbias.reshape(-1), cg.reshape(-1)]
        pad = -(HEADS * TAPS) % 128
        smalls[layer] = jnp.concatenate(flat + [jnp.zeros((pad,), f32)]).reshape(-1, 128)
    grad_inputs = from_docs(grad.astype(bf16), docs).astype(f32)

    small = jnp.stack(smalls)
    small = small + swap(small)
    small = sum_over(small, "part")
    small = sum_over(small, "doc").reshape(LAYERS, -1)
    vec = [small[:, i * width : (i + 1) * width] for i in range(4)]
    at = 4 * width
    ff = 2 * up_bias.shape[1]
    gbias = small[:, at : at + ff]
    gconv = small[:, at + ff : at + ff + HEADS * TAPS].reshape(LAYERS, HEADS, TAPS)
    m = [jnp.stack([mats[l][i] for l in range(LAYERS)]) for i in range(6)]
    return (
        output, grad_inputs, m[0], m[1], m[2], gconv, m[3], vec[0], vec[1], m[4], gbias, m[5],
        vec[2], vec[3],
    )


def solution(mesh):
    seq = ("doc", "part")
    rows = P(None, ("doc", "part", "core"), None)
    placed = (
        rows, rows, P(), P(None, None, "core"), P(None, None, "core"), P(None, None, "core"),
        P(None, "core", None), P(None, "core", None), P(), P(), P(None, None, "core"),
        P(None, "core"), P(None, "core", None), P(), P(),
    )
    outs = (
        rows, rows, P(None, seq, "core"), P(None, seq, "core"), P(None, seq, "core"), P(),
        P(None, "core", seq), P(), P(), P(None, seq, "core"), P(), P(None, "core", seq), P(), P(),
    )

    def run(*args):
        docs = args[0].shape[0]
        seq_size = mesh.shape["seq"]
        cut = Mesh(
            mesh.devices.reshape(docs, seq_size // docs, mesh.shape["head"]),
            ("doc", "part", "core"),
        )
        return jax.shard_map(local, mesh=cut, in_specs=placed, out_specs=outs, check_vma=False)(*args)

    return run
```

```python
import jax
import jax.numpy as jnp
from jax import lax
from jax.experimental import pallas as pl
from jax.experimental.pallas import tpu as pltpu
from jax.sharding import Mesh, PartitionSpec as P

HEADS = 12
HEAD_DIM = 64
LANDMARKS = 64
TAPS = 33
RIM = TAPS // 2
PINV_STEPS = 6
LAYERS = 2
OWN_HEADS = 2
OWN_COLS = OWN_HEADS * HEAD_DIM
SCALE = HEAD_DIM ** (-0.5)
EPS = 1e-05
MASKED = -1e30
FF_TILE = 512
VMEM_LIMIT = 52 * 1024 * 1024

f32 = jnp.float32
bf16 = jnp.bfloat16

NN = ((1,), (0,))
NT = ((1,), (1,))
TN = ((0,), (0,))


def dg(a, b, dims):
    return lax.dot_general(a, b, (dims, ((), ())), preferred_element_type=f32)


def split2(x):
    hi = x.astype(bf16)
    return hi, (x - hi.astype(f32)).astype(bf16)


def split3(x):
    hi = x.astype(bf16)
    rest = x - hi.astype(f32)
    mid = rest.astype(bf16)
    return hi, mid, (rest - mid.astype(f32)).astype(bf16)


def dot3(a, b, dims):
    a1, a2 = split2(a)
    b1, b2 = split2(b)
    return dg(a1, b1, dims) + (dg(a1, b2, dims) + dg(a2, b1, dims))


def mm(a, b):
    a1, a2, a3 = split3(a)
    b1, b2, b3 = split3(b)
    n = b.shape[1]
    top = jnp.concatenate([b1, b2, b3], axis=1)
    low = jnp.concatenate([b1, b2, jnp.zeros_like(b3)], axis=1)
    wide = dg(jnp.concatenate([a1, a2], axis=1), jnp.concatenate([top, low], axis=0), NN)
    last = dg(a3, b1, NN)
    return wide[:, :n] + (wide[:, n : 2 * n] + (wide[:, 2 * n :] + last))


def head_mask(rows, cols):
    r = lax.broadcasted_iota(jnp.int32, (rows, cols), 0) // HEAD_DIM
    c = lax.broadcasted_iota(jnp.int32, (rows, cols), 1) // HEAD_DIM
    return r == c


def spread(x):
    n = x.shape[1]
    tall = jnp.concatenate([x] * (n // HEAD_DIM), axis=0)
    return jnp.where(head_mask(n, n), tall, 0.0)


def collect(x):
    n = x.shape[1]
    x = jnp.where(head_mask(n, n), x, 0.0)
    total = x[0:HEAD_DIM]
    for h in range(1, n // HEAD_DIM):
        total = total + x[h * HEAD_DIM : (h + 1) * HEAD_DIM]
    return total


def head_max(s):
    lane = lax.broadcasted_iota(jnp.int32, s.shape, 1) // HEAD_DIM
    out = s
    for h in range(s.shape[1] // HEAD_DIM):
        top = jnp.max(jnp.where(lane == h, s, MASKED), axis=1, keepdims=True)
        out = jnp.where(lane == h, top, out)
    return out


def head_sum(e):
    n = e.shape[1]
    ones = jnp.where(head_mask(n, n), 1.0, 0.0).astype(bf16)
    e1, e2 = split2(e)
    return dg(e1, ones, NN) + dg(e2, ones, NN)


def down_form(lanes):
    n = lanes.shape[1]
    return collect(jnp.broadcast_to(lanes, (n, n)).T)


def norm_rows(r):
    mean = jnp.mean(r, axis=-1, keepdims=True)
    c = r - mean
    q = lax.rsqrt(jnp.mean(c * c, axis=-1, keepdims=True) + EPS)
    return c * q, q


def norm_pull(r, gy, gain):
    n, q = norm_rows(r)
    dgain = jnp.sum(gy * n, axis=0, keepdims=True)
    dshift = jnp.sum(gy, axis=0, keepdims=True)
    a = gy * gain
    am = jnp.mean(a, axis=-1, keepdims=True)
    anm = jnp.mean(a * n, axis=-1, keepdims=True)
    return q * (a - am - n * anm), dgain, dshift


def conv_block(padded, taps, rows, flip=False):
    acc = None
    for res in range(8):
        sh = padded if res == 0 else padded[res : res + rows + 24]
        for a in range(5):
            r = 8 * a + res
            if r < TAPS:
                t = TAPS - 1 - r if flip else r
                term = sh[8 * a : 8 * a + rows] * taps[t : t + 1]
                acc = term if acc is None else acc + term
    return acc


def place():
    return lax.axis_index("part"), lax.axis_index("core")


def padded_chunk(mid_ref, prev_ref, next_ref, c, rows, lanes, chunks):
    part, core = place()
    parts = lax.axis_size("part")
    first = jnp.where(jnp.logical_and(part == 0, core == 0), 1, 0)
    last = jnp.where(jnp.logical_and(part == parts - 1, core == 1), 1, 0)
    zero_before = jnp.logical_and(first == 1, c == 0)
    zero_after = jnp.logical_and(last == 1, c == chunks - 1)
    at_prev = RIM * jnp.maximum(c - first, 0)
    at_next = RIM * jnp.minimum(c + last, chunks - 1)
    before = prev_ref[pl.ds(pl.multiple_of(at_prev, RIM), RIM), lanes]
    after = next_ref[pl.ds(pl.multiple_of(at_next, RIM), RIM), lanes]
    return jnp.concatenate(
        [
            jnp.where(zero_before, 0.0, before),
            mid_ref[rows * c : rows * (c + 1), lanes],
            jnp.where(zero_after, 0.0, after),
        ],
        axis=0,
    )


def write_rims(x, tail_ref, head_ref, chunks):
    rows = x.shape[0] // chunks
    half = x.shape[1] // 2
    for c in range(chunks):
        here = slice(RIM * c, RIM * (c + 1))
        for ref, at in ((tail_ref, rows * (c + 1) - RIM), (head_ref, rows * c)):
            ref[here, :half] = x[at : at + RIM, half:]
            ref[here, half:] = x[at : at + RIM, :half]


def write_pieces(out_ref, rows, own, oth):
    _, core = place()
    parts = out_ref.shape[0] // 2
    for p in range(parts):
        out_ref[2 * p + core, rows] = own(p)
        out_ref[2 * p + 1 - core, rows] = oth(p)


def read_owned(got_ref, rows, owners):
    _, core = place()
    return jnp.concatenate(
        [got_ref[2 * p + core, rows] for p in range(owners)]
        + [got_ref[2 * p + 1 - core, rows] for p in range(owners)],
        axis=1,
    )


def own_lanes(owners):
    at = jnp.minimum(place()[0], owners - 1) * OWN_COLS
    return pl.ds(pl.multiple_of(at, OWN_COLS), OWN_COLS)


ANY = pl.BlockSpec(memory_space=pl.ANY)


class In:
    def __init__(self, buf, src=None, sem=None):
        self.buf, self.shape, self.dtype = buf, buf.shape, buf.dtype
        self.copy = None
        if src is not None:
            self.copy = pltpu.make_async_copy(src, buf, sem)
            self.copy.start()

    def wait(self):
        if self.copy is not None:
            self.copy.wait()
            self.copy = None

    def __getitem__(self, at):
        self.wait()
        return self.buf[at]


class Out:
    def __init__(self, buf, dst, next_sem, flushed):
        self.dst, self.buf, self.shape, self.dtype = dst, buf, buf.shape, buf.dtype
        self.next_sem, self.flushed, self.done = next_sem, flushed, dst is None

    def __getitem__(self, at):
        return self.buf[at]

    def __setitem__(self, at, value):
        self.buf[at] = value

    def flush(self, at=None):
        if self.dst is None:
            return
        src, dst = (self.buf, self.dst) if at is None else (self.buf.at[at], self.dst.at[at])
        copy = pltpu.make_async_copy(src, dst, self.next_sem())
        copy.start()
        self.flushed.append(copy)
        self.done = True


def call(body, ins, outs, scratch=(), cost=(0, 0), after=()):
    n, extra = len(ins), len(after)
    late = [x for x in ins if isinstance(x, tuple)]
    shapes = [x[0] if x[1] is None else jax.eval_shape(lambda v, at=x[1]: v[at], x[0]) for x in late]
    kinds = [("hbm",) if len(o) == 2 else ("vmem", "hbm") if o[2] else ("vmem",) for o in outs]
    flat = [(o[0], o[1], k) for o, ks in zip(outs, kinds) for k in ks]
    alone = [o for o in outs if len(o) == 2]

    def kernel(*refs):
        given_refs = refs[:n]
        made_refs = list(refs[n + extra : n + extra + len(flat)])
        rest = refs[n + extra + len(flat) :]
        bufs = list(rest[: len(shapes) + len(alone)])
        user, sems = rest[len(shapes) + len(alone) : -1], rest[-1]
        count = [0]

        def next_sem():
            count[0] += 1
            return sems.at[count[0] - 1]

        given, made, flushed = [], [], []
        for ref, x in zip(given_refs, ins):
            if isinstance(x, tuple):
                src = ref if x[1] is None else ref.at[x[1]]
                given.append(In(bufs.pop(0), src, next_sem()))
            else:
                given.append(In(ref))
        for ks in kinds:
            buf = made_refs.pop(0) if "vmem" in ks else bufs.pop(0)
            dst = made_refs.pop(0) if "hbm" in ks else None
            made.append(Out(buf, dst, next_sem, flushed))
        body(given, made, *user)
        for x in given:
            x.wait()
        for o in made:
            if not o.done:
                o.flush()
        for copy in flushed:
            copy.wait()

    space = {"vmem": pl.BlockSpec(memory_space=pltpu.VMEM), "hbm": pl.BlockSpec(memory_space=pltpu.HBM)}
    scratch_shapes = [pltpu.VMEM(x.shape, x.dtype) for x in shapes]
    scratch_shapes += [pltpu.VMEM(o[0], o[1]) for o in alone] + list(scratch)
    scratch_shapes += [pltpu.SemaphoreType.DMA((len(shapes) + 4 * len(outs) + 24,))]
    got = list(pl.pallas_call(
        kernel,
        out_shape=[jax.ShapeDtypeStruct(shape, t) for shape, t, _ in flat],
        in_specs=[space["hbm" if isinstance(x, tuple) else "vmem"] for x in ins] + [ANY] * extra,
        out_specs=[space[k] for _s, _t, k in flat],
        scratch_shapes=scratch_shapes,
        compiler_params=pltpu.CompilerParams(vmem_limit_bytes=VMEM_LIMIT),
        cost_estimate=pl.CostEstimate(flops=cost[0], bytes_accessed=cost[1], transcendentals=0),
    )(*[x[0] if isinstance(x, tuple) else x for x in ins], *after))
    return [tuple(got.pop(0) for _ in ks) if len(ks) == 2 else got.pop(0) for ks in kinds]


def far_off(*arrays):
    return [(x, None) for x in arrays]


class Cols:
    def __init__(self, ref, start, size):
        self.ref, self.start, self.size = ref, start, size
        self.shape = (ref.shape[0], size)

    def _at(self, at):
        if at is Ellipsis:
            return slice(None), slice(self.start, self.start + self.size)
        rows, cols = at
        first, last = cols.start or 0, self.size if cols.stop is None else cols.stop
        return rows, slice(self.start + first, self.start + last)

    def __getitem__(self, at):
        return self.ref[self._at(at)]

    def __setitem__(self, at, value):
        self.ref[self._at(at)] = value


def lanes_of(x, at, size):
    return x, (slice(None), slice(at, at + size))


def prepare_taps(conv):
    layers, _, taps = conv.shape
    width = HEADS * HEAD_DIM

    def body(ins, outs):
        (c_ref,), (t_ref,) = ins, outs
        at = lax.broadcasted_iota(jnp.int32, (16, width), 1) // HEAD_DIM
        hot = jnp.where(lax.broadcasted_iota(jnp.int32, (16, width), 0) == at, 1.0, 0.0).astype(bf16)
        for layer in range(layers):
            c1, c2, c3 = split3(c_ref[layer])
            t_ref[layer] = dg(c1, hot, TN) + (dg(c2, hot, TN) + dg(c3, hot, TN))

    return call(body, [conv], [((layers, taps, width), f32, None)])[0]


def project(xr, weights, valid, layer, chunks, after=()):
    rows, width = xr.shape
    half = width // 2

    def body(ins, outs):
        x_ref, valid_ref, w0, w1 = ins
        out, tail_ref, head_ref = outs
        x = x_ref[...]
        va = valid_ref[...]
        for i in range(3):
            cols = slice(i * half, (i + 1) * half)
            for w, at in ((w0, 2 * i * half), (w1, (2 * i + 1) * half)):
                p = dg(x, w[:, cols], NN)
                out[:, at : at + half] = p * va if i == 2 else p
        out.flush()
        write_rims(Cols(out, 2 * width, width), tail_ref, head_ref, chunks)

    outs = [((rows, 3 * width), f32)] + [((RIM * chunks, width), f32, None)] * 2
    return call(
        body, [xr, valid] + [(w, layer) for w in weights], outs, after=after,
        cost=(2 * rows * width * 6 * half, 4 * width * 6 * half),
    )


def scores(qkv, xtot, xoth, icounts, weights, valid, layer, parts):
    rows, width = qkv.shape[0], qkv.shape[1] // 3
    half = width // 2
    owners = half // OWN_COLS
    pieces = 2 * parts

    def body(ins, outs, part):
        xt_ref, xo_ref, ic_ref, w0, w1, valid_ref, kv_ref, q_ref = ins
        ne_ref, marks_ref, qk_ref, out_ref = outs
        k_ref, v_ref = (Cols(kv_ref, i * width, width) for i in range(2))
        near_ref, e_ref = (Cols(ne_ref, i * width, width) for i in range(2))
        qm_ref, km_ref = (Cols(marks_ref, i * width, width) for i in range(2))
        _, core = place()
        mark = slice(0, LANDMARKS)
        xt, xo = xt_ref[...], xo_ref[...]
        xb = jnp.concatenate(
            [jnp.where(core == 0, xt, xo), jnp.where(core == 0, xo, xt)], axis=1
        )
        x1, x2, x3 = split3(xb * ic_ref[...])
        xs = jnp.concatenate([x1, x2, x3], axis=0)
        for w, at in ((w0, 0), (w1, half)):
            p = dg(xs, w[...], NN)
            p = p[:LANDMARKS] + (p[LANDMARKS : 2 * LANDMARKS] + p[2 * LANDMARKS :])
            qm_ref[mark, at : at + half] = p[:, :half]
            km_ref[mark, at : at + half] = p[:, half:]
        own = pl.multiple_of(jnp.minimum(place()[0], owners - 1) * OWN_COLS, OWN_COLS)
        qk_ref[mark] = marks_ref[mark, pl.ds(own, OWN_COLS)]
        qk_ref[LANDMARKS : 2 * LANDMARKS] = marks_ref[mark, pl.ds(width + own, OWN_COLS)]
        live = valid_ref[...] > 0
        for b in range(width // 256):
            at = slice(256 * b, 256 * (b + 1))
            s = dot3(k_ref[:, at], spread(qm_ref[mark, at] * SCALE), NT)
            s = jnp.where(live, s, MASKED)
            top = jnp.max(s, axis=0, keepdims=True)
            e = jnp.where(live, jnp.exp(s - top), 0.0)
            e_ref[:, at] = e
            part[mark, at] = collect(dot3(e, v_ref[:, at], TN))
            last = jnp.concatenate(
                [top, jnp.sum(e, axis=0, keepdims=True), jnp.zeros((6, 256), f32)], axis=0
            )
            part[LANDMARKS : LANDMARKS + 8, at] = last
            qm_ref[LANDMARKS : LANDMARKS + 8, at] = last
            km_ref[LANDMARKS : LANDMARKS + 8, at] = jnp.zeros((8, 256), f32)
        marks_ref.flush()

        def cols(base):
            def piece(p):
                if p >= owners:
                    return jnp.zeros((LANDMARKS + 8, OWN_COLS), f32)
                return part[:, base + p * OWN_COLS : base + (p + 1) * OWN_COLS]
            return piece

        write_pieces(out_ref, slice(None), cols(0), cols(half))
        for b in range(width // 256):
            at = slice(256 * b, 256 * (b + 1))
            s = dot3(q_ref[:, at] * SCALE, spread(km_ref[mark, at]), NT)
            e = jnp.exp(s - head_max(s))
            near_ref[:, at] = e / head_sum(e)
        ne_ref.flush()

    ins = [xtot, xoth, icounts]
    ins += [(w, (layer, slice(None), slice(0, width))) for w in weights]
    ins += [valid, lanes_of(qkv, width, 2 * width), lanes_of(qkv, 0, width)]
    outs = [((rows, 2 * width), f32), ((LANDMARKS + 8, 2 * width), f32)]
    outs += [((2 * LANDMARKS, OWN_COLS), f32, None), ((pieces, LANDMARKS + 8, OWN_COLS), f32, None)]
    return call(
        body, ins, outs, [pltpu.VMEM((LANDMARKS + 8, width), f32)],
        cost=(2 * rows * width * 256 * 9, 10 * 4 * rows * width),
    )


def eye(n):
    return jnp.where(
        lax.broadcasted_iota(jnp.int32, (n, n), 0) == lax.broadcasted_iota(jnp.int32, (n, n), 1),
        1.0, 0.0,
    )


def head_total(column):
    n = column.shape[0]
    row = lax.broadcasted_iota(jnp.int32, (n, 1), 0) // HEAD_DIM
    out = column
    for h in range(n // HEAD_DIM):
        s = jnp.sum(column[h * HEAD_DIM : (h + 1) * HEAD_DIM], axis=0, keepdims=True)
        out = jnp.where(row == h, s, out)
    return out


def inverse(qk):
    n = OWN_COLS

    def body(ins, outs):
        (qk_ref,) = ins
        kept_ref, end_ref = outs
        ident = eye(n)
        s = mm(spread(qk_ref[:LANDMARKS] * SCALE), spread(qk_ref[LANDMARKS:]).T)
        s = jnp.where(head_mask(n, n), s, MASKED)
        e = jnp.exp(s - jnp.max(s, axis=1, keepdims=True))
        a = e / jnp.sum(e, axis=1, keepdims=True)
        kept_ref[0] = a
        kept_ref[1] = qk_ref[...]
        z = a.T / head_total(jnp.sum(a * a, axis=1, keepdims=True))
        for step in range(PINV_STEPS):
            p = mm(a, z)
            t2 = 15.0 * ident - mm(p, 7.0 * ident - p)
            t3 = 13.0 * ident - mm(p, t2)
            for i, m in enumerate((z, p, t2, t3)):
                kept_ref[3 + 4 * step + i] = m
            z = 0.25 * mm(z, t3)
        kept_ref[2] = z
        end_ref[...] = z

    outs = [((3 + 4 * PINV_STEPS, n, n), f32), ((n, n), f32, None)]
    return call(body, [qk], outs, cost=(2 * n**3 * 6 * 25 * 4, 4 * 26 * n * n))


def merge(parts, z):
    count, rows, n = parts.shape

    def body(ins, outs):
        (p_ref, z_ref), (out_ref, sum_ref) = ins, outs
        top = p_ref[0, LANDMARKS : LANDMARKS + 1]
        for d in range(1, count):
            top = jnp.maximum(top, p_ref[d, LANDMARKS : LANDMARKS + 1])
        total = jnp.zeros_like(top)
        carried = jnp.zeros((LANDMARKS, n), f32)
        for d in range(count):
            w = jnp.exp(p_ref[d, LANDMARKS : LANDMARKS + 1] - top)
            total = total + w * p_ref[d, LANDMARKS + 1 : LANDMARKS + 2]
            carried = carried + down_form(w) * p_ref[d, 0:LANDMARKS]
        summary = carried / down_form(total)
        sum_ref[...] = summary
        mixed = collect(mm(z_ref[...], spread(summary)))
        last = jnp.concatenate([top, total, jnp.zeros((6, n), f32)], axis=0)
        for d in range(count):
            out_ref[d, 0:LANDMARKS] = mixed
            out_ref[d, LANDMARKS : LANDMARKS + 8] = last

    return call(body, [parts, z], [((count, rows, n), f32, None), ((LANDMARKS, n), f32, None)])


def halves(x):
    half = x.shape[1] // 2
    first = place()[1] == 0
    left, right = x[:, :half], x[:, half:]
    return jnp.where(first, left, right), jnp.where(first, right, left)


def forward_rows(ne, got, qkv, prev, nxt, taps, x, weights, gains, valid, inside, layer, after=()):
    wo, wu, wd, bias = weights
    rows, width = x.shape
    chunks = prev.shape[0] // RIM
    chunk = rows // chunks
    half = width // 2
    owners = half // OWN_COLS
    ffh = wu[0].shape[2]
    tiles = ffh // FF_TILE

    def body(ins, outs, att):
        (v_ref, prev_ref, next_ref, taps_ref, got_ref, near_ref, x_ref, g1, s1, bias_ref, g2, s2,
         valid_ref, in_ref, o0, o1, u0, d0, u1, d1) = ins
        mix_ref, pack_ref, own_ref, rr_ref, dgelu_ref, xn_ref, xr_ref, keep_ref, send_ref = outs
        for b in range(width // 128):
            at = slice(128 * b, 128 * (b + 1))
            taps_here = taps_ref[layer, :, at]
            for c in range(chunks):
                padded = padded_chunk(v_ref, prev_ref, next_ref, c, chunk, at, chunks)
                att[chunk * c : chunk * (c + 1), at] = conv_block(padded, taps_here, chunk)
        mix_ref[...] = read_owned(got_ref, slice(None), owners)
        mix_ref.flush()
        for b in range(width // 256):
            at = slice(256 * b, 256 * (b + 1))
            att[:, at] += dot3(near_ref[:, at], spread(mix_ref[0:LANDMARKS, at]), NN)
        low = att[...].astype(bf16)
        own_ref[:, :half] = low[:, :half]
        pack_ref[:, width : width + half] = low[:, half:]
        r1 = x_ref[...].astype(f32) + (
            dg(low[:, :half], o0[...], NN) + dg(low[:, half:], o1[...], NN)
        )
        rr_ref[:, :width] = r1
        n, _q = norm_rows(r1)
        first = n * g1[layer : layer + 1] + s1[layer : layer + 1]
        pack_ref[:, :width] = first.astype(bf16)
        att[...] = first
        for t in range(2 * tiles):
            at = slice(t * FF_TILE, (t + 1) * FF_TILE)
            here = slice(t % tiles * FF_TILE, (t % tiles + 1) * FF_TILE)
            u, d = ((u0, d0), (u1, d1))[t // tiles]
            up = dg(pack_ref[:, :width], u[:, here], NN) + bias_ref[:, at]
            phi = 0.5 * (1.0 + lax.erf(up * (0.5**0.5)))
            dgelu_ref[:, at] = (
                phi + up * (jnp.exp(-0.5 * up * up) * 0.3989422804014327)
            ).astype(dgelu_ref.dtype)
            hid = (up * phi).astype(bf16)
            if t < tiles:
                own_ref[:, half + here.start : half + here.stop] = hid
            else:
                base = width + half
                pack_ref[:, base + here.start : base + here.stop] = hid
            att[...] += dg(hid, d[here], NN)
            if t == tiles - 1:
                own_ref.flush()
        dgelu_ref.flush()
        r2 = att[...]
        rr_ref[:, width:] = r2
        rr_ref.flush()
        n, _q = norm_rows(r2)
        xn = (n * g2[layer : layer + 1] + s2[layer : layer + 1]) * valid_ref[...]
        xn_ref[...] = xn
        xr = xn.astype(bf16)
        xr_ref[...] = xr
        pack_ref[:, width + half + ffh :] = xr
        pack_ref.flush()
        keep_ref[...], send_ref[...] = halves(dg(in_ref[...], xr, TN))

    g1, s1, g2, s2 = gains
    at = lambda w: (w, layer)
    ins = [lanes_of(qkv, 2 * width, width), prev, nxt, taps, got, lanes_of(ne, 0, width), x, g1, s1, bias, g2, s2, valid, inside,
           at(wo[0]), at(wo[1]), at(wu[0]), at(wd[0]), at(wu[1]), at(wd[1])]
    outs = [((LANDMARKS + 8, width), f32), ((rows, 2 * width + half + ffh), bf16),
            ((rows, half + ffh), bf16), ((rows, 2 * width), f32), ((rows, 2 * ffh), bf16),
            ((rows, width), f32, None), ((rows, width), bf16, None),
            ((LANDMARKS, half), f32, None), ((LANDMARKS, half), f32, None)]
    return call(
        body, ins, outs, [pltpu.VMEM((rows, width), f32)],
        cost=(2 * rows * width * (4 * ffh + width) * 2, 30 * rows * width * 4), after=after,
    )


def backward_rows(g, rr, dgelu, ne, mixed, qkv, marks, weights, gains, valid, layer, chunks, parts,
                  after=()):
    wo, wu, wd = weights
    rows, width = rr.shape[0], rr.shape[1] // 2
    half = width // 2
    owners = half // OWN_COLS
    ffh = wu[0].shape[2]
    tiles = ffh // FF_TILE
    pieces = 2 * parts

    def body(ins, outs, acc, mk):
        (g_ref, g2, valid_ref, g1, rr_ref, dgelu_ref, d0, u0, d1, u1, o0, o1, near_ref, mix_ref,
         km_ref, q_ref) = ins
        (pack_ref, gu_ref, bias_ref, gr1_ref, gatt_ref, gqn_ref, out_ref, small_ref,
         tail_ref, head_ref) = outs
        mark = slice(0, LANDMARKS)
        gy = g_ref[...].astype(f32) * valid_ref[...]
        gr2, dgain, dshift = norm_pull(rr_ref[:, width:], gy, g2[layer : layer + 1])
        acc[...] = gr2
        pack_ref[:, :width] = gr2.astype(bf16)
        small_ref[2:3] = dgain
        small_ref[3:4] = dshift
        for t in range(2 * tiles):
            at = slice(t * FF_TILE, (t + 1) * FF_TILE)
            here = slice(t % tiles * FF_TILE, (t % tiles + 1) * FF_TILE)
            u, d = ((u0, d0), (u1, d1))[t // tiles]
            gh = dg(pack_ref[:, :width], d[here], NT)
            gu = (gh * dgelu_ref[:, at].astype(f32)).astype(bf16)
            bias_ref[:, at] = jnp.sum(gu.astype(f32), axis=0, keepdims=True)
            if t < tiles:
                gu_ref[:, here] = gu
            else:
                pack_ref[:, 2 * width + here.start : 2 * width + here.stop] = gu
            acc[...] += dg(gu, u[:, here], NT)
            if t == tiles - 1:
                gu_ref.flush()
        gr1, dgain, dshift = norm_pull(rr_ref[:, :width], acc[...], g1[layer : layer + 1])
        small_ref[0:1] = dgain
        small_ref[1:2] = dshift
        small_ref[4:8] = jnp.zeros((4, width), f32)
        gr1_ref[...] = gr1
        gb = gr1.astype(bf16)
        pack_ref[:, width : 2 * width] = gb
        pack_ref.flush()
        gatt_ref[:, :half] = dg(gb, o0[...], NT)
        gatt_ref[:, half:] = dg(gb, o1[...], NT)
        write_rims(gatt_ref, tail_ref, head_ref, chunks)
        for b in range(width // 256):
            at = slice(256 * b, 256 * (b + 1))
            gatt = gatt_ref[:, at]
            nr = near_ref[:, at]
            gn = dot3(gatt, spread(mix_ref[mark, at]), NT)
            gs = nr * (gn - head_sum(nr * gn)) * SCALE
            gqn_ref[:, at] = dot3(gs, spread(km_ref[mark, at]), NN)
            mk[mark, at] = collect(dot3(nr, gatt, TN))
            mk[LANDMARKS:, at] = collect(dot3(gs, q_ref[:, at], TN))

        def cols(base):
            def piece(p):
                if p >= owners:
                    return jnp.zeros((2 * LANDMARKS, OWN_COLS), f32)
                return mk[:, base + p * OWN_COLS : base + (p + 1) * OWN_COLS]
            return piece

        write_pieces(out_ref, slice(None), cols(0), cols(half))

    g1, g2 = gains
    at = lambda w: (w, layer)
    ins = [g, g2, valid, g1, *far_off(rr, dgelu), at(wd[0]), at(wu[0]), at(wd[1]), at(wu[1]),
           at(wo[0]), at(wo[1]), lanes_of(ne, 0, width), (mixed, None), lanes_of(marks, width, width),
           lanes_of(qkv, 0, width)]
    row = ((rows, width), f32, None)
    rim = ((RIM * chunks, width), f32, None)
    outs = [((rows, 2 * width + ffh), bf16), ((rows, ffh), bf16), ((1, 2 * ffh), f32, None),
            row, row, row, ((pieces, 2 * LANDMARKS, OWN_COLS), f32, None), ((8, width), f32, None),
            rim, rim]
    return call(
        body, ins, outs,
        [pltpu.VMEM((rows, width), f32), pltpu.VMEM((2 * LANDMARKS, width), f32)],
        cost=(2 * rows * width * (4 * ffh + width) * 2, 30 * rows * width * 4), after=after,
    )


def inverse_pull(parts, summary, kept, after=()):
    count, rows, n = parts.shape

    def body(ins, outs):
        s_ref, g_ref, kept_ref = ins
        (out_ref,) = outs
        ident = eye(n)
        mask = head_mask(n, n)
        g = g_ref[0]
        for d in range(1, count):
            g = g + g_ref[d]
        gm = spread(g[0:LANDMARKS])
        sm = s_ref[...]
        sb = spread(sm)
        a = kept_ref[0]
        at = a.T
        gz = mm(gm, sb.T)
        gs = collect(mm(kept_ref[2].T, gm))
        ga = jnp.zeros((n, n), f32)
        for step in reversed(range(PINV_STEPS)):
            z, p, t2, t3 = (kept_ref[3 + 4 * step + i] for i in range(4))
            zt, pt = z.T, p.T
            gt3 = 0.25 * mm(zt, gz)
            gt2 = -mm(pt, gt3)
            gt1 = -mm(pt, gt2)
            gp = -(mm(gt3, t2.T) + mm(gt2, (7.0 * ident - p).T) + gt1)
            gz = 0.25 * mm(gz, t3.T) + mm(at, gp)
            ga = ga + mm(gp, zt)
        norm = head_total(jnp.sum(a * a, axis=1, keepdims=True))
        gn = -head_total(jnp.sum(gz * at, axis=1, keepdims=True)) / (norm * norm)
        ga = ga + gz.T / norm + 2.0 * a * gn
        gsc = jnp.where(mask, a * (ga - jnp.sum(a * ga, axis=1, keepdims=True)), 0.0) * SCALE
        centre = jnp.sum(spread(gs * sm), axis=1, keepdims=True)
        out = jnp.concatenate(
            [
                gs,
                collect(mm(gsc, spread(kept_ref[1, LANDMARKS:]))),
                g[LANDMARKS:] + collect(mm(gsc.T, spread(kept_ref[1, :LANDMARKS]))),
                jnp.broadcast_to(centre, (n, n)).T[0:8],
            ],
            axis=0,
        )
        for d in range(count):
            out_ref[d] = out

    return call(
        body, [summary, parts, (kept, None)],
        [((count, 3 * LANDMARKS + 8, n), f32, None)],
        cost=(2 * n**3 * 6 * 52 * 4, 4 * 26 * n * n), after=after,
    )[0]


def conv_pull(qkv, gatt, prev, nxt, vprev, vnext, taps, layer, after=()):
    rows, width = gatt.shape
    chunks = prev.shape[0] // RIM
    chunk = rows // chunks

    def body(ins, outs):
        v_ref, vprev_ref, vnext_ref, ga_ref, taps_ref, prev_ref, next_ref = ins
        gv_ref, cg_ref = outs
        for b in range(width // 128):
            at = slice(128 * b, 128 * (b + 1))
            taps_here = taps_ref[layer, :, at]
            sums = [None] * TAPS
            for c in range(chunks):
                here = slice(chunk * c, chunk * (c + 1))
                gv_ref[here, at] = conv_block(
                    padded_chunk(ga_ref, prev_ref, next_ref, c, chunk, at, chunks),
                    taps_here, chunk, flip=True,
                )
                vp = padded_chunk(v_ref, vprev_ref, vnext_ref, c, chunk, at, chunks)
                ga = ga_ref[here, at]
                for res in range(8):
                    sh = vp if res == 0 else vp[res : res + chunk + 24]
                    for a in range(5):
                        r = 8 * a + res
                        if r < TAPS:
                            prod = ga * sh[8 * a : 8 * a + chunk]
                            s = prod[0:8]
                            for j in range(1, chunk // 8):
                                s = s + prod[8 * j : 8 * (j + 1)]
                            sums[r] = s if sums[r] is None else sums[r] + s
            for r in range(TAPS):
                cg_ref[r : r + 1, at] = jnp.sum(sums[r], axis=0, keepdims=True)
        cg_ref[TAPS:] = jnp.zeros((40 - TAPS, width), f32)

    return call(
        body, [lanes_of(qkv, 2 * width, width), vprev, vnext, gatt, taps, prev, nxt],
        [((rows, width), f32, None), ((40, width), f32, None)],
        cost=(2 * rows * width * TAPS * 40, 4 * 4 * rows * width), after=after,
    )


def far_pull(ne, marks, mixed, got, qkv, gvc, inside, icounts, valid, after=()):
    rows, width = gvc.shape
    half = width // 2
    owners = half // OWN_COLS

    def body(ins, outs, mk, gq):
        got_ref, mix_ref, in_ref, ic_ref, e_ref, kv_ref, qm_ref, gvc_ref, valid_ref = ins
        gk_ref, gv_ref, gmid_ref, own_ref, oth_ref = outs
        k_ref, v_ref = (Cols(kv_ref, i * width, width) for i in range(2))
        mark = slice(0, LANDMARKS)
        mk[...] = read_owned(got_ref, slice(None), owners)
        gmid_ref[...] = mk[LANDMARKS : 2 * LANDMARKS]
        tops = mix_ref[LANDMARKS : LANDMARKS + 1, :]
        scale = jnp.exp(qm_ref[LANDMARKS : LANDMARKS + 1, :] - tops)
        scale = scale / mix_ref[LANDMARKS + 1 : LANDMARKS + 2, :]
        ins3 = jnp.concatenate([in_ref[...]] * 3, axis=1)
        live = valid_ref[...]
        for b in range(width // 256):
            at = slice(256 * b, 256 * (b + 1))
            far = e_ref[:, at] * scale[:, at]
            gs = spread(mk[mark, at])
            gf = dot3(v_ref[:, at], gs, NT)
            sc = far * (gf - mk[3 * LANDMARKS : 3 * LANDMARKS + 1, at]) * SCALE
            gq[:, at] = collect(dot3(sc, k_ref[:, at], TN))
            gv = dot3(far, gs, NN) + gvc_ref[:, at]
            gv_ref[:, at] = (gv * live).astype(bf16)
            gkm = mk[2 * LANDMARKS : 3 * LANDMARKS, at] * ic_ref[...]
            gk = dot3(sc, spread(qm_ref[mark, at]), NN) + dg(
                ins3, jnp.concatenate(split3(gkm), axis=0), NN
            )
            gk_ref[:, at] = gk.astype(bf16)
        own_ref[...] = gq[:, :half]
        oth_ref[...] = gq[:, half:]

    ins = [got, (mixed, None), inside, icounts, lanes_of(ne, width, width),
           lanes_of(qkv, width, 2 * width), lanes_of(marks, 0, width), gvc, valid]
    outs = [((rows, width), bf16, None)] * 2 + [((LANDMARKS, width), f32, None)]
    outs += [((LANDMARKS, half), f32, None)] * 2
    return call(
        body, ins, outs,
        [pltpu.VMEM((3 * LANDMARKS + 8, width), f32), pltpu.VMEM((LANDMARKS, width), f32)],
        cost=(2 * rows * width * 256 * 15, 12 * 4 * rows * width), after=after,
    )


def input_pull(gqn, gtot, goth, gmid, inside, icounts, gk, gv, gr1, weights, layer, low_out,
               after=()):
    rows, width = gqn.shape
    half = width // 2

    def body(ins, outs):
        (gr1_ref, gk_ref, gv_ref, w0, w1, gqn_ref, gt_ref, go_ref, gmid_ref, in_ref, ic_ref) = ins
        own_ref, oth_ref, gx_ref = outs
        gm = jnp.concatenate([gt_ref[...], go_ref[...]], axis=1)
        gm = (gm + gmid_ref[...]) * ic_ref[...]
        ins3 = jnp.concatenate([in_ref[...]] * 3, axis=1)
        gq = (gqn_ref[...] + dg(ins3, jnp.concatenate(split3(gm), axis=0), NN)).astype(bf16)
        for i, g in enumerate((gq, gk_ref[...], gv_ref[...])):
            own_ref[:, i * half : (i + 1) * half] = g[:, :half]
            oth_ref[:, i * half : (i + 1) * half] = g[:, half:]
        gx = gr1_ref[...] + (dg(own_ref[...], w0[...], NT) + dg(oth_ref[...], w1[...], NT))
        gx_ref[...] = gx.astype(gx_ref.dtype)

    ins = [gr1, gk, gv, (weights[0], layer), (weights[1], layer), gqn, gtot, goth, gmid, inside,
           icounts]
    outs = [((rows, 3 * half), bf16, None)] * 2 + [((rows, width), low_out, None)]
    return call(
        body, ins, outs, cost=(2 * rows * width * 3 * width, 8 * 4 * rows * width), after=after,
    )


def split_rows(tmp, keep_ref, send_ref, cols, me, low_first, docs, parts, r):
    bit = 1 if low_first else parts // 2
    mine = (me // bit) % 2
    for d in range(docs):
        for m in range(parts // 2):
            to = slice((d * parts // 2 + m) * r, (d * parts // 2 + m + 1) * r)
            for ref, b in ((keep_ref, mine), (send_ref, 1 - mine)):
                block_at = d * parts + (2 * m + b if low_first else m + bit * b)
                ref[to, cols] = tmp[pl.ds(pl.multiple_of(block_at * r, r), r)]


def weight_grads(arrays, lefts, rights, tiles, docs, parts, after=()):
    cols = 384
    shapes = [
        x if not isinstance(x, tuple) or x[1] is None else jax.eval_shape(lambda v, at=x[1]: v[at], x[0])
        for x in arrays
    ]
    shapes = [x[0] if isinstance(x, tuple) else x for x in shapes]
    rows, width = shapes[0].shape[0], lefts[0][2]
    r = width // (docs * parts)
    split = r % 16 == 0
    sizes = [sum(1 for t in tiles if t[3] == dest) * cols for dest in (0, 1)]

    def body(given, outs, lt, tmp):
        me = place()[0]
        done = [0, 0]
        last = None
        for left, right, t, dest in tiles:
            if left != last:
                for side in range(2):
                    i, at = lefts[left][side]
                    lt[:, side * rows : (side + 1) * rows] = given[i][:, at : at + width].T
                last = left
            both = []
            for i, at in rights[right]:
                both.append(given[i][:, at + t * cols : at + (t + 1) * cols])
            x = dg(lt[...], jnp.concatenate(both, axis=0), NN).astype(bf16)
            to = slice(done[dest] * cols, (done[dest] + 1) * cols)
            done[dest] += 1
            mine = outs[2 * dest : 2 * dest + 2] if split else outs[dest : dest + 1]
            if split:
                tmp[...] = x
                split_rows(tmp, *mine, to, me, dest == 0, docs, parts, r)
            else:
                mine[0][:, to] = x
            if to.stop == sizes[dest]:
                for o in reversed(mine):
                    o.flush()

    outs = []
    for size in sizes:
        outs += [((width // 2, size), bf16)] * 2 if split else [((width, size), bf16)]
    return call(
        body, arrays, outs, [pltpu.VMEM((width, 2 * rows), bf16), pltpu.VMEM((width, cols), bf16)],
        cost=(2 * width * 2 * rows * cols * len(tiles), 2 * width * cols * len(tiles)), after=after,
    )


def fold(sums, docs, parts, after=()):
    ka, _, kb, _ = sums
    rows = ka.shape[0] // 2
    r = rows // docs

    def body(ins, outs, ta, tb):
        me = place()[0]
        for i, (tmp, mine) in enumerate(((ta, me // 2), (tb, me % 2))):
            keep, got = ins[2 * i : 2 * i + 2]
            keep_ref, send_ref = outs[2 * i : 2 * i + 2]
            tmp[...] = (keep[...].astype(f32) + got[...].astype(f32)).astype(bf16)
            for d in range(docs):
                to = slice(d * r, (d + 1) * r)
                for ref, m in ((send_ref, 1 - mine), (keep_ref, mine)):
                    ref[to] = tmp[pl.ds(pl.multiple_of((2 * d + m) * r, r), r)]
            send_ref.flush()
            keep_ref.flush()

    outs = [((rows, x.shape[1]), bf16) for x in (ka, ka, kb, kb)]
    scratch = [pltpu.VMEM(x.shape, bf16) for x in (ka, kb)]
    return call(body, far_off(*sums), outs, scratch, cost=(1000, 4 * ka.size), after=after)


def fold_last(sums, docs, after=()):
    ka, _, kb, _ = sums
    r = ka.shape[0] // docs
    na, nb = ka.shape[1], kb.shape[1]

    def body(ins, outs):
        a, ga, b, gb = ins
        (out,) = outs
        for d in range(docs):
            at = slice(d * r, (d + 1) * r)
            out[d, :, :na] = (a[at].astype(f32) + ga[at].astype(f32)).astype(bf16)
            out[d, :, na:] = (b[at].astype(f32) + gb[at].astype(f32)).astype(bf16)

    return call(
        body, far_off(*sums), [((docs, r, na + nb), bf16)], cost=(1000, 4 * ka.size), after=after
    )[0]


def pack_small(smalls, biases, convs, after=()):
    layers = len(smalls)
    width = smalls[0].shape[1]
    ff = biases[0].shape[1]
    nv, nb = 4 * width // 128, ff // 128
    rows = nv + nb + 40

    def body(ins, outs):
        (out_ref,) = outs
        _, core = place()
        r = lax.broadcasted_iota(jnp.int32, (width, 128), 0) // HEAD_DIM
        c = lax.broadcasted_iota(jnp.int32, (width, 128), 1)
        head = r + (HEADS // 2) * core
        head = jnp.where(head >= HEADS, head - HEADS, head)
        hot = jnp.where(head == c, 1.0, 0.0).astype(bf16)
        for layer in range(layers):
            s_ref, b_ref, c_ref = ins[3 * layer : 3 * layer + 3]
            for j in range(width // 128):
                for k in range(4):
                    out_ref[layer, k * (width // 128) + j : k * (width // 128) + j + 1] = (
                        s_ref[k : k + 1, 128 * j : 128 * (j + 1)]
                    )
            for j in range(nb):
                lane = slice(128 * j, 128 * (j + 1))
                oth = 128 * ((j + nb // 2) % nb)
                piece = jnp.where(core == 0, b_ref[:, lane], b_ref[:, oth : oth + 128])
                out_ref[layer, nv + j : nv + j + 1] = piece
            c1, c2, c3 = split3(c_ref[...])
            out_ref[layer, nv + nb :] = dg(c1, hot, NN) + (dg(c2, hot, NN) + dg(c3, hot, NN))

    ins = [x for layer in range(layers) for x in (smalls[layer], biases[layer], convs[layer])]
    return call(body, ins, [((layers, rows, 128), f32, None)], after=after)[0]


def partner(x, axis, mask):
    n = lax.axis_size(axis)
    return lax.ppermute(x, axis, [(i, i ^ mask) for i in range(n)])


def swap(x):
    return partner(x, "core", 1)


def sum_over(x, axis):
    n = lax.axis_size(axis)
    if n <= 4:
        parts = [partner(x, axis, m) for m in range(1, n)]
        for p in parts:
            x = x + p
        return x
    bit = 1
    while bit < n:
        x = x + partner(x, axis, bit)
        bit *= 2
    return x


def total_and_other(keep, send):
    parts = lax.axis_size("part")
    mine = keep + swap(send)
    got = exchange(jnp.broadcast_to(mine[None], (parts, *mine.shape)), "part")
    total = got[0]
    for p in range(1, parts):
        total = total + got[p]
    return total, swap(total)


def exchange(x, axes):
    return lax.all_to_all(x, axes, 0, 0, tiled=True)


def rims(tails, heads):
    n = 2 * lax.axis_size("part")
    axes = ("part", "core")
    return (
        lax.ppermute(tails, axes, [(i, (i + 1) % n) for i in range(n)]),
        lax.ppermute(heads, axes, [((i + 1) % n, i) for i in range(n)]),
    )


def halve_parts(keep, got, n, low_first):
    me = lax.axis_index("part")
    parts = lax.axis_size("part")
    docs = lax.axis_size("doc")
    cols = keep.shape[1]
    bit = parts // n if low_first else n // 2
    while n > 1:
        shape = (docs, n // 2, 2, -1, cols) if low_first else (docs, 2, n // 2, -1, cols)
        axis = 2 if low_first else 1
        mine = (me // bit) % 2
        k, g = keep.reshape(shape), got.reshape(shape)
        pick = lambda x, i: lax.dynamic_index_in_dim(x, i, axis, keepdims=False).astype(f32)
        send = (pick(k, 1 - mine) + pick(g, 1 - mine)).astype(bf16)
        keep = (pick(k, mine) + pick(g, mine)).astype(bf16)
        got = partner(send, "part", bit)
        n //= 2
        bit = bit * 2 if low_first else bit // 2
    return (keep.astype(f32) + got.astype(f32)).astype(bf16).reshape(docs, -1, cols)


def first_halves(outs):
    parts = lax.axis_size("part")
    docs = lax.axis_size("doc")
    if len(outs) == 2:
        pieces = []
        for x, low_first in zip(outs, (True, False)):
            bit = 1 if low_first else parts // 2
            shape = (docs, parts // 2, 2, -1, x.shape[1]) if low_first else (
                docs, 2, parts // 2, -1, x.shape[1])
            axis = 2 if low_first else 1
            mine = (lax.axis_index("part") // bit) % 2
            v = x.reshape(shape)
            for i in (mine, 1 - mine):
                pieces.append(
                    lax.dynamic_index_in_dim(v, i, axis, keepdims=False).reshape(-1, x.shape[1])
                )
        outs = pieces
    ka, sa, kb, sb = outs
    return ka, partner(sa, "part", 1), kb, partner(sb, "part", parts // 2)


def second_halves(sums, after=()):
    parts = lax.axis_size("part")
    docs = lax.axis_size("doc")
    if parts == 4 and sums[0].shape[0] // (2 * docs) % 16 == 0:
        ka, sa, kb, sb = fold(sums, docs, parts, after)
        return ka, partner(sa, "part", 2), kb, partner(sb, "part", 1)
    out = []
    for keep, got, low_first in ((*sums[:2], True), (*sums[2:], False)):
        x = halve_parts(keep, got, parts // 2, low_first).reshape(-1, keep.shape[1])
        out += [x, jnp.zeros_like(x)]
    return tuple(out)


def third(sums, after=()):
    docs = lax.axis_size("doc")
    if sums[0].shape[0] // docs % 16 == 0:
        x = fold_last(sums, docs, after)
    else:
        ka, ga, kb, gb = (x.reshape(docs, -1, x.shape[1]) for x in sums)
        x = jnp.concatenate([ka + ga, kb + gb], axis=2)
    return x


def finish(feeds, att):
    layers = len(feeds)
    docs, r, nf = feeds[0].shape
    half = att.shape[2] // (3 * layers)
    ffh = (nf - half) // 2

    def body(ins, outs):
        q_ref, k_ref, v_ref, o_ref, u_ref, d_ref = outs

        def total(ref, at, size):
            s = ref[0, :, at : at + size].astype(f32)
            for d in range(1, docs):
                s = s + ref[d, :, at : at + size].astype(f32)
            return s

        for layer in reversed(range(layers)):
            ff = ins[layers - 1 - layer]
            u_ref[layer] = total(ff, 0, ffh)
            o_ref[layer] = total(ff, ffh, half).T
            for j in range(ffh // half):
                d_ref[layer, j * half : (j + 1) * half] = total(ff, ffh + half + j * half, half).T
        for layer in range(layers):
            for j, ref in enumerate((q_ref, k_ref, v_ref)):
                ref[layer] = total(ins[layers], (3 * layer + j) * half, half)

    ins = far_off(*reversed(feeds), att)
    outs = [((layers, r, half), f32)] * 3 + [
        ((layers, half, r), f32), ((layers, r, ffh), f32), ((layers, ffh, r), f32)
    ]
    return call(body, ins, outs)


def local(inputs, cotangent, lengths, query_weight, key_weight, value_weight, conv_weight,
          out_weight, gain_one, shift_one, up_weight, up_bias, down_weight, gain_two, shift_two):
    docs, chunk, width = inputs.shape
    parts = lax.axis_size("part")
    doc, part, core = (lax.axis_index(a) for a in ("doc", "part", "core"))
    half = query_weight.shape[2]
    ffh = up_weight.shape[2]
    rows = docs * chunk
    group = ("part", "core")

    state = exchange(inputs, "doc").reshape(rows, width)
    wqkv = jnp.concatenate([query_weight, key_weight, value_weight], axis=2)
    wqkv = (wqkv, swap(wqkv))

    length = lengths[doc]
    place = ((jnp.arange(docs, dtype=jnp.int32) * parts + part) * 2 + core) * chunk
    place = (place[:, None] + jnp.arange(chunk, dtype=jnp.int32)[None, :]).reshape(rows)
    valid = (place < length).astype(f32)[:, None]
    bounds = jnp.arange(LANDMARKS + 1, dtype=jnp.int32) * length // LANDMARKS
    inside = (
        (place[:, None] >= bounds[None, :-1]) & (place[:, None] < bounds[None, 1:])
    ).astype(bf16)
    icounts = 1.0 / (bounds[1:] - bounds[:-1]).astype(f32)[:, None]

    xbar = dg(inside, state, TN)
    first = core == 0
    keep = jnp.where(first, xbar[:, : width // 2], xbar[:, width // 2 :])
    send = jnp.where(first, xbar[:, width // 2 :], xbar[:, : width // 2])
    wo = (out_weight, swap(out_weight))
    wu = (up_weight, swap(up_weight))
    wd = (down_weight, swap(down_weight))
    bias = jnp.concatenate([up_bias, swap(up_bias)], axis=1)
    conv = jnp.concatenate([conv_weight, swap(conv_weight)], axis=1)
    taps = prepare_taps(jnp.pad(conv, ((0, 0), (0, 16 - HEADS), (0, 40 - TAPS))))
    grad = exchange(cotangent, "doc").reshape(rows, width)

    low = state
    low_got = swap(state)
    kept = []
    for layer in range(LAYERS):
        xtot, xoth = total_and_other(keep, send)
        qkv, tails, heads = project(
            low, wqkv, valid, layer, docs, after=(grad, wo[1], wu[1], wd[1]) if layer == 0 else ()
        )
        vprev, vnext = rims(tails, heads)
        ne, marks, qk, pieces = scores(
            qkv, xtot, xoth, icounts, wqkv, valid, layer, parts
        )
        inv, end = inverse(qk)
        merged, summary = merge(exchange(pieces, group), end)
        mixed, pack, own, rr, dgelu, nxt_state, nxt_low, keep, send = forward_rows(
            ne, exchange(merged, group), qkv, vprev, vnext, taps, state,
            (wo, wu, wd, bias[layer : layer + 1]), (gain_one, shift_one, gain_two, shift_two),
            valid, inside, layer,
        )
        pack_got = swap(pack)
        kept.append(dict(
            low=(low, low_got), qkv=qkv, vprev=vprev, vnext=vnext, ne=ne, marks=marks,
            inv=inv, summary=summary, mixed=mixed, pack=(pack, pack_got), own=own, rr=rr,
            dgelu=dgelu,
        ))
        state, low = nxt_state, nxt_low
        at = width + half + ffh
        low_got = lanes_of(pack_got, at, width)
        kept[-1]["next_low"] = (lanes_of(pack, at, width), low_got)
    output = exchange(state.reshape(docs, chunk, width), "doc")

    smalls, biases, convs = [None] * LAYERS, [None] * LAYERS, [None] * LAYERS
    ff_sums = None
    att_args = []
    for layer in reversed(range(LAYERS)):
        s = kept[layer]
        pack, gu, gbias, gr1, gatt, gqn, pieces, small, tails, heads = backward_rows(
            grad, s["rr"], s["dgelu"], s["ne"], s["mixed"], s["qkv"], s["marks"],
            (wo, wu, wd), (gain_one, gain_two), valid, layer, docs, parts,
            after=() if ff_sums is None else (output,),
        )
        pieces = exchange(pieces, group)
        gprev, gnext = rims(tails, heads)
        pack_got = swap(pack)
        before = (gprev, gnext)
        if ff_sums is not None:
            ff_sums = second_halves(ff_sums, after=(small,))
            before = (gprev, gnext, ff_sums[0])
        pulled = inverse_pull(pieces, s["summary"], s["inv"], after=before)
        got = exchange(pulled, group)
        gvc, cg = conv_pull(
            s["qkv"], gatt, gprev, gnext, s["vprev"], s["vnext"], taps, layer, after=(pulled,)
        )
        gk, gv, gmid, gown, goth = far_pull(
            s["ne"], s["marks"], s["mixed"], got, s["qkv"], gvc, inside, icounts, valid,
        )
        gown, goth = total_and_other(gown, goth)
        fpack, fpack_got = s["pack"]
        arrays = [(pack, None), (pack_got, None), (gu, None), lanes_of(fpack, 0, width),
                  lanes_of(fpack_got, 0, width + half + ffh), (s["own"], None)]
        lefts = [((3, 0), (4, 0), width), ((0, 0), (1, 0), width), ((0, width), (1, width), width)]
        rights = [((2, 0), (1, 2 * width)), ((5, half), (4, width + half)), ((5, 0), (4, width))]
        nt = ffh // 384
        tiles = [(0, 0, j, 0) for j in range(nt)] + [(2, 2, 0, 0)] + [(1, 1, j, 1) for j in range(nt)]
        sums = weight_grads(arrays, lefts, rights, tiles, docs, parts, after=(gk,))
        before = (sums[0],)
        if ff_sums is not None:
            ff_above = third(ff_sums, after=before)
            before = (ff_above,)
            ff_above = exchange(ff_above, "doc")
        qkv, qkv_send, grad = input_pull(
            gqn, gown, goth, gmid, inside, icounts, gk, gv, gr1, wqkv, layer,
            f32 if layer > 0 else bf16, after=before,
        )
        qkv_got = swap(qkv_send)
        ff_sums = first_halves(sums)
        low_pair = s["low"] if layer == 0 else kept[layer - 1]["next_low"]
        low, low_got = low_pair if isinstance(low_pair[0], tuple) else far_off(*low_pair)
        att_args.append([low, low_got, (qkv, None), (qkv_got, None)])
        smalls[layer], biases[layer], convs[layer] = small, gbias, cg
    att_args.reverse()
    att = weight_grads(
        [x for args in att_args for x in args],
        [((4 * l, 0), (4 * l + 1, 0), width) for l in range(LAYERS)],
        [((4 * l + 2, 0), (4 * l + 3, 0)) for l in range(LAYERS)],
        [(l, l, j, l) for l in range(LAYERS) for j in range(3)], docs, parts,
    )
    grad_inputs = exchange(grad.reshape(docs, chunk, width), "doc")
    ff_sums = second_halves(ff_sums, after=(att[0], ff_above))
    att = second_halves(first_halves(att), after=(ff_sums[0], grad_inputs))
    small = pack_small(smalls, biases, convs, after=(ff_sums[0],))
    small = sum_over(small + swap(small), "part")
    ff_now = third(ff_sums, after=(att[0], small))
    small = sum_over(small, "doc")
    att = third(att, after=(ff_now, small))
    ff_now, att = exchange(ff_now, "doc"), exchange(att, "doc")
    grad_inputs = grad_inputs.astype(f32)

    nv = width // 128
    vec = [small[:, i * nv : (i + 1) * nv].reshape(LAYERS, width) for i in range(4)]
    nb = 2 * ffh // 128
    gbias = small[:, 4 * nv : 4 * nv + nb].reshape(LAYERS, 2 * ffh)
    gconv = jnp.swapaxes(small[:, 4 * nv + nb : 4 * nv + nb + TAPS, :HEADS], 1, 2)
    q, k, v, o, u, d = finish([ff_now, ff_above], att)
    return (
        output, grad_inputs, q, k, v, gconv, o, vec[0], vec[1], u, gbias, d, vec[2], vec[3],
    )


def solution(mesh):
    seq = ("doc", "part")
    rows = P(None, ("doc", "part", "core"), None)
    placed = (
        rows, rows, P(), P(None, None, "core"), P(None, None, "core"), P(None, None, "core"),
        P(None, "core", None), P(None, "core", None), P(), P(), P(None, None, "core"),
        P(None, "core"), P(None, "core", None), P(), P(),
    )
    outs = (
        rows, rows, P(None, seq, "core"), P(None, seq, "core"), P(None, seq, "core"), P(),
        P(None, "core", seq), P(), P(), P(None, seq, "core"), P(), P(None, "core", seq), P(), P(),
    )

    def run(*args):
        docs = args[0].shape[0]
        seq_size = mesh.shape["seq"]
        cut = Mesh(
            mesh.devices.reshape(docs, seq_size // docs, mesh.shape["head"]),
            ("doc", "part", "core"),
        )
        return jax.shard_map(local, mesh=cut, in_specs=placed, out_specs=outs, check_vma=False)(*args)

    return run
```

```python
import jax
import jax.numpy as jnp
from jax import lax
from jax.experimental import pallas as pl
from jax.experimental.pallas import tpu as pltpu
from jax.sharding import Mesh, PartitionSpec as P

HEADS = 12
HEAD_DIM = 64
LANDMARKS = 64
TAPS = 33
RIM = TAPS // 2
PINV_STEPS = 6
LAYERS = 2
OWN_HEADS = 2
OWN_COLS = OWN_HEADS * HEAD_DIM
SCALE = HEAD_DIM ** (-0.5)
EPS = 1e-05
MASKED = -1e30
FF_TILE = 512
VMEM_LIMIT = 52 * 1024 * 1024

f32 = jnp.float32
bf16 = jnp.bfloat16

NN = ((1,), (0,))
NT = ((1,), (1,))
TN = ((0,), (0,))


def dg(a, b, dims):
    return lax.dot_general(a, b, (dims, ((), ())), preferred_element_type=f32)


def split2(x):
    hi = x.astype(bf16)
    return hi, (x - hi.astype(f32)).astype(bf16)


def split3(x):
    hi = x.astype(bf16)
    rest = x - hi.astype(f32)
    mid = rest.astype(bf16)
    return hi, mid, (rest - mid.astype(f32)).astype(bf16)


def dot3(a, b, dims):
    a1, a2 = split2(a)
    b1, b2 = split2(b)
    return dg(a1, b1, dims) + (dg(a1, b2, dims) + dg(a2, b1, dims))


def mm(a, b):
    a1, a2, a3 = split3(a)
    b1, b2, b3 = split3(b)
    n = b.shape[1]
    top = jnp.concatenate([b1, b2, b3], axis=1)
    low = jnp.concatenate([b1, b2, jnp.zeros_like(b3)], axis=1)
    wide = dg(jnp.concatenate([a1, a2], axis=1), jnp.concatenate([top, low], axis=0), NN)
    last = dg(a3, b1, NN)
    return wide[:, :n] + (wide[:, n : 2 * n] + (wide[:, 2 * n :] + last))


def head_mask(rows, cols):
    r = lax.broadcasted_iota(jnp.int32, (rows, cols), 0) // HEAD_DIM
    c = lax.broadcasted_iota(jnp.int32, (rows, cols), 1) // HEAD_DIM
    return r == c


def spread(x):
    n = x.shape[1]
    tall = jnp.concatenate([x] * (n // HEAD_DIM), axis=0)
    return jnp.where(head_mask(n, n), tall, 0.0)


def collect(x):
    n = x.shape[1]
    x = jnp.where(head_mask(n, n), x, 0.0)
    total = x[0:HEAD_DIM]
    for h in range(1, n // HEAD_DIM):
        total = total + x[h * HEAD_DIM : (h + 1) * HEAD_DIM]
    return total


def head_max(s):
    lane = lax.broadcasted_iota(jnp.int32, s.shape, 1) // HEAD_DIM
    out = s
    for h in range(s.shape[1] // HEAD_DIM):
        top = jnp.max(jnp.where(lane == h, s, MASKED), axis=1, keepdims=True)
        out = jnp.where(lane == h, top, out)
    return out


def head_sum(e):
    n = e.shape[1]
    ones = jnp.where(head_mask(n, n), 1.0, 0.0).astype(bf16)
    e1, e2 = split2(e)
    return dg(e1, ones, NN) + dg(e2, ones, NN)


def down_form(lanes):
    n = lanes.shape[1]
    return collect(jnp.broadcast_to(lanes, (n, n)).T)


def norm_rows(r):
    mean = jnp.mean(r, axis=-1, keepdims=True)
    c = r - mean
    q = lax.rsqrt(jnp.mean(c * c, axis=-1, keepdims=True) + EPS)
    return c * q, q


def norm_pull(r, gy, gain):
    n, q = norm_rows(r)
    dgain = jnp.sum(gy * n, axis=0, keepdims=True)
    dshift = jnp.sum(gy, axis=0, keepdims=True)
    a = gy * gain
    am = jnp.mean(a, axis=-1, keepdims=True)
    anm = jnp.mean(a * n, axis=-1, keepdims=True)
    return q * (a - am - n * anm), dgain, dshift


def conv_block(padded, taps, rows, flip=False):
    acc = None
    for res in range(8):
        sh = padded if res == 0 else padded[res : res + rows + 24]
        for a in range(5):
            r = 8 * a + res
            if r < TAPS:
                t = TAPS - 1 - r if flip else r
                term = sh[8 * a : 8 * a + rows] * taps[t : t + 1]
                acc = term if acc is None else acc + term
    return acc


def place():
    return lax.axis_index("part"), lax.axis_index("core")


def padded_chunk(mid_ref, prev_ref, next_ref, c, rows, lanes, chunks):
    part, core = place()
    parts = lax.axis_size("part")
    first = jnp.where(jnp.logical_and(part == 0, core == 0), 1, 0)
    last = jnp.where(jnp.logical_and(part == parts - 1, core == 1), 1, 0)
    zero_before = jnp.logical_and(first == 1, c == 0)
    zero_after = jnp.logical_and(last == 1, c == chunks - 1)
    at_prev = RIM * jnp.maximum(c - first, 0)
    at_next = RIM * jnp.minimum(c + last, chunks - 1)
    before = prev_ref[pl.ds(pl.multiple_of(at_prev, RIM), RIM), lanes]
    after = next_ref[pl.ds(pl.multiple_of(at_next, RIM), RIM), lanes]
    return jnp.concatenate(
        [
            jnp.where(zero_before, 0.0, before),
            mid_ref[rows * c : rows * (c + 1), lanes],
            jnp.where(zero_after, 0.0, after),
        ],
        axis=0,
    )


def write_rims(x, tail_ref, head_ref, chunks):
    rows = x.shape[0] // chunks
    half = x.shape[1] // 2
    for c in range(chunks):
        here = slice(RIM * c, RIM * (c + 1))
        for ref, at in ((tail_ref, rows * (c + 1) - RIM), (head_ref, rows * c)):
            ref[here, :half] = x[at : at + RIM, half:]
            ref[here, half:] = x[at : at + RIM, :half]


def write_pieces(out_ref, rows, own, oth):
    _, core = place()
    parts = out_ref.shape[0] // 2
    for p in range(parts):
        out_ref[2 * p + core, rows] = own(p)
        out_ref[2 * p + 1 - core, rows] = oth(p)


def read_owned(got_ref, rows, owners):
    _, core = place()
    return jnp.concatenate(
        [got_ref[2 * p + core, rows] for p in range(owners)]
        + [got_ref[2 * p + 1 - core, rows] for p in range(owners)],
        axis=1,
    )


def own_lanes(owners):
    at = jnp.minimum(place()[0], owners - 1) * OWN_COLS
    return pl.ds(pl.multiple_of(at, OWN_COLS), OWN_COLS)


ANY = pl.BlockSpec(memory_space=pl.ANY)


class In:
    def __init__(self, buf, src=None, sem=None):
        self.buf, self.shape, self.dtype = buf, buf.shape, buf.dtype
        self.copy = None
        if src is not None:
            self.copy = pltpu.make_async_copy(src, buf, sem)
            self.copy.start()

    def wait(self):
        if self.copy is not None:
            self.copy.wait()
            self.copy = None

    def __getitem__(self, at):
        self.wait()
        return self.buf[at]


class Out:
    def __init__(self, buf, dst, next_sem, flushed):
        self.dst, self.buf, self.shape, self.dtype = dst, buf, buf.shape, buf.dtype
        self.next_sem, self.flushed, self.done = next_sem, flushed, dst is None

    def __getitem__(self, at):
        return self.buf[at]

    def __setitem__(self, at, value):
        self.buf[at] = value

    def flush(self, at=None):
        if self.dst is None:
            return
        src, dst = (self.buf, self.dst) if at is None else (self.buf.at[at], self.dst.at[at])
        copy = pltpu.make_async_copy(src, dst, self.next_sem())
        copy.start()
        self.flushed.append(copy)
        self.done = True


def call(body, ins, outs, scratch=(), cost=(0, 0), after=()):
    n, extra = len(ins), len(after)
    late = [x for x in ins if isinstance(x, tuple)]
    shapes = [x[0] if x[1] is None else jax.eval_shape(lambda v, at=x[1]: v[at], x[0]) for x in late]
    kinds = [("hbm",) if len(o) == 2 else ("vmem", "hbm") if o[2] else ("vmem",) for o in outs]
    flat = [(o[0], o[1], k) for o, ks in zip(outs, kinds) for k in ks]
    alone = [o for o in outs if len(o) == 2]

    def kernel(*refs):
        given_refs = refs[:n]
        made_refs = list(refs[n + extra : n + extra + len(flat)])
        rest = refs[n + extra + len(flat) :]
        bufs = list(rest[: len(shapes) + len(alone)])
        user, sems = rest[len(shapes) + len(alone) : -1], rest[-1]
        count = [0]

        def next_sem():
            count[0] += 1
            return sems.at[count[0] - 1]

        given, made, flushed = [], [], []
        for ref, x in zip(given_refs, ins):
            if isinstance(x, tuple):
                src = ref if x[1] is None else ref.at[x[1]]
                given.append(In(bufs.pop(0), src, next_sem()))
            else:
                given.append(In(ref))
        for ks in kinds:
            buf = made_refs.pop(0) if "vmem" in ks else bufs.pop(0)
            dst = made_refs.pop(0) if "hbm" in ks else None
            made.append(Out(buf, dst, next_sem, flushed))
        body(given, made, *user)
        for x in given:
            x.wait()
        for o in made:
            if not o.done:
                o.flush()
        for copy in flushed:
            copy.wait()

    space = {"vmem": pl.BlockSpec(memory_space=pltpu.VMEM), "hbm": pl.BlockSpec(memory_space=pltpu.HBM)}
    scratch_shapes = [pltpu.VMEM(x.shape, x.dtype) for x in shapes]
    scratch_shapes += [pltpu.VMEM(o[0], o[1]) for o in alone] + list(scratch)
    scratch_shapes += [pltpu.SemaphoreType.DMA((len(shapes) + 4 * len(outs) + 24,))]
    got = list(pl.pallas_call(
        kernel,
        out_shape=[jax.ShapeDtypeStruct(shape, t) for shape, t, _ in flat],
        in_specs=[space["hbm" if isinstance(x, tuple) else "vmem"] for x in ins] + [ANY] * extra,
        out_specs=[space[k] for _s, _t, k in flat],
        scratch_shapes=scratch_shapes,
        compiler_params=pltpu.CompilerParams(vmem_limit_bytes=VMEM_LIMIT),
        cost_estimate=pl.CostEstimate(flops=cost[0], bytes_accessed=cost[1], transcendentals=0),
    )(*[x[0] if isinstance(x, tuple) else x for x in ins], *after))
    return [tuple(got.pop(0) for _ in ks) if len(ks) == 2 else got.pop(0) for ks in kinds]


def far_off(*arrays):
    return [(x, None) for x in arrays]


class Cols:
    def __init__(self, ref, start, size):
        self.ref, self.start, self.size = ref, start, size
        self.shape = (ref.shape[0], size)

    def _at(self, at):
        if at is Ellipsis:
            return slice(None), slice(self.start, self.start + self.size)
        rows, cols = at
        first, last = cols.start or 0, self.size if cols.stop is None else cols.stop
        return rows, slice(self.start + first, self.start + last)

    def __getitem__(self, at):
        return self.ref[self._at(at)]

    def __setitem__(self, at, value):
        self.ref[self._at(at)] = value


def lanes_of(x, at, size):
    return x, (slice(None), slice(at, at + size))


def prepare_taps(conv):
    layers, _, taps = conv.shape
    width = HEADS * HEAD_DIM

    def body(ins, outs):
        (c_ref,), (t_ref,) = ins, outs
        at = lax.broadcasted_iota(jnp.int32, (16, width), 1) // HEAD_DIM
        hot = jnp.where(lax.broadcasted_iota(jnp.int32, (16, width), 0) == at, 1.0, 0.0).astype(bf16)
        for layer in range(layers):
            c1, c2, c3 = split3(c_ref[layer])
            t_ref[layer] = dg(c1, hot, TN) + (dg(c2, hot, TN) + dg(c3, hot, TN))

    return call(body, [conv], [((layers, taps, width), f32, None)])[0]


def scores(xr, xtot, xoth, icounts, weights, valid, layer, chunks, parts, after=()):
    rows, width = xr.shape
    half = width // 2
    owners = half // OWN_COLS
    pieces = 2 * parts

    def body(ins, outs, part):
        xt_ref, xo_ref, ic_ref, x_ref, valid_ref, w0, w1 = ins
        ne_ref, marks_ref, qk_ref, out_ref, qkv_ref, tail_ref, head_ref = outs
        q_ref, k_ref, v_ref = (Cols(qkv_ref, i * width, width) for i in range(3))
        near_ref, e_ref = (Cols(ne_ref, i * width, width) for i in range(2))
        qm_ref, km_ref = (Cols(marks_ref, i * width, width) for i in range(2))
        _, core = place()
        mark = slice(0, LANDMARKS)
        xt, xo = xt_ref[...], xo_ref[...]
        xb = jnp.concatenate(
            [jnp.where(core == 0, xt, xo), jnp.where(core == 0, xo, xt)], axis=1
        )
        x1, x2, x3 = split3(xb * ic_ref[...])
        xs = jnp.concatenate([x1, x2, x3], axis=0)
        x = x_ref[...]
        va = valid_ref[...]
        for w, at in ((w0, 0), (w1, half)):
            for i, ref in enumerate((q_ref, k_ref, v_ref)):
                p = dg(x, w[:, i * half : (i + 1) * half], NN)
                ref[:, at : at + half] = p * va if i == 2 else p
            p = dg(xs, w[:, :width], NN)
            p = p[:LANDMARKS] + (p[LANDMARKS : 2 * LANDMARKS] + p[2 * LANDMARKS :])
            qm_ref[mark, at : at + half] = p[:, :half]
            km_ref[mark, at : at + half] = p[:, half:]
        own = pl.multiple_of(jnp.minimum(place()[0], owners - 1) * OWN_COLS, OWN_COLS)
        qk_ref[mark] = marks_ref[mark, pl.ds(own, OWN_COLS)]
        qk_ref[LANDMARKS : 2 * LANDMARKS] = marks_ref[mark, pl.ds(width + own, OWN_COLS)]
        qkv_ref.flush()
        write_rims(v_ref, tail_ref, head_ref, chunks)
        live = va > 0
        for b in range(width // 256):
            at = slice(256 * b, 256 * (b + 1))
            s = dot3(k_ref[:, at], spread(qm_ref[mark, at] * SCALE), NT)
            s = jnp.where(live, s, MASKED)
            top = jnp.max(s, axis=0, keepdims=True)
            e = jnp.where(live, jnp.exp(s - top), 0.0)
            e_ref[:, at] = e
            part[mark, at] = collect(dot3(e, v_ref[:, at], TN))
            last = jnp.concatenate(
                [top, jnp.sum(e, axis=0, keepdims=True), jnp.zeros((6, 256), f32)], axis=0
            )
            part[LANDMARKS : LANDMARKS + 8, at] = last
            qm_ref[LANDMARKS : LANDMARKS + 8, at] = last
            km_ref[LANDMARKS : LANDMARKS + 8, at] = jnp.zeros((8, 256), f32)
        marks_ref.flush()

        def cols(base):
            def piece(p):
                if p >= owners:
                    return jnp.zeros((LANDMARKS + 8, OWN_COLS), f32)
                return part[:, base + p * OWN_COLS : base + (p + 1) * OWN_COLS]
            return piece

        write_pieces(out_ref, slice(None), cols(0), cols(half))
        for b in range(width // 256):
            at = slice(256 * b, 256 * (b + 1))
            s = dot3(q_ref[:, at] * SCALE, spread(km_ref[mark, at]), NT)
            e = jnp.exp(s - head_max(s))
            near_ref[:, at] = e / head_sum(e)
        ne_ref.flush()

    ins = [xtot, xoth, icounts, xr, valid] + [(w, layer) for w in weights]
    outs = [((rows, 2 * width), f32), ((LANDMARKS + 8, 2 * width), f32)]
    outs += [((2 * LANDMARKS, OWN_COLS), f32, None), ((pieces, LANDMARKS + 8, OWN_COLS), f32, None)]
    outs += [((rows, 3 * width), f32)] + [((RIM * chunks, width), f32, None)] * 2
    return call(
        body, ins, outs, [pltpu.VMEM((LANDMARKS + 8, width), f32)],
        cost=(2 * rows * width * 256 * 9, 10 * 4 * rows * width), after=after,
    )


def eye(n):
    return jnp.where(
        lax.broadcasted_iota(jnp.int32, (n, n), 0) == lax.broadcasted_iota(jnp.int32, (n, n), 1),
        1.0, 0.0,
    )


def head_total(column):
    n = column.shape[0]
    row = lax.broadcasted_iota(jnp.int32, (n, 1), 0) // HEAD_DIM
    out = column
    for h in range(n // HEAD_DIM):
        s = jnp.sum(column[h * HEAD_DIM : (h + 1) * HEAD_DIM], axis=0, keepdims=True)
        out = jnp.where(row == h, s, out)
    return out


def inverse(qk, after=()):
    n = OWN_COLS

    def body(ins, outs):
        (qk_ref,) = ins
        kept_ref, end_ref = outs
        ident = eye(n)
        s = mm(spread(qk_ref[:LANDMARKS] * SCALE), spread(qk_ref[LANDMARKS:]).T)
        s = jnp.where(head_mask(n, n), s, MASKED)
        e = jnp.exp(s - jnp.max(s, axis=1, keepdims=True))
        a = e / jnp.sum(e, axis=1, keepdims=True)
        kept_ref[0] = a
        kept_ref[1] = qk_ref[...]
        z = a.T / head_total(jnp.sum(a * a, axis=1, keepdims=True))
        for step in range(PINV_STEPS):
            p = mm(a, z)
            t2 = 15.0 * ident - mm(p, 7.0 * ident - p)
            t3 = 13.0 * ident - mm(p, t2)
            for i, m in enumerate((z, p, t2, t3)):
                kept_ref[3 + 4 * step + i] = m
            z = 0.25 * mm(z, t3)
        kept_ref[2] = z
        end_ref[...] = z

    outs = [((3 + 4 * PINV_STEPS, n, n), f32), ((n, n), f32, None)]
    return call(body, [qk], outs, cost=(2 * n**3 * 6 * 25 * 4, 4 * 26 * n * n), after=after)


def merge(parts, z):
    count, rows, n = parts.shape

    def body(ins, outs):
        (p_ref, z_ref), (out_ref, sum_ref) = ins, outs
        top = p_ref[0, LANDMARKS : LANDMARKS + 1]
        for d in range(1, count):
            top = jnp.maximum(top, p_ref[d, LANDMARKS : LANDMARKS + 1])
        total = jnp.zeros_like(top)
        carried = jnp.zeros((LANDMARKS, n), f32)
        for d in range(count):
            w = jnp.exp(p_ref[d, LANDMARKS : LANDMARKS + 1] - top)
            total = total + w * p_ref[d, LANDMARKS + 1 : LANDMARKS + 2]
            carried = carried + down_form(w) * p_ref[d, 0:LANDMARKS]
        summary = carried / down_form(total)
        sum_ref[...] = summary
        mixed = collect(mm(z_ref[...], spread(summary)))
        last = jnp.concatenate([top, total, jnp.zeros((6, n), f32)], axis=0)
        for d in range(count):
            out_ref[d, 0:LANDMARKS] = mixed
            out_ref[d, LANDMARKS : LANDMARKS + 8] = last

    return call(body, [parts, z], [((count, rows, n), f32, None), ((LANDMARKS, n), f32, None)])


def halves(x):
    half = x.shape[1] // 2
    first = place()[1] == 0
    left, right = x[:, :half], x[:, half:]
    return jnp.where(first, left, right), jnp.where(first, right, left)


def forward_rows(ne, got, qkv, prev, nxt, taps, x, weights, gains, valid, inside, layer, after=()):
    wo, wu, wd, bias = weights
    rows, width = x.shape
    chunks = prev.shape[0] // RIM
    chunk = rows // chunks
    half = width // 2
    owners = half // OWN_COLS
    ffh = wu[0].shape[2]
    tiles = ffh // FF_TILE

    def body(ins, outs, att):
        (v_ref, prev_ref, next_ref, taps_ref, got_ref, near_ref, x_ref, g1, s1, bias_ref, g2, s2,
         valid_ref, in_ref, o0, o1, u0, d0, u1, d1) = ins
        mix_ref, pack_ref, own_ref, rr_ref, dgelu_ref, xn_ref, xr_ref, keep_ref, send_ref = outs
        for b in range(width // 128):
            at = slice(128 * b, 128 * (b + 1))
            taps_here = taps_ref[layer, :, at]
            for c in range(chunks):
                padded = padded_chunk(v_ref, prev_ref, next_ref, c, chunk, at, chunks)
                att[chunk * c : chunk * (c + 1), at] = conv_block(padded, taps_here, chunk)
        mix_ref[...] = read_owned(got_ref, slice(None), owners)
        mix_ref.flush()
        for b in range(width // 256):
            at = slice(256 * b, 256 * (b + 1))
            att[:, at] += dot3(near_ref[:, at], spread(mix_ref[0:LANDMARKS, at]), NN)
        low = att[...].astype(bf16)
        own_ref[:, :half] = low[:, :half]
        pack_ref[:, width : width + half] = low[:, half:]
        r1 = x_ref[...].astype(f32) + (
            dg(low[:, :half], o0[...], NN) + dg(low[:, half:], o1[...], NN)
        )
        rr_ref[:, :width] = r1
        rr_ref.flush((slice(None), slice(0, width)))
        n, _q = norm_rows(r1)
        first = n * g1[layer : layer + 1] + s1[layer : layer + 1]
        pack_ref[:, :width] = first.astype(bf16)
        pack_ref.flush((slice(None), slice(0, width + half)))
        att[...] = first
        for t in range(2 * tiles):
            at = slice(t * FF_TILE, (t + 1) * FF_TILE)
            here = slice(t % tiles * FF_TILE, (t % tiles + 1) * FF_TILE)
            u, d = ((u0, d0), (u1, d1))[t // tiles]
            up = dg(pack_ref[:, :width], u[:, here], NN) + bias_ref[:, at]
            phi = 0.5 * (1.0 + lax.erf(up * (0.5**0.5)))
            dgelu_ref[:, at] = (
                phi + up * (jnp.exp(-0.5 * up * up) * 0.3989422804014327)
            ).astype(dgelu_ref.dtype)
            hid = (up * phi).astype(bf16)
            if t < tiles:
                own_ref[:, half + here.start : half + here.stop] = hid
            else:
                base = width + half
                pack_ref[:, base + here.start : base + here.stop] = hid
            att[...] += dg(hid, d[here], NN)
            if t == tiles - 1:
                own_ref.flush()
                dgelu_ref.flush((slice(None), slice(0, ffh)))
        dgelu_ref.flush((slice(None), slice(ffh, 2 * ffh)))
        r2 = att[...]
        rr_ref[:, width:] = r2
        rr_ref.flush((slice(None), slice(width, 2 * width)))
        n, _q = norm_rows(r2)
        xn = (n * g2[layer : layer + 1] + s2[layer : layer + 1]) * valid_ref[...]
        xn_ref[...] = xn
        xr = xn.astype(bf16)
        xr_ref[...] = xr
        pack_ref[:, width + half + ffh :] = xr
        pack_ref.flush((slice(None), slice(width + half, 2 * width + half + ffh)))
        keep_ref[...], send_ref[...] = halves(dg(in_ref[...], xr, TN))

    g1, s1, g2, s2 = gains
    at = lambda w: (w, layer)
    ins = [lanes_of(qkv, 2 * width, width), prev, nxt, taps, got, lanes_of(ne, 0, width), x, g1, s1, bias, g2, s2, valid, inside,
           at(wo[0]), at(wo[1]), at(wu[0]), at(wd[0]), at(wu[1]), at(wd[1])]
    outs = [((LANDMARKS + 8, width), f32), ((rows, 2 * width + half + ffh), bf16),
            ((rows, half + ffh), bf16), ((rows, 2 * width), f32), ((rows, 2 * ffh), bf16),
            ((rows, width), f32, None), ((rows, width), bf16, None),
            ((LANDMARKS, half), f32, None), ((LANDMARKS, half), f32, None)]
    return call(
        body, ins, outs, [pltpu.VMEM((rows, width), f32)],
        cost=(2 * rows * width * (4 * ffh + width) * 2, 30 * rows * width * 4), after=after,
    )


def backward_rows(g, rr, dgelu, ne, mixed, qkv, marks, weights, gains, valid, layer, chunks, parts,
                  after=()):
    wo, wu, wd = weights
    rows, width = rr.shape[0], rr.shape[1] // 2
    half = width // 2
    owners = half // OWN_COLS
    ffh = wu[0].shape[2]
    tiles = ffh // FF_TILE
    pieces = 2 * parts

    def body(ins, outs, acc, mk):
        (g_ref, g2, valid_ref, g1, rr_ref, dgelu_ref, d0, u0, d1, u1, o0, o1, near_ref, mix_ref,
         km_ref, q_ref) = ins
        (pack_ref, gu_ref, bias_ref, gr1_ref, gatt_ref, gqn_ref, out_ref, small_ref,
         tail_ref, head_ref) = outs
        mark = slice(0, LANDMARKS)
        gy = g_ref[...].astype(f32) * valid_ref[...]
        gr2, dgain, dshift = norm_pull(rr_ref[:, width:], gy, g2[layer : layer + 1])
        acc[...] = gr2
        pack_ref[:, :width] = gr2.astype(bf16)
        small_ref[2:3] = dgain
        small_ref[3:4] = dshift
        for t in range(2 * tiles):
            at = slice(t * FF_TILE, (t + 1) * FF_TILE)
            here = slice(t % tiles * FF_TILE, (t % tiles + 1) * FF_TILE)
            u, d = ((u0, d0), (u1, d1))[t // tiles]
            gh = dg(pack_ref[:, :width], d[here], NT)
            gu = (gh * dgelu_ref[:, at].astype(f32)).astype(bf16)
            bias_ref[:, at] = jnp.sum(gu.astype(f32), axis=0, keepdims=True)
            if t < tiles:
                gu_ref[:, here] = gu
            else:
                pack_ref[:, 2 * width + here.start : 2 * width + here.stop] = gu
            acc[...] += dg(gu, u[:, here], NT)
            if t == tiles - 1:
                gu_ref.flush()
        gr1, dgain, dshift = norm_pull(rr_ref[:, :width], acc[...], g1[layer : layer + 1])
        small_ref[0:1] = dgain
        small_ref[1:2] = dshift
        small_ref[4:8] = jnp.zeros((4, width), f32)
        gr1_ref[...] = gr1
        gb = gr1.astype(bf16)
        pack_ref[:, width : 2 * width] = gb
        pack_ref.flush()
        gatt_ref[:, :half] = dg(gb, o0[...], NT)
        gatt_ref[:, half:] = dg(gb, o1[...], NT)
        write_rims(gatt_ref, tail_ref, head_ref, chunks)
        for b in range(width // 256):
            at = slice(256 * b, 256 * (b + 1))
            gatt = gatt_ref[:, at]
            nr = near_ref[:, at]
            gn = dot3(gatt, spread(mix_ref[mark, at]), NT)
            gs = nr * (gn - head_sum(nr * gn)) * SCALE
            gqn_ref[:, at] = dot3(gs, spread(km_ref[mark, at]), NN)
            mk[mark, at] = collect(dot3(nr, gatt, TN))
            mk[LANDMARKS:, at] = collect(dot3(gs, q_ref[:, at], TN))

        def cols(base):
            def piece(p):
                if p >= owners:
                    return jnp.zeros((2 * LANDMARKS, OWN_COLS), f32)
                return mk[:, base + p * OWN_COLS : base + (p + 1) * OWN_COLS]
            return piece

        write_pieces(out_ref, slice(None), cols(0), cols(half))

    g1, g2 = gains
    at = lambda w: (w, layer)
    ins = [g, g2, valid, g1, *far_off(rr, dgelu), at(wd[0]), at(wu[0]), at(wd[1]), at(wu[1]),
           at(wo[0]), at(wo[1]), lanes_of(ne, 0, width), (mixed, None), lanes_of(marks, width, width),
           lanes_of(qkv, 0, width)]
    row = ((rows, width), f32, None)
    rim = ((RIM * chunks, width), f32, None)
    outs = [((rows, 2 * width + ffh), bf16), ((rows, ffh), bf16), ((1, 2 * ffh), f32, None),
            row, row, row, ((pieces, 2 * LANDMARKS, OWN_COLS), f32, None), ((8, width), f32, None),
            rim, rim]
    return call(
        body, ins, outs,
        [pltpu.VMEM((rows, width), f32), pltpu.VMEM((2 * LANDMARKS, width), f32)],
        cost=(2 * rows * width * (4 * ffh + width) * 2, 30 * rows * width * 4), after=after,
    )


def inverse_pull(parts, summary, kept, after=()):
    count, rows, n = parts.shape

    def body(ins, outs):
        s_ref, g_ref, kept_ref = ins
        (out_ref,) = outs
        ident = eye(n)
        mask = head_mask(n, n)
        g = g_ref[0]
        for d in range(1, count):
            g = g + g_ref[d]
        gm = spread(g[0:LANDMARKS])
        sm = s_ref[...]
        sb = spread(sm)
        a = kept_ref[0]
        at = a.T
        gz = mm(gm, sb.T)
        gs = collect(mm(kept_ref[2].T, gm))
        ga = jnp.zeros((n, n), f32)
        for step in reversed(range(PINV_STEPS)):
            z, p, t2, t3 = (kept_ref[3 + 4 * step + i] for i in range(4))
            zt, pt = z.T, p.T
            gt3 = 0.25 * mm(zt, gz)
            gt2 = -mm(pt, gt3)
            gt1 = -mm(pt, gt2)
            gp = -(mm(gt3, t2.T) + mm(gt2, (7.0 * ident - p).T) + gt1)
            gz = 0.25 * mm(gz, t3.T) + mm(at, gp)
            ga = ga + mm(gp, zt)
        norm = head_total(jnp.sum(a * a, axis=1, keepdims=True))
        gn = -head_total(jnp.sum(gz * at, axis=1, keepdims=True)) / (norm * norm)
        ga = ga + gz.T / norm + 2.0 * a * gn
        gsc = jnp.where(mask, a * (ga - jnp.sum(a * ga, axis=1, keepdims=True)), 0.0) * SCALE
        centre = jnp.sum(spread(gs * sm), axis=1, keepdims=True)
        out = jnp.concatenate(
            [
                gs,
                collect(mm(gsc, spread(kept_ref[1, LANDMARKS:]))),
                g[LANDMARKS:] + collect(mm(gsc.T, spread(kept_ref[1, :LANDMARKS]))),
                jnp.broadcast_to(centre, (n, n)).T[0:8],
            ],
            axis=0,
        )
        for d in range(count):
            out_ref[d] = out

    return call(
        body, [summary, parts, (kept, None)],
        [((count, 3 * LANDMARKS + 8, n), f32, None)],
        cost=(2 * n**3 * 6 * 52 * 4, 4 * 26 * n * n), after=after,
    )[0]


def conv_pull(qkv, gatt, prev, nxt, vprev, vnext, taps, layer, after=()):
    rows, width = gatt.shape
    chunks = prev.shape[0] // RIM
    chunk = rows // chunks

    def body(ins, outs):
        v_ref, vprev_ref, vnext_ref, ga_ref, taps_ref, prev_ref, next_ref = ins
        gv_ref, cg_ref = outs
        for b in range(width // 128):
            at = slice(128 * b, 128 * (b + 1))
            taps_here = taps_ref[layer, :, at]
            sums = [None] * TAPS
            for c in range(chunks):
                here = slice(chunk * c, chunk * (c + 1))
                gv_ref[here, at] = conv_block(
                    padded_chunk(ga_ref, prev_ref, next_ref, c, chunk, at, chunks),
                    taps_here, chunk, flip=True,
                )
                vp = padded_chunk(v_ref, vprev_ref, vnext_ref, c, chunk, at, chunks)
                ga = ga_ref[here, at]
                for res in range(8):
                    sh = vp if res == 0 else vp[res : res + chunk + 24]
                    for a in range(5):
                        r = 8 * a + res
                        if r < TAPS:
                            prod = ga * sh[8 * a : 8 * a + chunk]
                            s = prod[0:8]
                            for j in range(1, chunk // 8):
                                s = s + prod[8 * j : 8 * (j + 1)]
                            sums[r] = s if sums[r] is None else sums[r] + s
            for r in range(TAPS):
                cg_ref[r : r + 1, at] = jnp.sum(sums[r], axis=0, keepdims=True)
        cg_ref[TAPS:] = jnp.zeros((40 - TAPS, width), f32)

    return call(
        body, [lanes_of(qkv, 2 * width, width), vprev, vnext, gatt, taps, prev, nxt],
        [((rows, width), f32, None), ((40, width), f32, None)],
        cost=(2 * rows * width * TAPS * 40, 4 * 4 * rows * width), after=after,
    )


def far_pull(ne, marks, mixed, got, qkv, gvc, inside, icounts, valid, extra=()):
    rows, width = gvc.shape
    half = width // 2
    owners = half // OWN_COLS

    def body(ins, outs, mk, gq):
        got_ref, mix_ref, in_ref, ic_ref, e_ref, kv_ref, qm_ref, gvc_ref, valid_ref, *more = ins
        gk_ref, gv_ref, gmid_ref, own_ref, oth_ref = outs
        k_ref, v_ref = (Cols(kv_ref, i * width, width) for i in range(2))
        mark = slice(0, LANDMARKS)
        mk[...] = read_owned(got_ref, slice(None), owners)
        gmid_ref[...] = mk[LANDMARKS : 2 * LANDMARKS]
        tops = mix_ref[LANDMARKS : LANDMARKS + 1, :]
        scale = jnp.exp(qm_ref[LANDMARKS : LANDMARKS + 1, :] - tops)
        scale = scale / mix_ref[LANDMARKS + 1 : LANDMARKS + 2, :]
        ins3 = jnp.concatenate([in_ref[...]] * 3, axis=1)
        live = valid_ref[...]
        for b in range(width // 256):
            at = slice(256 * b, 256 * (b + 1))
            far = e_ref[:, at] * scale[:, at]
            gs = spread(mk[mark, at])
            gf = dot3(v_ref[:, at], gs, NT)
            sc = far * (gf - mk[3 * LANDMARKS : 3 * LANDMARKS + 1, at]) * SCALE
            gq[:, at] = collect(dot3(sc, k_ref[:, at], TN))
            gv = dot3(far, gs, NN) + gvc_ref[:, at]
            gv_ref[:, at] = (gv * live).astype(bf16)
            gkm = mk[2 * LANDMARKS : 3 * LANDMARKS, at] * ic_ref[...]
            gk = dot3(sc, spread(qm_ref[mark, at]), NN) + dg(
                ins3, jnp.concatenate(split3(gkm), axis=0), NN
            )
            gk_ref[:, at] = gk.astype(bf16)
        own_ref[mark] = gq[:, :half]
        oth_ref[mark] = gq[:, half:]
        for x, ref in zip(more, (own_ref, oth_ref)):
            ref[LANDMARKS:] = x[...]

    ins = [got, (mixed, None), inside, icounts, lanes_of(ne, width, width),
           lanes_of(qkv, width, 2 * width), lanes_of(marks, 0, width), gvc, valid, *extra]
    sums = LANDMARKS + (extra[0].shape[0] if extra else 0)
    outs = [((rows, width), bf16, None)] * 2 + [((LANDMARKS, width), f32, None)]
    outs += [((sums, half), f32, None)] * 2
    return call(
        body, ins, outs,
        [pltpu.VMEM((3 * LANDMARKS + 8, width), f32), pltpu.VMEM((LANDMARKS, width), f32)],
        cost=(2 * rows * width * 256 * 15, 12 * 4 * rows * width),
    )


def input_pull(gqn, gtot, goth, gmid, inside, icounts, gk, gv, gr1, weights, layer, low_out,
               after=()):
    rows, width = gqn.shape
    half = width // 2

    def body(ins, outs):
        (gr1_ref, gk_ref, gv_ref, w0, w1, gqn_ref, gt_ref, go_ref, gmid_ref, in_ref, ic_ref) = ins
        own_ref, oth_ref, gx_ref = outs
        gm = jnp.concatenate([gt_ref[:LANDMARKS], go_ref[:LANDMARKS]], axis=1)
        gm = (gm + gmid_ref[...]) * ic_ref[...]
        ins3 = jnp.concatenate([in_ref[...]] * 3, axis=1)
        gq = (gqn_ref[...] + dg(ins3, jnp.concatenate(split3(gm), axis=0), NN)).astype(bf16)
        for i, g in enumerate((gq, gk_ref[...], gv_ref[...])):
            own_ref[:, i * half : (i + 1) * half] = g[:, :half]
            oth_ref[:, i * half : (i + 1) * half] = g[:, half:]
        gx = gr1_ref[...] + (dg(own_ref[...], w0[...], NT) + dg(oth_ref[...], w1[...], NT))
        gx_ref[...] = gx.astype(gx_ref.dtype)

    ins = [gr1, gk, gv, (weights[0], layer), (weights[1], layer), gqn, gtot, goth, gmid, inside,
           icounts]
    outs = [((rows, 3 * half), bf16, None)] * 2 + [((rows, width), low_out, None)]
    return call(
        body, ins, outs, cost=(2 * rows * width * 3 * width, 8 * 4 * rows * width), after=after,
    )


def split_rows(tmp, keep_ref, send_ref, cols, me, low_first, docs, parts, r):
    bit = 1 if low_first else parts // 2
    mine = (me // bit) % 2
    for d in range(docs):
        for m in range(parts // 2):
            to = slice((d * parts // 2 + m) * r, (d * parts // 2 + m + 1) * r)
            for ref, b in ((keep_ref, mine), (send_ref, 1 - mine)):
                block_at = d * parts + (2 * m + b if low_first else m + bit * b)
                ref[to, cols] = tmp[pl.ds(pl.multiple_of(block_at * r, r), r)]


def weight_grads(arrays, lefts, rights, tiles, docs, parts, after=()):
    cols = 384
    shapes = [
        x if not isinstance(x, tuple) or x[1] is None else jax.eval_shape(lambda v, at=x[1]: v[at], x[0])
        for x in arrays
    ]
    shapes = [x[0] if isinstance(x, tuple) else x for x in shapes]
    rows, width = shapes[0].shape[0], lefts[0][2]
    r = width // (docs * parts)
    split = r % 16 == 0
    sizes = [sum(1 for t in tiles if t[3] == dest) * cols for dest in (0, 1)]

    def body(given, outs, lt, tmp):
        me = place()[0]
        done = [0, 0]
        last = None
        for left, right, t, dest in tiles:
            if left != last:
                for side in range(2):
                    i, at = lefts[left][side]
                    lt[:, side * rows : (side + 1) * rows] = given[i][:, at : at + width].T
                last = left
            both = []
            for i, at in rights[right]:
                both.append(given[i][:, at + t * cols : at + (t + 1) * cols])
            x = dg(lt[...], jnp.concatenate(both, axis=0), NN).astype(bf16)
            to = slice(done[dest] * cols, (done[dest] + 1) * cols)
            done[dest] += 1
            mine = outs[2 * dest : 2 * dest + 2] if split else outs[dest : dest + 1]
            if split:
                tmp[...] = x
                split_rows(tmp, *mine, to, me, dest == 0, docs, parts, r)
            else:
                mine[0][:, to] = x
            if to.stop == sizes[dest]:
                for o in reversed(mine):
                    o.flush()

    outs = []
    for size in sizes:
        outs += [((width // 2, size), bf16)] * 2 if split else [((width, size), bf16)]
    return call(
        body, arrays, outs, [pltpu.VMEM((width, 2 * rows), bf16), pltpu.VMEM((width, cols), bf16)],
        cost=(2 * width * 2 * rows * cols * len(tiles), 2 * width * cols * len(tiles)), after=after,
    )


def fold(sums, docs, parts, after=()):
    ka, _, kb, _ = sums
    rows = ka.shape[0] // 2
    r = rows // docs

    def body(ins, outs, ta, tb):
        me = place()[0]
        for i, (tmp, mine) in enumerate(((ta, me // 2), (tb, me % 2))):
            keep, got = ins[2 * i : 2 * i + 2]
            keep_ref, send_ref = outs[2 * i : 2 * i + 2]
            tmp[...] = (keep[...].astype(f32) + got[...].astype(f32)).astype(bf16)
            for d in range(docs):
                to = slice(d * r, (d + 1) * r)
                for ref, m in ((send_ref, 1 - mine), (keep_ref, mine)):
                    ref[to] = tmp[pl.ds(pl.multiple_of((2 * d + m) * r, r), r)]
            send_ref.flush()
            keep_ref.flush()

    outs = [((rows, x.shape[1]), bf16) for x in (ka, ka, kb, kb)]
    scratch = [pltpu.VMEM(x.shape, bf16) for x in (ka, kb)]
    return call(body, far_off(*sums), outs, scratch, cost=(1000, 4 * ka.size), after=after)


def fold_last(sums, docs, after=()):
    ka, _, kb, _ = sums
    r = ka.shape[0] // docs
    na, nb = ka.shape[1], kb.shape[1]

    def body(ins, outs):
        a, ga, b, gb = ins
        (out,) = outs
        for d in range(docs):
            at = slice(d * r, (d + 1) * r)
            out[d, :, :na] = (a[at].astype(f32) + ga[at].astype(f32)).astype(bf16)
            out[d, :, na:] = (b[at].astype(f32) + gb[at].astype(f32)).astype(bf16)

    return call(
        body, far_off(*sums), [((docs, r, na + nb), bf16)], cost=(1000, 4 * ka.size), after=after
    )[0]


SMALL_ROWS = 24


def pack_small(smalls, biases, convs):
    layers = len(smalls)
    width = smalls[0].shape[1]
    ff = biases[0].shape[1]
    nb = ff // width
    each = 4 + nb + HEADS * 128 // width

    def body(ins, outs, pack):
        _, core = place()
        r = lax.broadcasted_iota(jnp.int32, (width, 16), 0) // HEAD_DIM
        c = lax.broadcasted_iota(jnp.int32, (width, 16), 1)
        head = r + (HEADS // 2) * core
        head = jnp.where(head >= HEADS, head - HEADS, head)
        hot = jnp.where(head == c, 1.0, 0.0).astype(bf16)
        pack[...] = jnp.zeros(pack.shape, f32)
        for layer in range(layers):
            s_ref, b_ref, c_ref = ins[3 * layer : 3 * layer + 3]
            base = each * layer
            pack[base : base + 4] = s_ref[0:4]
            for j in range(nb):
                oth = (j + nb // 2) % nb
                pack[base + 4 + j : base + 5 + j] = jnp.where(
                    core == 0,
                    b_ref[:, j * width : (j + 1) * width],
                    b_ref[:, oth * width : (oth + 1) * width],
                )
            c1, c2, c3 = split3(c_ref[...])
            sums = dg(hot, c1, ((0,), (1,)))
            sums = sums + (dg(hot, c2, ((0,), (1,))) + dg(hot, c3, ((0,), (1,))))
            for h in range(HEADS):
                row, at = base + 4 + nb + h * 128 // width, h * 128 % width
                pack[row : row + 1, at : at + c_ref.shape[0]] = sums[h : h + 1]
        outs[0][...], outs[1][...] = halves(pack[...])

    ins = [x for layer in range(layers) for x in (smalls[layer], biases[layer], convs[layer])]
    out = ((SMALL_ROWS, width // 2), f32, None)
    return call(body, ins, [out, out], [pltpu.VMEM((SMALL_ROWS, width), f32)])


def partner(x, axis, mask):
    n = lax.axis_size(axis)
    return lax.ppermute(x, axis, [(i, i ^ mask) for i in range(n)])


def swap(x):
    return partner(x, "core", 1)


def sum_over(x, axis):
    n = lax.axis_size(axis)
    if n <= 4:
        parts = [partner(x, axis, m) for m in range(1, n)]
        for p in parts:
            x = x + p
        return x
    bit = 1
    while bit < n:
        x = x + partner(x, axis, bit)
        bit *= 2
    return x


def by_core(own, oth, axis):
    first = lax.axis_index("core") == 0
    return jnp.where(
        first, jnp.concatenate([own, oth], axis=axis), jnp.concatenate([oth, own], axis=axis)
    )


def total_and_other(keep, send):
    parts = lax.axis_size("part")
    mine = keep + swap(send)
    got = exchange(jnp.broadcast_to(mine[None], (parts, *mine.shape)), "part")
    total = got[0]
    for p in range(1, parts):
        total = total + got[p]
    return total, swap(total)


def xor_order(x, index):
    n = x.shape[0]
    bit = 1
    while bit < n:
        other = jnp.stack([x[k ^ bit] for k in range(n)])
        x = jnp.where((index & bit) > 0, other, x)
        bit *= 2
    return x


def exchange(x, axes):
    return lax.all_to_all(x, axes, 0, 0, tiled=True)


def rims(tails, heads):
    n = 2 * lax.axis_size("part")
    axes = ("part", "core")
    return (
        lax.ppermute(tails, axes, [(i, (i + 1) % n) for i in range(n)]),
        lax.ppermute(heads, axes, [((i + 1) % n, i) for i in range(n)]),
    )


def halve_parts(keep, got, n, low_first):
    me = lax.axis_index("part")
    parts = lax.axis_size("part")
    docs = lax.axis_size("doc")
    cols = keep.shape[1]
    bit = parts // n if low_first else n // 2
    while n > 1:
        shape = (docs, n // 2, 2, -1, cols) if low_first else (docs, 2, n // 2, -1, cols)
        axis = 2 if low_first else 1
        mine = (me // bit) % 2
        k, g = keep.reshape(shape), got.reshape(shape)
        pick = lambda x, i: lax.dynamic_index_in_dim(x, i, axis, keepdims=False).astype(f32)
        send = (pick(k, 1 - mine) + pick(g, 1 - mine)).astype(bf16)
        keep = (pick(k, mine) + pick(g, mine)).astype(bf16)
        got = partner(send, "part", bit)
        n //= 2
        bit = bit * 2 if low_first else bit // 2
    return (keep.astype(f32) + got.astype(f32)).astype(bf16).reshape(docs, -1, cols)


def first_halves(outs):
    parts = lax.axis_size("part")
    docs = lax.axis_size("doc")
    if len(outs) == 2:
        pieces = []
        for x, low_first in zip(outs, (True, False)):
            bit = 1 if low_first else parts // 2
            shape = (docs, parts // 2, 2, -1, x.shape[1]) if low_first else (
                docs, 2, parts // 2, -1, x.shape[1])
            axis = 2 if low_first else 1
            mine = (lax.axis_index("part") // bit) % 2
            v = x.reshape(shape)
            for i in (mine, 1 - mine):
                pieces.append(
                    lax.dynamic_index_in_dim(v, i, axis, keepdims=False).reshape(-1, x.shape[1])
                )
        outs = pieces
    ka, sa, kb, sb = outs
    return ka, partner(sa, "part", 1), kb, partner(sb, "part", parts // 2)


def second_halves(sums, after=()):
    parts = lax.axis_size("part")
    docs = lax.axis_size("doc")
    if parts == 4 and sums[0].shape[0] // (2 * docs) % 16 == 0:
        ka, sa, kb, sb = fold(sums, docs, parts, after)
        return ka, partner(sa, "part", 2), kb, partner(sb, "part", 1)
    out = []
    for keep, got, low_first in ((*sums[:2], True), (*sums[2:], False)):
        x = halve_parts(keep, got, parts // 2, low_first).reshape(-1, keep.shape[1])
        out += [x, jnp.zeros_like(x)]
    return tuple(out)


def third(sums, after=()):
    docs = lax.axis_size("doc")
    if sums[0].shape[0] // docs % 16 == 0:
        x = fold_last(sums, docs, after)
    else:
        ka, ga, kb, gb = (x.reshape(docs, -1, x.shape[1]) for x in sums)
        x = jnp.concatenate([ka + ga, kb + gb], axis=2)
    return x


def finish(feeds, att):
    layers = len(feeds)
    docs, r, nf = feeds[0].shape
    half = att.shape[2] // (3 * layers)
    ffh = (nf - half) // 2

    def body(ins, outs):
        q_ref, k_ref, v_ref, o_ref, u_ref, d_ref = outs

        def total(ref, at, size):
            s = ref[0, :, at : at + size].astype(f32)
            for d in range(1, docs):
                s = s + ref[d, :, at : at + size].astype(f32)
            return s

        for layer in reversed(range(layers)):
            ff = ins[layers - 1 - layer]
            u_ref[layer] = total(ff, 0, ffh)
            o_ref[layer] = total(ff, ffh, half).T
            for j in range(ffh // half):
                d_ref[layer, j * half : (j + 1) * half] = total(ff, ffh + half + j * half, half).T
        for layer in range(layers):
            for j, ref in enumerate((q_ref, k_ref, v_ref)):
                ref[layer] = total(ins[layers], (3 * layer + j) * half, half)

    ins = far_off(*reversed(feeds), att)
    outs = [((layers, r, half), f32)] * 3 + [
        ((layers, half, r), f32), ((layers, r, ffh), f32), ((layers, ffh, r), f32)
    ]
    return call(body, ins, outs)


def local(inputs, cotangent, lengths, query_weight, key_weight, value_weight, conv_weight,
          out_weight, gain_one, shift_one, up_weight, up_bias, down_weight, gain_two, shift_two):
    docs, chunk, width = inputs.shape
    parts = lax.axis_size("part")
    doc, part, core = (lax.axis_index(a) for a in ("doc", "part", "core"))
    half = query_weight.shape[2]
    ffh = up_weight.shape[2]
    rows = docs * chunk
    group = ("part", "core")

    state = exchange(inputs, "doc").reshape(rows, width)
    wqkv = jnp.concatenate([query_weight, key_weight, value_weight], axis=2)
    wqkv = (wqkv, swap(wqkv))

    length = lengths[doc]
    place = ((jnp.arange(docs, dtype=jnp.int32) * parts + part) * 2 + core) * chunk
    place = (place[:, None] + jnp.arange(chunk, dtype=jnp.int32)[None, :]).reshape(rows)
    valid = (place < length).astype(f32)[:, None]
    bounds = jnp.arange(LANDMARKS + 1, dtype=jnp.int32) * length // LANDMARKS
    inside = (
        (place[:, None] >= bounds[None, :-1]) & (place[:, None] < bounds[None, 1:])
    ).astype(bf16)
    icounts = 1.0 / (bounds[1:] - bounds[:-1]).astype(f32)[:, None]

    xbar = dg(inside, state, TN)
    first = core == 0
    keep = jnp.where(first, xbar[:, : width // 2], xbar[:, width // 2 :])
    send = jnp.where(first, xbar[:, width // 2 :], xbar[:, : width // 2])
    wo = (out_weight, swap(out_weight))
    wu = (up_weight, swap(up_weight))
    wd = (down_weight, swap(down_weight))
    bias = jnp.concatenate([up_bias, swap(up_bias)], axis=1)
    conv = jnp.concatenate([conv_weight, swap(conv_weight)], axis=1)
    taps = prepare_taps(jnp.pad(conv, ((0, 0), (0, 16 - HEADS), (0, 40 - TAPS))))
    grad = xor_order(cotangent, doc)
    grad = jnp.stack([grad[0]] + [partner(grad[d], "doc", d) for d in range(1, docs)])
    grad = xor_order(grad, doc).reshape(rows, width)

    low = state
    low_got = swap(state)
    kept = []
    for layer in range(LAYERS):
        xtot, xoth = total_and_other(keep, send)
        ne, marks, qk, pieces, qkv, tails, heads = scores(
            low, xtot, xoth, icounts, wqkv, valid, layer, docs, parts,
            after=(wo[1], wu[1], wd[1]) if layer == 0 else (),
        )
        vprev, vnext = rims(tails, heads)
        inv, end = inverse(qk, after=(grad,) if layer == 0 else ())
        merged, summary = merge(exchange(pieces, group), end)
        mixed, pack, own, rr, dgelu, nxt_state, nxt_low, keep, send = forward_rows(
            ne, exchange(merged, group), qkv, vprev, vnext, taps, state,
            (wo, wu, wd, bias[layer : layer + 1]), (gain_one, shift_one, gain_two, shift_two),
            valid, inside, layer,
        )
        pack_got = swap(pack)
        kept.append(dict(
            low=(low, low_got), qkv=qkv, vprev=vprev, vnext=vnext, ne=ne, marks=marks,
            inv=inv, summary=summary, mixed=mixed, pack=(pack, pack_got), own=own, rr=rr,
            dgelu=dgelu,
        ))
        state, low = nxt_state, nxt_low
        at = width + half + ffh
        low_got = lanes_of(pack_got, at, width)
        kept[-1]["next_low"] = (lanes_of(pack, at, width), low_got)
    output = exchange(low.reshape(docs, chunk, width), "doc")

    smalls, biases, convs = [None] * LAYERS, [None] * LAYERS, [None] * LAYERS
    ff_sums = None
    att_args = []
    for layer in reversed(range(LAYERS)):
        s = kept[layer]
        pack, gu, gbias, gr1, gatt, gqn, pieces, small, tails, heads = backward_rows(
            grad, s["rr"], s["dgelu"], s["ne"], s["mixed"], s["qkv"], s["marks"],
            (wo, wu, wd), (gain_one, gain_two), valid, layer, docs, parts,
        )
        pieces = exchange(pieces, group)
        gprev, gnext = rims(tails, heads)
        pack_got = swap(pack)
        before = (gprev, gnext)
        if ff_sums is not None:
            ff_sums = second_halves(ff_sums, after=(small, output))
            before = (gprev, gnext, ff_sums[0])
        pulled = inverse_pull(pieces, s["summary"], s["inv"], after=before)
        got = exchange(pulled, group)
        gvc, cg = conv_pull(
            s["qkv"], gatt, gprev, gnext, s["vprev"], s["vnext"], taps, layer, after=(pulled,)
        )
        smalls[layer], biases[layer], convs[layer] = small, gbias, cg
        gk, gv, gmid, gown, goth = far_pull(
            s["ne"], s["marks"], s["mixed"], got, s["qkv"], gvc, inside, icounts, valid,
            extra=pack_small(smalls, biases, convs) if layer == 0 else (),
        )
        gown, goth = total_and_other(gown, goth)
        fpack, fpack_got = s["pack"]
        arrays = [(pack, None), (pack_got, None), (gu, None), lanes_of(fpack, 0, width),
                  lanes_of(fpack_got, 0, width + half + ffh), (s["own"], None)]
        lefts = [((3, 0), (4, 0), width), ((0, 0), (1, 0), width), ((0, width), (1, width), width)]
        rights = [((2, 0), (1, 2 * width)), ((5, half), (4, width + half)), ((5, 0), (4, width))]
        nt = ffh // 384
        tiles = [(0, 0, j, 0) for j in range(nt)] + [(2, 2, 0, 0)] + [(1, 1, j, 1) for j in range(nt)]
        sums = weight_grads(arrays, lefts, rights, tiles, docs, parts, after=(gk,))
        before = (sums[0],)
        if ff_sums is not None:
            ff_above = third(ff_sums, after=before)
            before = (ff_above,)
            ff_above = exchange(ff_above, "doc")
        qkv, qkv_send, grad = input_pull(
            gqn, gown, goth, gmid, inside, icounts, gk, gv, gr1, wqkv, layer,
            f32 if layer > 0 else bf16, after=before,
        )
        qkv_got = swap(qkv_send)
        ff_sums = first_halves(sums)
        low_pair = s["low"] if layer == 0 else kept[layer - 1]["next_low"]
        low, low_got = low_pair if isinstance(low_pair[0], tuple) else far_off(*low_pair)
        att_args.append([low, low_got, (qkv, None), (qkv_got, None)])
    small = by_core(gown[LANDMARKS:], goth[LANDMARKS:], 1)
    att_args.reverse()
    att = weight_grads(
        [x for args in att_args for x in args],
        [((4 * l, 0), (4 * l + 1, 0), width) for l in range(LAYERS)],
        [((4 * l + 2, 0), (4 * l + 3, 0)) for l in range(LAYERS)],
        [(l, l, j, l) for l in range(LAYERS) for j in range(3)], docs, parts,
    )
    small = sum_over(small, "doc")
    ff_sums = second_halves(ff_sums, after=(att[0], ff_above, small))
    grad_inputs = exchange(grad.reshape(docs, chunk, width), "doc")
    ff_now = third(ff_sums, after=(grad_inputs,))
    att = second_halves(first_halves(att), after=(ff_now,))
    ff_now = exchange(ff_now, "doc")
    att = exchange(third(att, after=(ff_now,)), "doc")
    grad_inputs = grad_inputs.astype(f32)

    nb = 2 * ffh // width
    each = 4 + nb + HEADS * 128 // width
    small = small[: LAYERS * each].reshape(LAYERS, each, width)
    vec = [small[:, i] for i in range(4)]
    gbias = small[:, 4 : 4 + nb].reshape(LAYERS, 2 * ffh)
    gconv = small[:, 4 + nb :].reshape(LAYERS, HEADS, 128)[:, :, :TAPS]
    q, k, v, o, u, d = finish([ff_now, ff_above], att)
    return (
        output.astype(f32), grad_inputs, q, k, v, gconv, o, vec[0], vec[1], u, gbias, d, vec[2], vec[3],
    )


def solution(mesh):
    seq = ("doc", "part")
    rows = P(None, ("doc", "part", "core"), None)
    placed = (
        rows, rows, P(), P(None, None, "core"), P(None, None, "core"), P(None, None, "core"),
        P(None, "core", None), P(None, "core", None), P(), P(), P(None, None, "core"),
        P(None, "core"), P(None, "core", None), P(), P(),
    )
    outs = (
        rows, rows, P(None, seq, "core"), P(None, seq, "core"), P(None, seq, "core"), P(),
        P(None, "core", seq), P(), P(), P(None, seq, "core"), P(), P(None, "core", seq), P(), P(),
    )

    def run(*args):
        docs = args[0].shape[0]
        seq_size = mesh.shape["seq"]
        cut = Mesh(
            mesh.devices.reshape(docs, seq_size // docs, mesh.shape["head"]),
            ("doc", "part", "core"),
        )
        return jax.shard_map(local, mesh=cut, in_specs=placed, out_specs=outs, check_vma=False)(*args)

    return run
```

```python
import jax
import jax.numpy as jnp
from jax import lax
from jax.experimental import pallas as pl
from jax.experimental.pallas import tpu as pltpu
from jax.sharding import Mesh, PartitionSpec as P

HEADS = 12
HEAD_DIM = 64
LANDMARKS = 64
TAPS = 33
RIM = TAPS // 2
PINV_STEPS = 6
LAYERS = 2
OWN_HEADS = 2
OWN_COLS = OWN_HEADS * HEAD_DIM
SCALE = HEAD_DIM ** (-0.5)
EPS = 1e-05
MASKED = -1e30
FF_TILE = 512
VMEM_LIMIT = 52 * 1024 * 1024

f32 = jnp.float32
bf16 = jnp.bfloat16

NN = ((1,), (0,))
NT = ((1,), (1,))
TN = ((0,), (0,))


def dg(a, b, dims):
    return lax.dot_general(a, b, (dims, ((), ())), preferred_element_type=f32)


def split2(x):
    hi = x.astype(bf16)
    return hi, (x - hi.astype(f32)).astype(bf16)


def split3(x):
    hi = x.astype(bf16)
    rest = x - hi.astype(f32)
    mid = rest.astype(bf16)
    return hi, mid, (rest - mid.astype(f32)).astype(bf16)


def dot3(a, b, dims):
    a1, a2 = split2(a)
    b1, b2 = split2(b)
    return dg(a1, b1, dims) + (dg(a1, b2, dims) + dg(a2, b1, dims))


def mm(a, b):
    a1, a2, a3 = split3(a)
    b1, b2, b3 = split3(b)
    n = b.shape[1]
    top = jnp.concatenate([b1, b2, b3], axis=1)
    low = jnp.concatenate([b1, b2, jnp.zeros_like(b3)], axis=1)
    wide = dg(jnp.concatenate([a1, a2], axis=1), jnp.concatenate([top, low], axis=0), NN)
    last = dg(a3, b1, NN)
    return wide[:, :n] + (wide[:, n : 2 * n] + (wide[:, 2 * n :] + last))


def head_mask(rows, cols):
    r = lax.broadcasted_iota(jnp.int32, (rows, cols), 0) // HEAD_DIM
    c = lax.broadcasted_iota(jnp.int32, (rows, cols), 1) // HEAD_DIM
    return r == c


def spread(x):
    n = x.shape[1]
    tall = jnp.concatenate([x] * (n // HEAD_DIM), axis=0)
    return jnp.where(head_mask(n, n), tall, 0.0)


def collect(x):
    n = x.shape[1]
    x = jnp.where(head_mask(n, n), x, 0.0)
    total = x[0:HEAD_DIM]
    for h in range(1, n // HEAD_DIM):
        total = total + x[h * HEAD_DIM : (h + 1) * HEAD_DIM]
    return total


def head_max(s):
    lane = lax.broadcasted_iota(jnp.int32, s.shape, 1) // HEAD_DIM
    out = s
    for h in range(s.shape[1] // HEAD_DIM):
        top = jnp.max(jnp.where(lane == h, s, MASKED), axis=1, keepdims=True)
        out = jnp.where(lane == h, top, out)
    return out


def head_sum(e):
    n = e.shape[1]
    ones = jnp.where(head_mask(n, n), 1.0, 0.0).astype(bf16)
    e1, e2 = split2(e)
    return dg(e1, ones, NN) + dg(e2, ones, NN)


def down_form(lanes):
    n = lanes.shape[1]
    return collect(jnp.broadcast_to(lanes, (n, n)).T)


def norm_rows(r):
    mean = jnp.mean(r, axis=-1, keepdims=True)
    c = r - mean
    q = lax.rsqrt(jnp.mean(c * c, axis=-1, keepdims=True) + EPS)
    return c * q, q


def norm_pull(r, gy, gain):
    n, q = norm_rows(r)
    dgain = jnp.sum(gy * n, axis=0, keepdims=True)
    dshift = jnp.sum(gy, axis=0, keepdims=True)
    a = gy * gain
    am = jnp.mean(a, axis=-1, keepdims=True)
    anm = jnp.mean(a * n, axis=-1, keepdims=True)
    return q * (a - am - n * anm), dgain, dshift


def conv_block(padded, taps, rows, flip=False):
    acc = None
    for res in range(8):
        sh = padded if res == 0 else padded[res : res + rows + 24]
        for a in range(5):
            r = 8 * a + res
            if r < TAPS:
                t = TAPS - 1 - r if flip else r
                term = sh[8 * a : 8 * a + rows] * taps[t : t + 1]
                acc = term if acc is None else acc + term
    return acc


def place():
    return lax.axis_index("part"), lax.axis_index("core")


def padded_chunk(mid_ref, prev_ref, next_ref, c, rows, lanes, chunks):
    part, core = place()
    parts = lax.axis_size("part")
    first = jnp.where(jnp.logical_and(part == 0, core == 0), 1, 0)
    last = jnp.where(jnp.logical_and(part == parts - 1, core == 1), 1, 0)
    zero_before = jnp.logical_and(first == 1, c == 0)
    zero_after = jnp.logical_and(last == 1, c == chunks - 1)
    at_prev = RIM * jnp.maximum(c - first, 0)
    at_next = RIM * jnp.minimum(c + last, chunks - 1)
    before = prev_ref[pl.ds(pl.multiple_of(at_prev, RIM), RIM), lanes]
    after = next_ref[pl.ds(pl.multiple_of(at_next, RIM), RIM), lanes]
    return jnp.concatenate(
        [
            jnp.where(zero_before, 0.0, before),
            mid_ref[rows * c : rows * (c + 1), lanes],
            jnp.where(zero_after, 0.0, after),
        ],
        axis=0,
    )


def write_rims(x, tail_ref, head_ref, chunks):
    rows = x.shape[0] // chunks
    half = x.shape[1] // 2
    for c in range(chunks):
        here = slice(RIM * c, RIM * (c + 1))
        for ref, at in ((tail_ref, rows * (c + 1) - RIM), (head_ref, rows * c)):
            ref[here, :half] = x[at : at + RIM, half:]
            ref[here, half:] = x[at : at + RIM, :half]


def write_pieces(out_ref, rows, own, oth):
    _, core = place()
    parts = out_ref.shape[0] // 2
    for p in range(parts):
        out_ref[2 * p + core, rows] = own(p)
        out_ref[2 * p + 1 - core, rows] = oth(p)


def read_owned(got_ref, rows, owners):
    _, core = place()
    return jnp.concatenate(
        [got_ref[2 * p + core, rows] for p in range(owners)]
        + [got_ref[2 * p + 1 - core, rows] for p in range(owners)],
        axis=1,
    )


def own_lanes(owners):
    at = jnp.minimum(place()[0], owners - 1) * OWN_COLS
    return pl.ds(pl.multiple_of(at, OWN_COLS), OWN_COLS)


ANY = pl.BlockSpec(memory_space=pl.ANY)


class In:
    def __init__(self, buf, src=None, sem=None):
        self.buf, self.shape, self.dtype = buf, buf.shape, buf.dtype
        self.copy = None
        if src is not None:
            self.copy = pltpu.make_async_copy(src, buf, sem)
            self.copy.start()

    def wait(self):
        if self.copy is not None:
            self.copy.wait()
            self.copy = None

    def __getitem__(self, at):
        self.wait()
        return self.buf[at]


class Out:
    def __init__(self, buf, dst, next_sem, flushed):
        self.dst, self.buf, self.shape, self.dtype = dst, buf, buf.shape, buf.dtype
        self.next_sem, self.flushed, self.done = next_sem, flushed, dst is None

    def __getitem__(self, at):
        return self.buf[at]

    def __setitem__(self, at, value):
        self.buf[at] = value

    def flush(self, at=None):
        if self.dst is None:
            return
        src, dst = (self.buf, self.dst) if at is None else (self.buf.at[at], self.dst.at[at])
        copy = pltpu.make_async_copy(src, dst, self.next_sem())
        copy.start()
        self.flushed.append(copy)
        self.done = True


def call(body, ins, outs, scratch=(), cost=(0, 0), after=()):
    n, extra = len(ins), len(after)
    late = [x for x in ins if isinstance(x, tuple)]
    shapes = [x[0] if x[1] is None else jax.eval_shape(lambda v, at=x[1]: v[at], x[0]) for x in late]
    kinds = [("hbm",) if len(o) == 2 else ("vmem", "hbm") if o[2] else ("vmem",) for o in outs]
    flat = [(o[0], o[1], k) for o, ks in zip(outs, kinds) for k in ks]
    alone = [o for o in outs if len(o) == 2]

    def kernel(*refs):
        given_refs = refs[:n]
        made_refs = list(refs[n + extra : n + extra + len(flat)])
        rest = refs[n + extra + len(flat) :]
        bufs = list(rest[: len(shapes) + len(alone)])
        user, sems = rest[len(shapes) + len(alone) : -1], rest[-1]
        count = [0]

        def next_sem():
            count[0] += 1
            return sems.at[count[0] - 1]

        given, made, flushed = [], [], []
        for ref, x in zip(given_refs, ins):
            if isinstance(x, tuple):
                src = ref if x[1] is None else ref.at[x[1]]
                given.append(In(bufs.pop(0), src, next_sem()))
            else:
                given.append(In(ref))
        for ks in kinds:
            buf = made_refs.pop(0) if "vmem" in ks else bufs.pop(0)
            dst = made_refs.pop(0) if "hbm" in ks else None
            made.append(Out(buf, dst, next_sem, flushed))
        body(given, made, *user)
        for x in given:
            x.wait()
        for o in made:
            if not o.done:
                o.flush()
        for copy in flushed:
            copy.wait()

    space = {"vmem": pl.BlockSpec(memory_space=pltpu.VMEM), "hbm": pl.BlockSpec(memory_space=pltpu.HBM)}
    scratch_shapes = [pltpu.VMEM(x.shape, x.dtype) for x in shapes]
    scratch_shapes += [pltpu.VMEM(o[0], o[1]) for o in alone] + list(scratch)
    scratch_shapes += [pltpu.SemaphoreType.DMA((len(shapes) + 4 * len(outs) + 24,))]
    got = list(pl.pallas_call(
        kernel,
        out_shape=[jax.ShapeDtypeStruct(shape, t) for shape, t, _ in flat],
        in_specs=[space["hbm" if isinstance(x, tuple) else "vmem"] for x in ins] + [ANY] * extra,
        out_specs=[space[k] for _s, _t, k in flat],
        scratch_shapes=scratch_shapes,
        compiler_params=pltpu.CompilerParams(vmem_limit_bytes=VMEM_LIMIT),
        cost_estimate=pl.CostEstimate(flops=cost[0], bytes_accessed=cost[1], transcendentals=0),
    )(*[x[0] if isinstance(x, tuple) else x for x in ins], *after))
    return [tuple(got.pop(0) for _ in ks) if len(ks) == 2 else got.pop(0) for ks in kinds]


def far_off(*arrays):
    return [(x, None) for x in arrays]


class Cols:
    def __init__(self, ref, start, size):
        self.ref, self.start, self.size = ref, start, size
        self.shape = (ref.shape[0], size)

    def _at(self, at):
        if at is Ellipsis:
            return slice(None), slice(self.start, self.start + self.size)
        rows, cols = at
        first, last = cols.start or 0, self.size if cols.stop is None else cols.stop
        return rows, slice(self.start + first, self.start + last)

    def __getitem__(self, at):
        return self.ref[self._at(at)]

    def __setitem__(self, at, value):
        self.ref[self._at(at)] = value


def lanes_of(x, at, size):
    return x, (slice(None), slice(at, at + size))


def prepare_taps(conv):
    layers, _, taps = conv.shape
    width = HEADS * HEAD_DIM

    def body(ins, outs):
        (c_ref,), (t_ref,) = ins, outs
        at = lax.broadcasted_iota(jnp.int32, (16, width), 1) // HEAD_DIM
        hot = jnp.where(lax.broadcasted_iota(jnp.int32, (16, width), 0) == at, 1.0, 0.0).astype(bf16)
        for layer in range(layers):
            c1, c2, c3 = split3(c_ref[layer])
            t_ref[layer] = dg(c1, hot, TN) + (dg(c2, hot, TN) + dg(c3, hot, TN))

    return call(body, [conv], [((layers, taps, width), f32, None)])[0]


def project(xr, weights, valid, layer, chunks, after=()):
    rows, width = xr.shape
    half = width // 2

    def body(ins, outs):
        x_ref, valid_ref, w0, w1 = ins
        out, tail_ref, head_ref = outs
        x = x_ref[...]
        va = valid_ref[...]
        for i in range(3):
            cols = slice(i * half, (i + 1) * half)
            for w, at in ((w0, 2 * i * half), (w1, (2 * i + 1) * half)):
                p = dg(x, w[:, cols], NN)
                out[:, at : at + half] = p * va if i == 2 else p
        out.flush()
        write_rims(Cols(out, 2 * width, width), tail_ref, head_ref, chunks)

    outs = [((rows, 3 * width), f32)] + [((RIM * chunks, width), f32, None)] * 2
    return call(
        body, [xr, valid] + [(w, layer) for w in weights], outs, after=after,
        cost=(2 * rows * width * 6 * half, 4 * width * 6 * half),
    )


def scores(qkv, xtot, xoth, icounts, weights, valid, layer, parts, after=()):
    rows, width = qkv.shape[0], qkv.shape[1] // 3
    half = width // 2
    owners = half // OWN_COLS
    pieces = 2 * parts

    def body(ins, outs, part):
        xt_ref, xo_ref, ic_ref, w0, w1, valid_ref, kv_ref, q_ref = ins
        ne_ref, marks_ref, qk_ref, out_ref = outs
        k_ref, v_ref = (Cols(kv_ref, i * width, width) for i in range(2))
        near_ref, e_ref = (Cols(ne_ref, i * width, width) for i in range(2))
        qm_ref, km_ref = (Cols(marks_ref, i * width, width) for i in range(2))
        _, core = place()
        mark = slice(0, LANDMARKS)
        xt, xo = xt_ref[...], xo_ref[...]
        xb = jnp.concatenate(
            [jnp.where(core == 0, xt, xo), jnp.where(core == 0, xo, xt)], axis=1
        )
        x1, x2, x3 = split3(xb * ic_ref[...])
        xs = jnp.concatenate([x1, x2, x3], axis=0)
        for w, at in ((w0, 0), (w1, half)):
            p = dg(xs, w[...], NN)
            p = p[:LANDMARKS] + (p[LANDMARKS : 2 * LANDMARKS] + p[2 * LANDMARKS :])
            qm_ref[mark, at : at + half] = p[:, :half]
            km_ref[mark, at : at + half] = p[:, half:]
        own = pl.multiple_of(jnp.minimum(place()[0], owners - 1) * OWN_COLS, OWN_COLS)
        qk_ref[mark] = marks_ref[mark, pl.ds(own, OWN_COLS)]
        qk_ref[LANDMARKS : 2 * LANDMARKS] = marks_ref[mark, pl.ds(width + own, OWN_COLS)]
        live = valid_ref[...] > 0
        for b in range(width // 256):
            at = slice(256 * b, 256 * (b + 1))
            s = dot3(k_ref[:, at], spread(qm_ref[mark, at] * SCALE), NT)
            s = jnp.where(live, s, MASKED)
            top = jnp.max(s, axis=0, keepdims=True)
            e = jnp.where(live, jnp.exp(s - top), 0.0)
            e_ref[:, at] = e
            part[mark, at] = collect(dot3(e, v_ref[:, at], TN))
            last = jnp.concatenate(
                [top, jnp.sum(e, axis=0, keepdims=True), jnp.zeros((6, 256), f32)], axis=0
            )
            part[LANDMARKS : LANDMARKS + 8, at] = last
            qm_ref[LANDMARKS : LANDMARKS + 8, at] = last
            km_ref[LANDMARKS : LANDMARKS + 8, at] = jnp.zeros((8, 256), f32)
        marks_ref.flush()

        def cols(base):
            def piece(p):
                if p >= owners:
                    return jnp.zeros((LANDMARKS + 8, OWN_COLS), f32)
                return part[:, base + p * OWN_COLS : base + (p + 1) * OWN_COLS]
            return piece

        write_pieces(out_ref, slice(None), cols(0), cols(half))
        for b in range(width // 256):
            at = slice(256 * b, 256 * (b + 1))
            s = dot3(q_ref[:, at] * SCALE, spread(km_ref[mark, at]), NT)
            e = jnp.exp(s - head_max(s))
            near_ref[:, at] = e / head_sum(e)
        ne_ref.flush()

    ins = [xtot, xoth, icounts]
    ins += [(w, (layer, slice(None), slice(0, width))) for w in weights]
    ins += [valid, lanes_of(qkv, width, 2 * width), lanes_of(qkv, 0, width)]
    outs = [((rows, 2 * width), f32), ((LANDMARKS + 8, 2 * width), f32)]
    outs += [((2 * LANDMARKS, OWN_COLS), f32, None), ((pieces, LANDMARKS + 8, OWN_COLS), f32, None)]
    return call(
        body, ins, outs, [pltpu.VMEM((LANDMARKS + 8, width), f32)],
        cost=(2 * rows * width * 256 * 9, 10 * 4 * rows * width), after=after,
    )


def eye(n):
    return jnp.where(
        lax.broadcasted_iota(jnp.int32, (n, n), 0) == lax.broadcasted_iota(jnp.int32, (n, n), 1),
        1.0, 0.0,
    )


def head_total(column):
    n = column.shape[0]
    row = lax.broadcasted_iota(jnp.int32, (n, 1), 0) // HEAD_DIM
    out = column
    for h in range(n // HEAD_DIM):
        s = jnp.sum(column[h * HEAD_DIM : (h + 1) * HEAD_DIM], axis=0, keepdims=True)
        out = jnp.where(row == h, s, out)
    return out


def inverse(qk):
    n = OWN_COLS

    def body(ins, outs):
        (qk_ref,) = ins
        kept_ref, end_ref = outs
        ident = eye(n)
        s = mm(spread(qk_ref[:LANDMARKS] * SCALE), spread(qk_ref[LANDMARKS:]).T)
        s = jnp.where(head_mask(n, n), s, MASKED)
        e = jnp.exp(s - jnp.max(s, axis=1, keepdims=True))
        a = e / jnp.sum(e, axis=1, keepdims=True)
        kept_ref[0] = a
        kept_ref[1] = qk_ref[...]
        z = a.T / head_total(jnp.sum(a * a, axis=1, keepdims=True))
        for step in range(PINV_STEPS):
            p = mm(a, z)
            t2 = 15.0 * ident - mm(p, 7.0 * ident - p)
            t3 = 13.0 * ident - mm(p, t2)
            for i, m in enumerate((z, p, t2, t3)):
                kept_ref[3 + 4 * step + i] = m
            z = 0.25 * mm(z, t3)
        kept_ref[2] = z
        end_ref[...] = z

    outs = [((3 + 4 * PINV_STEPS, n, n), f32), ((n, n), f32, None)]
    return call(body, [qk], outs, cost=(2 * n**3 * 6 * 25 * 4, 4 * 26 * n * n))


def merge(parts, z):
    count, rows, n = parts.shape

    def body(ins, outs):
        (p_ref, z_ref), (out_ref, sum_ref) = ins, outs
        top = p_ref[0, LANDMARKS : LANDMARKS + 1]
        for d in range(1, count):
            top = jnp.maximum(top, p_ref[d, LANDMARKS : LANDMARKS + 1])
        total = jnp.zeros_like(top)
        carried = jnp.zeros((LANDMARKS, n), f32)
        for d in range(count):
            w = jnp.exp(p_ref[d, LANDMARKS : LANDMARKS + 1] - top)
            total = total + w * p_ref[d, LANDMARKS + 1 : LANDMARKS + 2]
            carried = carried + down_form(w) * p_ref[d, 0:LANDMARKS]
        summary = carried / down_form(total)
        sum_ref[...] = summary
        mixed = collect(mm(z_ref[...], spread(summary)))
        last = jnp.concatenate([top, total, jnp.zeros((6, n), f32)], axis=0)
        for d in range(count):
            out_ref[d, 0:LANDMARKS] = mixed
            out_ref[d, LANDMARKS : LANDMARKS + 8] = last

    return call(body, [parts, z], [((count, rows, n), f32, None), ((LANDMARKS, n), f32, None)])


def halves(x):
    half = x.shape[1] // 2
    first = place()[1] == 0
    left, right = x[:, :half], x[:, half:]
    return jnp.where(first, left, right), jnp.where(first, right, left)


def forward_rows(ne, got, qkv, prev, nxt, taps, x, weights, gains, valid, inside, layer, after=()):
    wo, wu, wd, bias = weights
    rows, width = x.shape
    chunks = prev.shape[0] // RIM
    chunk = rows // chunks
    half = width // 2
    owners = half // OWN_COLS
    ffh = wu[0].shape[2]
    tiles = ffh // FF_TILE

    def body(ins, outs, att):
        (v_ref, prev_ref, next_ref, taps_ref, got_ref, near_ref, x_ref, g1, s1, bias_ref, g2, s2,
         valid_ref, in_ref, o0, o1, u0, d0, u1, d1) = ins
        mix_ref, pack_ref, own_ref, rr_ref, dgelu_ref, xn_ref, xr_ref, keep_ref, send_ref = outs
        for b in range(width // 128):
            at = slice(128 * b, 128 * (b + 1))
            taps_here = taps_ref[layer, :, at]
            for c in range(chunks):
                padded = padded_chunk(v_ref, prev_ref, next_ref, c, chunk, at, chunks)
                att[chunk * c : chunk * (c + 1), at] = conv_block(padded, taps_here, chunk)
        mix_ref[...] = read_owned(got_ref, slice(None), owners)
        mix_ref.flush()
        for b in range(width // 256):
            at = slice(256 * b, 256 * (b + 1))
            att[:, at] += dot3(near_ref[:, at], spread(mix_ref[0:LANDMARKS, at]), NN)
        low = att[...].astype(bf16)
        own_ref[:, :half] = low[:, :half]
        pack_ref[:, width : width + half] = low[:, half:]
        r1 = x_ref[...].astype(f32) + (
            dg(low[:, :half], o0[...], NN) + dg(low[:, half:], o1[...], NN)
        )
        rr_ref[:, :width] = r1
        n, _q = norm_rows(r1)
        first = n * g1[layer : layer + 1] + s1[layer : layer + 1]
        pack_ref[:, :width] = first.astype(bf16)
        att[...] = first
        for t in range(2 * tiles):
            at = slice(t * FF_TILE, (t + 1) * FF_TILE)
            here = slice(t % tiles * FF_TILE, (t % tiles + 1) * FF_TILE)
            u, d = ((u0, d0), (u1, d1))[t // tiles]
            up = dg(pack_ref[:, :width], u[:, here], NN) + bias_ref[:, at]
            phi = 0.5 * (1.0 + lax.erf(up * (0.5**0.5)))
            dgelu_ref[:, at] = (
                phi + up * (jnp.exp(-0.5 * up * up) * 0.3989422804014327)
            ).astype(dgelu_ref.dtype)
            hid = (up * phi).astype(bf16)
            if t < tiles:
                own_ref[:, half + here.start : half + here.stop] = hid
            else:
                base = width + half
                pack_ref[:, base + here.start : base + here.stop] = hid
            att[...] += dg(hid, d[here], NN)
            if t == tiles - 1:
                own_ref.flush()
        dgelu_ref.flush()
        r2 = att[...]
        rr_ref[:, width:] = r2
        rr_ref.flush()
        n, _q = norm_rows(r2)
        xn = (n * g2[layer : layer + 1] + s2[layer : layer + 1]) * valid_ref[...]
        xn_ref[...] = xn
        xr = xn.astype(bf16)
        xr_ref[...] = xr
        pack_ref[:, width + half + ffh :] = xr
        pack_ref.flush()
        keep_ref[...], send_ref[...] = halves(dg(in_ref[...], xr, TN))

    g1, s1, g2, s2 = gains
    at = lambda w: (w, layer)
    ins = [lanes_of(qkv, 2 * width, width), prev, nxt, taps, got, lanes_of(ne, 0, width), x, g1, s1, bias, g2, s2, valid, inside,
           at(wo[0]), at(wo[1]), at(wu[0]), at(wd[0]), at(wu[1]), at(wd[1])]
    outs = [((LANDMARKS + 8, width), f32), ((rows, 2 * width + half + ffh), bf16),
            ((rows, half + ffh), bf16), ((rows, 2 * width), f32), ((rows, 2 * ffh), bf16),
            ((rows, width), f32, None), ((rows, width), bf16, None),
            ((LANDMARKS, half), f32, None), ((LANDMARKS, half), f32, None)]
    return call(
        body, ins, outs, [pltpu.VMEM((rows, width), f32)],
        cost=(2 * rows * width * (4 * ffh + width) * 2, 30 * rows * width * 4), after=after,
    )


def backward_rows(g, rr, dgelu, ne, mixed, qkv, marks, weights, gains, valid, layer, chunks, parts,
                  after=()):
    wo, wu, wd = weights
    rows, width = rr.shape[0], rr.shape[1] // 2
    half = width // 2
    owners = half // OWN_COLS
    ffh = wu[0].shape[2]
    tiles = ffh // FF_TILE
    pieces = 2 * parts

    def body(ins, outs, acc, mk):
        (g_ref, g2, valid_ref, g1, rr_ref, dgelu_ref, d0, u0, d1, u1, o0, o1, near_ref, mix_ref,
         km_ref, q_ref) = ins
        (pack_ref, gu_ref, bias_ref, gr1_ref, gatt_ref, gqn_ref, out_ref, small_ref,
         tail_ref, head_ref) = outs
        mark = slice(0, LANDMARKS)
        gy = g_ref[...].astype(f32) * valid_ref[...]
        gr2, dgain, dshift = norm_pull(rr_ref[:, width:], gy, g2[layer : layer + 1])
        acc[...] = gr2
        pack_ref[:, :width] = gr2.astype(bf16)
        small_ref[2:3] = dgain
        small_ref[3:4] = dshift
        for t in range(2 * tiles):
            at = slice(t * FF_TILE, (t + 1) * FF_TILE)
            here = slice(t % tiles * FF_TILE, (t % tiles + 1) * FF_TILE)
            u, d = ((u0, d0), (u1, d1))[t // tiles]
            gh = dg(pack_ref[:, :width], d[here], NT)
            gu = (gh * dgelu_ref[:, at].astype(f32)).astype(bf16)
            bias_ref[:, at] = jnp.sum(gu.astype(f32), axis=0, keepdims=True)
            if t < tiles:
                gu_ref[:, here] = gu
            else:
                pack_ref[:, 2 * width + here.start : 2 * width + here.stop] = gu
            acc[...] += dg(gu, u[:, here], NT)
            if t == tiles - 1:
                gu_ref.flush()
        gr1, dgain, dshift = norm_pull(rr_ref[:, :width], acc[...], g1[layer : layer + 1])
        small_ref[0:1] = dgain
        small_ref[1:2] = dshift
        small_ref[4:8] = jnp.zeros((4, width), f32)
        gr1_ref[...] = gr1
        gb = gr1.astype(bf16)
        pack_ref[:, width : 2 * width] = gb
        pack_ref.flush()
        gatt_ref[:, :half] = dg(gb, o0[...], NT)
        gatt_ref[:, half:] = dg(gb, o1[...], NT)
        write_rims(gatt_ref, tail_ref, head_ref, chunks)
        for b in range(width // 256):
            at = slice(256 * b, 256 * (b + 1))
            gatt = gatt_ref[:, at]
            nr = near_ref[:, at]
            gn = dot3(gatt, spread(mix_ref[mark, at]), NT)
            gs = nr * (gn - head_sum(nr * gn)) * SCALE
            gqn_ref[:, at] = dot3(gs, spread(km_ref[mark, at]), NN)
            mk[mark, at] = collect(dot3(nr, gatt, TN))
            mk[LANDMARKS:, at] = collect(dot3(gs, q_ref[:, at], TN))

        def cols(base):
            def piece(p):
                if p >= owners:
                    return jnp.zeros((2 * LANDMARKS, OWN_COLS), f32)
                return mk[:, base + p * OWN_COLS : base + (p + 1) * OWN_COLS]
            return piece

        write_pieces(out_ref, slice(None), cols(0), cols(half))

    g1, g2 = gains
    at = lambda w: (w, layer)
    ins = [g, g2, valid, g1, *far_off(rr, dgelu), at(wd[0]), at(wu[0]), at(wd[1]), at(wu[1]),
           at(wo[0]), at(wo[1]), lanes_of(ne, 0, width), (mixed, None), lanes_of(marks, width, width),
           lanes_of(qkv, 0, width)]
    row = ((rows, width), f32, None)
    rim = ((RIM * chunks, width), f32, None)
    outs = [((rows, 2 * width + ffh), bf16), ((rows, ffh), bf16), ((1, 2 * ffh), f32, None),
            row, row, row, ((pieces, 2 * LANDMARKS, OWN_COLS), f32, None), ((8, width), f32, None),
            rim, rim]
    return call(
        body, ins, outs,
        [pltpu.VMEM((rows, width), f32), pltpu.VMEM((2 * LANDMARKS, width), f32)],
        cost=(2 * rows * width * (4 * ffh + width) * 2, 30 * rows * width * 4), after=after,
    )


def inverse_pull(parts, summary, kept, after=()):
    count, rows, n = parts.shape

    def body(ins, outs):
        s_ref, g_ref, kept_ref = ins
        (out_ref,) = outs
        ident = eye(n)
        mask = head_mask(n, n)
        g = g_ref[0]
        for d in range(1, count):
            g = g + g_ref[d]
        gm = spread(g[0:LANDMARKS])
        sm = s_ref[...]
        sb = spread(sm)
        a = kept_ref[0]
        at = a.T
        gz = mm(gm, sb.T)
        gs = collect(mm(kept_ref[2].T, gm))
        ga = jnp.zeros((n, n), f32)
        for step in reversed(range(PINV_STEPS)):
            z, p, t2, t3 = (kept_ref[3 + 4 * step + i] for i in range(4))
            zt, pt = z.T, p.T
            gt3 = 0.25 * mm(zt, gz)
            gt2 = -mm(pt, gt3)
            gt1 = -mm(pt, gt2)
            gp = -(mm(gt3, t2.T) + mm(gt2, (7.0 * ident - p).T) + gt1)
            gz = 0.25 * mm(gz, t3.T) + mm(at, gp)
            ga = ga + mm(gp, zt)
        norm = head_total(jnp.sum(a * a, axis=1, keepdims=True))
        gn = -head_total(jnp.sum(gz * at, axis=1, keepdims=True)) / (norm * norm)
        ga = ga + gz.T / norm + 2.0 * a * gn
        gsc = jnp.where(mask, a * (ga - jnp.sum(a * ga, axis=1, keepdims=True)), 0.0) * SCALE
        centre = jnp.sum(spread(gs * sm), axis=1, keepdims=True)
        out = jnp.concatenate(
            [
                gs,
                collect(mm(gsc, spread(kept_ref[1, LANDMARKS:]))),
                g[LANDMARKS:] + collect(mm(gsc.T, spread(kept_ref[1, :LANDMARKS]))),
                jnp.broadcast_to(centre, (n, n)).T[0:8],
            ],
            axis=0,
        )
        for d in range(count):
            out_ref[d] = out

    return call(
        body, [summary, parts, (kept, None)],
        [((count, 3 * LANDMARKS + 8, n), f32, None)],
        cost=(2 * n**3 * 6 * 52 * 4, 4 * 26 * n * n), after=after,
    )[0]


def conv_pull(qkv, gatt, prev, nxt, vprev, vnext, taps, layer, after=()):
    rows, width = gatt.shape
    chunks = prev.shape[0] // RIM
    chunk = rows // chunks

    def body(ins, outs):
        v_ref, vprev_ref, vnext_ref, ga_ref, taps_ref, prev_ref, next_ref = ins
        gv_ref, cg_ref = outs
        for b in range(width // 128):
            at = slice(128 * b, 128 * (b + 1))
            taps_here = taps_ref[layer, :, at]
            sums = [None] * TAPS
            for c in range(chunks):
                here = slice(chunk * c, chunk * (c + 1))
                gv_ref[here, at] = conv_block(
                    padded_chunk(ga_ref, prev_ref, next_ref, c, chunk, at, chunks),
                    taps_here, chunk, flip=True,
                )
                vp = padded_chunk(v_ref, vprev_ref, vnext_ref, c, chunk, at, chunks)
                ga = ga_ref[here, at]
                for res in range(8):
                    sh = vp if res == 0 else vp[res : res + chunk + 24]
                    for a in range(5):
                        r = 8 * a + res
                        if r < TAPS:
                            prod = ga * sh[8 * a : 8 * a + chunk]
                            s = prod[0:8]
                            for j in range(1, chunk // 8):
                                s = s + prod[8 * j : 8 * (j + 1)]
                            sums[r] = s if sums[r] is None else sums[r] + s
            for r in range(TAPS):
                cg_ref[r : r + 1, at] = jnp.sum(sums[r], axis=0, keepdims=True)
        cg_ref[TAPS:] = jnp.zeros((40 - TAPS, width), f32)

    return call(
        body, [lanes_of(qkv, 2 * width, width), vprev, vnext, gatt, taps, prev, nxt],
        [((rows, width), f32, None), ((40, width), f32, None)],
        cost=(2 * rows * width * TAPS * 40, 4 * 4 * rows * width), after=after,
    )


def far_pull(ne, marks, mixed, got, qkv, gvc, inside, icounts, valid, after=()):
    rows, width = gvc.shape
    half = width // 2
    owners = half // OWN_COLS

    def body(ins, outs, mk, gq):
        got_ref, mix_ref, in_ref, ic_ref, e_ref, kv_ref, qm_ref, gvc_ref, valid_ref = ins
        gk_ref, gv_ref, gmid_ref, own_ref, oth_ref = outs
        k_ref, v_ref = (Cols(kv_ref, i * width, width) for i in range(2))
        mark = slice(0, LANDMARKS)
        mk[...] = read_owned(got_ref, slice(None), owners)
        gmid_ref[...] = mk[LANDMARKS : 2 * LANDMARKS]
        tops = mix_ref[LANDMARKS : LANDMARKS + 1, :]
        scale = jnp.exp(qm_ref[LANDMARKS : LANDMARKS + 1, :] - tops)
        scale = scale / mix_ref[LANDMARKS + 1 : LANDMARKS + 2, :]
        ins3 = jnp.concatenate([in_ref[...]] * 3, axis=1)
        live = valid_ref[...]
        for b in range(width // 256):
            at = slice(256 * b, 256 * (b + 1))
            far = e_ref[:, at] * scale[:, at]
            gs = spread(mk[mark, at])
            gf = dot3(v_ref[:, at], gs, NT)
            sc = far * (gf - mk[3 * LANDMARKS : 3 * LANDMARKS + 1, at]) * SCALE
            gq[:, at] = collect(dot3(sc, k_ref[:, at], TN))
            gv = dot3(far, gs, NN) + gvc_ref[:, at]
            gv_ref[:, at] = (gv * live).astype(bf16)
            gkm = mk[2 * LANDMARKS : 3 * LANDMARKS, at] * ic_ref[...]
            gk = dot3(sc, spread(qm_ref[mark, at]), NN) + dg(
                ins3, jnp.concatenate(split3(gkm), axis=0), NN
            )
            gk_ref[:, at] = gk.astype(bf16)
        own_ref[...] = gq[:, :half]
        oth_ref[...] = gq[:, half:]

    ins = [got, (mixed, None), inside, icounts, lanes_of(ne, width, width),
           lanes_of(qkv, width, 2 * width), lanes_of(marks, 0, width), gvc, valid]
    outs = [((rows, width), bf16, None)] * 2 + [((LANDMARKS, width), f32, None)]
    outs += [((LANDMARKS, half), f32, None)] * 2
    return call(
        body, ins, outs,
        [pltpu.VMEM((3 * LANDMARKS + 8, width), f32), pltpu.VMEM((LANDMARKS, width), f32)],
        cost=(2 * rows * width * 256 * 15, 12 * 4 * rows * width), after=after,
    )


def input_pull(gqn, gtot, goth, gmid, inside, icounts, gk, gv, gr1, weights, layer, low_out,
               after=()):
    rows, width = gqn.shape
    half = width // 2

    def body(ins, outs):
        (gr1_ref, gk_ref, gv_ref, w0, w1, gqn_ref, gt_ref, go_ref, gmid_ref, in_ref, ic_ref) = ins
        own_ref, oth_ref, gx_ref = outs
        gm = jnp.concatenate([gt_ref[...], go_ref[...]], axis=1)
        gm = (gm + gmid_ref[...]) * ic_ref[...]
        ins3 = jnp.concatenate([in_ref[...]] * 3, axis=1)
        gq = (gqn_ref[...] + dg(ins3, jnp.concatenate(split3(gm), axis=0), NN)).astype(bf16)
        for i, g in enumerate((gq, gk_ref[...], gv_ref[...])):
            own_ref[:, i * half : (i + 1) * half] = g[:, :half]
            oth_ref[:, i * half : (i + 1) * half] = g[:, half:]
        gx = gr1_ref[...] + (dg(own_ref[...], w0[...], NT) + dg(oth_ref[...], w1[...], NT))
        gx_ref[...] = gx.astype(gx_ref.dtype)

    ins = [gr1, gk, gv, (weights[0], layer), (weights[1], layer), gqn, gtot, goth, gmid, inside,
           icounts]
    outs = [((rows, 3 * half), bf16, None)] * 2 + [((rows, width), low_out, None)]
    return call(
        body, ins, outs, cost=(2 * rows * width * 3 * width, 8 * 4 * rows * width), after=after,
    )


def split_rows(tmp, keep_ref, send_ref, cols, me, low_first, docs, parts, r):
    bit = 1 if low_first else parts // 2
    mine = (me // bit) % 2
    for d in range(docs):
        for m in range(parts // 2):
            to = slice((d * parts // 2 + m) * r, (d * parts // 2 + m + 1) * r)
            for ref, b in ((keep_ref, mine), (send_ref, 1 - mine)):
                block_at = d * parts + (2 * m + b if low_first else m + bit * b)
                ref[to, cols] = tmp[pl.ds(pl.multiple_of(block_at * r, r), r)]


def weight_grads(arrays, lefts, rights, tiles, docs, parts, after=()):
    cols = 384
    shapes = [
        x if not isinstance(x, tuple) or x[1] is None else jax.eval_shape(lambda v, at=x[1]: v[at], x[0])
        for x in arrays
    ]
    shapes = [x[0] if isinstance(x, tuple) else x for x in shapes]
    rows, width = shapes[0].shape[0], lefts[0][2]
    r = width // (docs * parts)
    split = r % 16 == 0
    sizes = [sum(1 for t in tiles if t[3] == dest) * cols for dest in (0, 1)]

    def body(given, outs, lt, tmp):
        me = place()[0]
        done = [0, 0]
        last = None
        for left, right, t, dest in tiles:
            if left != last:
                for side in range(2):
                    i, at = lefts[left][side]
                    lt[:, side * rows : (side + 1) * rows] = given[i][:, at : at + width].T
                last = left
            both = []
            for i, at in rights[right]:
                both.append(given[i][:, at + t * cols : at + (t + 1) * cols])
            x = dg(lt[...], jnp.concatenate(both, axis=0), NN).astype(bf16)
            to = slice(done[dest] * cols, (done[dest] + 1) * cols)
            done[dest] += 1
            mine = outs[2 * dest : 2 * dest + 2] if split else outs[dest : dest + 1]
            if split:
                tmp[...] = x
                split_rows(tmp, *mine, to, me, dest == 0, docs, parts, r)
            else:
                mine[0][:, to] = x
            if to.stop == sizes[dest]:
                for o in reversed(mine):
                    o.flush()

    outs = []
    for size in sizes:
        outs += [((width // 2, size), bf16)] * 2 if split else [((width, size), bf16)]
    return call(
        body, arrays, outs, [pltpu.VMEM((width, 2 * rows), bf16), pltpu.VMEM((width, cols), bf16)],
        cost=(2 * width * 2 * rows * cols * len(tiles), 2 * width * cols * len(tiles)), after=after,
    )


def fold(sums, docs, parts, after=()):
    ka, _, kb, _ = sums
    rows = ka.shape[0] // 2
    r = rows // docs

    def body(ins, outs, ta, tb):
        me = place()[0]
        for i, (tmp, mine) in enumerate(((ta, me // 2), (tb, me % 2))):
            keep, got = ins[2 * i : 2 * i + 2]
            keep_ref, send_ref = outs[2 * i : 2 * i + 2]
            tmp[...] = (keep[...].astype(f32) + got[...].astype(f32)).astype(bf16)
            for d in range(docs):
                to = slice(d * r, (d + 1) * r)
                for ref, m in ((send_ref, 1 - mine), (keep_ref, mine)):
                    ref[to] = tmp[pl.ds(pl.multiple_of((2 * d + m) * r, r), r)]
            send_ref.flush()
            keep_ref.flush()

    outs = [((rows, x.shape[1]), bf16) for x in (ka, ka, kb, kb)]
    scratch = [pltpu.VMEM(x.shape, bf16) for x in (ka, kb)]
    return call(body, far_off(*sums), outs, scratch, cost=(1000, 4 * ka.size), after=after)


def fold_last(sums, docs, after=()):
    ka, _, kb, _ = sums
    r = ka.shape[0] // docs
    na, nb = ka.shape[1], kb.shape[1]

    def body(ins, outs):
        a, ga, b, gb = ins
        (out,) = outs
        for d in range(docs):
            at = slice(d * r, (d + 1) * r)
            out[d, :, :na] = (a[at].astype(f32) + ga[at].astype(f32)).astype(bf16)
            out[d, :, na:] = (b[at].astype(f32) + gb[at].astype(f32)).astype(bf16)

    return call(
        body, far_off(*sums), [((docs, r, na + nb), bf16)], cost=(1000, 4 * ka.size), after=after
    )[0]


def pack_small(smalls, biases, convs, after=()):
    layers = len(smalls)
    width = smalls[0].shape[1]
    ff = biases[0].shape[1]
    nv, nb = 4 * width // 128, ff // 128
    rows = nv + nb + 40

    def body(ins, outs):
        (out_ref,) = outs
        _, core = place()
        r = lax.broadcasted_iota(jnp.int32, (width, 128), 0) // HEAD_DIM
        c = lax.broadcasted_iota(jnp.int32, (width, 128), 1)
        head = r + (HEADS // 2) * core
        head = jnp.where(head >= HEADS, head - HEADS, head)
        hot = jnp.where(head == c, 1.0, 0.0).astype(bf16)
        for layer in range(layers):
            s_ref, b_ref, c_ref = ins[3 * layer : 3 * layer + 3]
            for j in range(width // 128):
                for k in range(4):
                    out_ref[layer, k * (width // 128) + j : k * (width // 128) + j + 1] = (
                        s_ref[k : k + 1, 128 * j : 128 * (j + 1)]
                    )
            for j in range(nb):
                lane = slice(128 * j, 128 * (j + 1))
                oth = 128 * ((j + nb // 2) % nb)
                piece = jnp.where(core == 0, b_ref[:, lane], b_ref[:, oth : oth + 128])
                out_ref[layer, nv + j : nv + j + 1] = piece
            c1, c2, c3 = split3(c_ref[...])
            out_ref[layer, nv + nb :] = dg(c1, hot, NN) + (dg(c2, hot, NN) + dg(c3, hot, NN))

    ins = [x for layer in range(layers) for x in (smalls[layer], biases[layer], convs[layer])]
    return call(body, ins, [((layers, rows, 128), f32, None)], after=after)[0]


def partner(x, axis, mask):
    n = lax.axis_size(axis)
    return lax.ppermute(x, axis, [(i, i ^ mask) for i in range(n)])


def swap(x):
    return partner(x, "core", 1)


def sum_over(x, axis):
    n = lax.axis_size(axis)
    if n <= 4:
        parts = [partner(x, axis, m) for m in range(1, n)]
        for p in parts:
            x = x + p
        return x
    bit = 1
    while bit < n:
        x = x + partner(x, axis, bit)
        bit *= 2
    return x


def total_and_other(keep, send):
    parts = lax.axis_size("part")
    mine = keep + swap(send)
    got = exchange(jnp.broadcast_to(mine[None], (parts, *mine.shape)), "part")
    total = got[0]
    for p in range(1, parts):
        total = total + got[p]
    return total, swap(total)


def exchange(x, axes):
    return lax.all_to_all(x, axes, 0, 0, tiled=True)


def rims(tails, heads):
    n = 2 * lax.axis_size("part")
    axes = ("part", "core")
    return (
        lax.ppermute(tails, axes, [(i, (i + 1) % n) for i in range(n)]),
        lax.ppermute(heads, axes, [((i + 1) % n, i) for i in range(n)]),
    )


def halve_parts(keep, got, n, low_first):
    me = lax.axis_index("part")
    parts = lax.axis_size("part")
    docs = lax.axis_size("doc")
    cols = keep.shape[1]
    bit = parts // n if low_first else n // 2
    while n > 1:
        shape = (docs, n // 2, 2, -1, cols) if low_first else (docs, 2, n // 2, -1, cols)
        axis = 2 if low_first else 1
        mine = (me // bit) % 2
        k, g = keep.reshape(shape), got.reshape(shape)
        pick = lambda x, i: lax.dynamic_index_in_dim(x, i, axis, keepdims=False).astype(f32)
        send = (pick(k, 1 - mine) + pick(g, 1 - mine)).astype(bf16)
        keep = (pick(k, mine) + pick(g, mine)).astype(bf16)
        got = partner(send, "part", bit)
        n //= 2
        bit = bit * 2 if low_first else bit // 2
    return (keep.astype(f32) + got.astype(f32)).astype(bf16).reshape(docs, -1, cols)


def first_halves(outs):
    parts = lax.axis_size("part")
    docs = lax.axis_size("doc")
    if len(outs) == 2:
        pieces = []
        for x, low_first in zip(outs, (True, False)):
            bit = 1 if low_first else parts // 2
            shape = (docs, parts // 2, 2, -1, x.shape[1]) if low_first else (
                docs, 2, parts // 2, -1, x.shape[1])
            axis = 2 if low_first else 1
            mine = (lax.axis_index("part") // bit) % 2
            v = x.reshape(shape)
            for i in (mine, 1 - mine):
                pieces.append(
                    lax.dynamic_index_in_dim(v, i, axis, keepdims=False).reshape(-1, x.shape[1])
                )
        outs = pieces
    ka, sa, kb, sb = outs
    return ka, partner(sa, "part", 1), kb, partner(sb, "part", parts // 2)


def second_halves(sums, after=()):
    parts = lax.axis_size("part")
    docs = lax.axis_size("doc")
    if parts == 4 and sums[0].shape[0] // (2 * docs) % 16 == 0:
        ka, sa, kb, sb = fold(sums, docs, parts, after)
        return ka, partner(sa, "part", 2), kb, partner(sb, "part", 1)
    out = []
    for keep, got, low_first in ((*sums[:2], True), (*sums[2:], False)):
        x = halve_parts(keep, got, parts // 2, low_first).reshape(-1, keep.shape[1])
        out += [x, jnp.zeros_like(x)]
    return tuple(out)


def third(sums, after=()):
    docs = lax.axis_size("doc")
    if sums[0].shape[0] // docs % 16 == 0:
        x = fold_last(sums, docs, after)
    else:
        ka, ga, kb, gb = (x.reshape(docs, -1, x.shape[1]) for x in sums)
        x = jnp.concatenate([ka + ga, kb + gb], axis=2)
    return x


def finish(feeds, att):
    layers = len(feeds)
    docs, r, nf = feeds[0].shape
    half = att.shape[2] // (3 * layers)
    ffh = (nf - half) // 2

    def body(ins, outs):
        q_ref, k_ref, v_ref, o_ref, u_ref, d_ref = outs

        def total(ref, at, size):
            s = ref[0, :, at : at + size].astype(f32)
            for d in range(1, docs):
                s = s + ref[d, :, at : at + size].astype(f32)
            return s

        for layer in reversed(range(layers)):
            ff = ins[layers - 1 - layer]
            u_ref[layer] = total(ff, 0, ffh)
            o_ref[layer] = total(ff, ffh, half).T
            for j in range(ffh // half):
                d_ref[layer, j * half : (j + 1) * half] = total(ff, ffh + half + j * half, half).T
        for layer in range(layers):
            for j, ref in enumerate((q_ref, k_ref, v_ref)):
                ref[layer] = total(ins[layers], (3 * layer + j) * half, half)

    ins = far_off(*reversed(feeds), att)
    outs = [((layers, r, half), f32)] * 3 + [
        ((layers, half, r), f32), ((layers, r, ffh), f32), ((layers, ffh, r), f32)
    ]
    return call(body, ins, outs)


def local(inputs, cotangent, lengths, query_weight, key_weight, value_weight, conv_weight,
          out_weight, gain_one, shift_one, up_weight, up_bias, down_weight, gain_two, shift_two):
    docs, chunk, width = inputs.shape
    parts = lax.axis_size("part")
    doc, part, core = (lax.axis_index(a) for a in ("doc", "part", "core"))
    half = query_weight.shape[2]
    ffh = up_weight.shape[2]
    rows = docs * chunk
    group = ("part", "core")

    state = exchange(inputs, "doc").reshape(rows, width)
    wqkv = jnp.concatenate([query_weight, key_weight, value_weight], axis=2)
    wqkv = (wqkv, swap(wqkv))

    length = lengths[doc]
    place = ((jnp.arange(docs, dtype=jnp.int32) * parts + part) * 2 + core) * chunk
    place = (place[:, None] + jnp.arange(chunk, dtype=jnp.int32)[None, :]).reshape(rows)
    valid = (place < length).astype(f32)[:, None]
    bounds = jnp.arange(LANDMARKS + 1, dtype=jnp.int32) * length // LANDMARKS
    inside = (
        (place[:, None] >= bounds[None, :-1]) & (place[:, None] < bounds[None, 1:])
    ).astype(bf16)
    icounts = 1.0 / (bounds[1:] - bounds[:-1]).astype(f32)[:, None]

    xbar = dg(inside, state, TN)
    first = core == 0
    keep = jnp.where(first, xbar[:, : width // 2], xbar[:, width // 2 :])
    send = jnp.where(first, xbar[:, width // 2 :], xbar[:, : width // 2])
    wo = (out_weight, swap(out_weight))
    wu = (up_weight, swap(up_weight))
    wd = (down_weight, swap(down_weight))
    bias = jnp.concatenate([up_bias, swap(up_bias)], axis=1)
    conv = jnp.concatenate([conv_weight, swap(conv_weight)], axis=1)
    taps = prepare_taps(jnp.pad(conv, ((0, 0), (0, 16 - HEADS), (0, 40 - TAPS))))
    grad = exchange(cotangent, "doc").reshape(rows, width)

    low = state
    low_got = swap(state)
    kept = []
    for layer in range(LAYERS):
        xtot, xoth = total_and_other(keep, send)
        qkv, tails, heads = project(
            low, wqkv, valid, layer, docs, after=(wo[1], wu[1], wd[1]) if layer == 0 else ()
        )
        vprev, vnext = rims(tails, heads)
        ne, marks, qk, pieces = scores(
            qkv, xtot, xoth, icounts, wqkv, valid, layer, parts,
            after=(grad,) if layer == 0 else (),
        )
        inv, end = inverse(qk)
        merged, summary = merge(exchange(pieces, group), end)
        mixed, pack, own, rr, dgelu, nxt_state, nxt_low, keep, send = forward_rows(
            ne, exchange(merged, group), qkv, vprev, vnext, taps, state,
            (wo, wu, wd, bias[layer : layer + 1]), (gain_one, shift_one, gain_two, shift_two),
            valid, inside, layer,
        )
        pack_got = swap(pack)
        kept.append(dict(
            low=(low, low_got), qkv=qkv, vprev=vprev, vnext=vnext, ne=ne, marks=marks,
            inv=inv, summary=summary, mixed=mixed, pack=(pack, pack_got), own=own, rr=rr,
            dgelu=dgelu,
        ))
        state, low = nxt_state, nxt_low
        at = width + half + ffh
        low_got = lanes_of(pack_got, at, width)
        kept[-1]["next_low"] = (lanes_of(pack, at, width), low_got)
    output = exchange(low.reshape(docs, chunk, width), "doc")

    smalls, biases, convs = [None] * LAYERS, [None] * LAYERS, [None] * LAYERS
    ff_sums = None
    att_args = []
    for layer in reversed(range(LAYERS)):
        s = kept[layer]
        pack, gu, gbias, gr1, gatt, gqn, pieces, small, tails, heads = backward_rows(
            grad, s["rr"], s["dgelu"], s["ne"], s["mixed"], s["qkv"], s["marks"],
            (wo, wu, wd), (gain_one, gain_two), valid, layer, docs, parts,
        )
        pieces = exchange(pieces, group)
        gprev, gnext = rims(tails, heads)
        pack_got = swap(pack)
        before = (gprev, gnext)
        if ff_sums is not None:
            ff_sums = second_halves(ff_sums, after=(small, output))
            before = (gprev, gnext, ff_sums[0])
        pulled = inverse_pull(pieces, s["summary"], s["inv"], after=before)
        got = exchange(pulled, group)
        gvc, cg = conv_pull(
            s["qkv"], gatt, gprev, gnext, s["vprev"], s["vnext"], taps, layer, after=(pulled,)
        )
        gk, gv, gmid, gown, goth = far_pull(
            s["ne"], s["marks"], s["mixed"], got, s["qkv"], gvc, inside, icounts, valid,
        )
        gown, goth = total_and_other(gown, goth)
        fpack, fpack_got = s["pack"]
        arrays = [(pack, None), (pack_got, None), (gu, None), lanes_of(fpack, 0, width),
                  lanes_of(fpack_got, 0, width + half + ffh), (s["own"], None)]
        lefts = [((3, 0), (4, 0), width), ((0, 0), (1, 0), width), ((0, width), (1, width), width)]
        rights = [((2, 0), (1, 2 * width)), ((5, half), (4, width + half)), ((5, 0), (4, width))]
        nt = ffh // 384
        tiles = [(0, 0, j, 0) for j in range(nt)] + [(2, 2, 0, 0)] + [(1, 1, j, 1) for j in range(nt)]
        sums = weight_grads(arrays, lefts, rights, tiles, docs, parts, after=(gk,))
        before = (sums[0],)
        if ff_sums is not None:
            ff_above = third(ff_sums, after=before)
            before = (ff_above,)
            ff_above = exchange(ff_above, "doc")
        qkv, qkv_send, grad = input_pull(
            gqn, gown, goth, gmid, inside, icounts, gk, gv, gr1, wqkv, layer,
            f32 if layer > 0 else bf16, after=before,
        )
        qkv_got = swap(qkv_send)
        ff_sums = first_halves(sums)
        low_pair = s["low"] if layer == 0 else kept[layer - 1]["next_low"]
        low, low_got = low_pair if isinstance(low_pair[0], tuple) else far_off(*low_pair)
        att_args.append([low, low_got, (qkv, None), (qkv_got, None)])
        smalls[layer], biases[layer], convs[layer] = small, gbias, cg
    att_args.reverse()
    att = weight_grads(
        [x for args in att_args for x in args],
        [((4 * l, 0), (4 * l + 1, 0), width) for l in range(LAYERS)],
        [((4 * l + 2, 0), (4 * l + 3, 0)) for l in range(LAYERS)],
        [(l, l, j, l) for l in range(LAYERS) for j in range(3)], docs, parts,
    )
    ff_sums = second_halves(ff_sums, after=(att[0], ff_above))
    grad_inputs = exchange(grad.reshape(docs, chunk, width), "doc")
    ff_now = third(ff_sums, after=(grad_inputs,))
    small = pack_small(smalls, biases, convs, after=(ff_now,))
    small = sum_over(sum_over(small + swap(small), "part"), "doc")
    att = second_halves(first_halves(att), after=(ff_now,))
    ff_now = exchange(ff_now, "doc")
    att = exchange(third(att, after=(ff_now, small)), "doc")
    grad_inputs = grad_inputs.astype(f32)

    nv = width // 128
    vec = [small[:, i * nv : (i + 1) * nv].reshape(LAYERS, width) for i in range(4)]
    nb = 2 * ffh // 128
    gbias = small[:, 4 * nv : 4 * nv + nb].reshape(LAYERS, 2 * ffh)
    gconv = jnp.swapaxes(small[:, 4 * nv + nb : 4 * nv + nb + TAPS, :HEADS], 1, 2)
    q, k, v, o, u, d = finish([ff_now, ff_above], att)
    return (
        output.astype(f32), grad_inputs, q, k, v, gconv, o, vec[0], vec[1], u, gbias, d, vec[2], vec[3],
    )


def solution(mesh):
    seq = ("doc", "part")
    rows = P(None, ("doc", "part", "core"), None)
    placed = (
        rows, rows, P(), P(None, None, "core"), P(None, None, "core"), P(None, None, "core"),
        P(None, "core", None), P(None, "core", None), P(), P(), P(None, None, "core"),
        P(None, "core"), P(None, "core", None), P(), P(),
    )
    outs = (
        rows, rows, P(None, seq, "core"), P(None, seq, "core"), P(None, seq, "core"), P(),
        P(None, "core", seq), P(), P(), P(None, seq, "core"), P(), P(None, "core", seq), P(), P(),
    )

    def run(*args):
        docs = args[0].shape[0]
        seq_size = mesh.shape["seq"]
        cut = Mesh(
            mesh.devices.reshape(docs, seq_size // docs, mesh.shape["head"]),
            ("doc", "part", "core"),
        )
        return jax.shard_map(local, mesh=cut, in_specs=placed, out_specs=outs, check_vma=False)(*args)

    return run
```
